512 devices in a mesh: rep: 64 (over z, x, core), head: 8 (over y).
Axes of the slice: x: 4, y: 8, z: 8, core: 2. Of those that a mesh axis runs over, the one named last changes fastest.
Arguments:
- states: float32 [128, 32, 128, 128], P('rep', 'head'), may hold values from -4 to 4
- conv_states: bfloat16 [128, 3, 3, 4096], P('rep', None, None, 'head'), may hold values from -6 to 6
- projected: bfloat16 [6, 128, 3, 4096], P(None, 'rep', None, 'head'), may hold values from -6 to 6
- conv_weight: float32 [4, 3, 4096], P(None, None, 'head'), may hold values from -3 to 3
- decay_input: float32 [6, 128, 4096], P(None, 'rep', 'head'), may hold values from -6 to 6
- decay_rate: float32 [32], P('head'), may hold values from 0.05 to 2
- beta_logit: float32 [6, 128, 32], P(None, 'rep', 'head'), may hold values from -6 to 6
- out_gate: bfloat16 [6, 128, 4096], P(None, 'rep', 'head'), may hold values from -6 to 6
- norm_gain: float32 [128], replicated, may hold values from 0.25 to 1.75
- out_weight: bfloat16 [4096, 2304], P('head'), may hold values from -0.125 to 0.125
- destinations: int32 [6, 128], replicated, may hold values from 0 to 127, as said below
- live_counts: int32 [6, 64], P(None, 'rep'), may hold values from 1 to 2
Outputs:
- layer_out: bfloat16 [6, 128, 2304], P(None, 'rep', 'head')
- states_out: float32 [128, 32, 128, 128], P('rep', 'head')
- conv_out: bfloat16 [128, 3, 3, 4096], P('rep', None, None, 'head')
The draws below stay inside these ranges and needn't reach their ends.
Inputs may be any that keep to these rules, and one draw needn't show every extreme that they name: For each step t, destinations[t] is a permutation of the 128 slots; slot g belongs to replica group g // 2. In every step, the number of slots g of each group with destinations[t, g] != g is exactly 1.
All inputs are finite; a program needn't handle non-finite values.
Results may differ from the reference program's by a relative error of at most 0.015.
Values may be sent and summed in bfloat16 or wider, within the bound.
A program may use at most 128 MiB of HBM per device.

```python
import math
import jax
import jax.numpy as jnp
from jax import lax

D = 2304
DK = 128
TAPS = 4
ROWS_DEV = 2
MOVE = 1
STEPS = 6
HEADS = 32
GROUPS = 64
ROWS_TOTAL = 128


def group_movers(key, group_total):
    keys = jax.random.split(key, group_total)
    picked = jax.vmap(lambda single: jax.random.permutation(single, ROWS_DEV)[:MOVE])(keys)
    return (jnp.arange(group_total, dtype=jnp.int32)[:, None] * ROWS_DEV + picked.astype(jnp.int32)).reshape(-1)


def draw_destinations(key, part):
    key = jax.random.fold_in(key, 7)
    group_total = ROWS_TOTAL // ROWS_DEV
    stacked = []
    for step_id in range(STEPS):
        step_key = jax.random.fold_in(key, step_id)
        first_key, second_key = jax.random.split(step_key)
        movers = group_movers(first_key, group_total)
        ordering = movers[jax.random.permutation(second_key, group_total * MOVE)]
        mapping = jnp.arange(ROWS_TOTAL, dtype=jnp.int32).at[ordering].set(jnp.roll(ordering, -1))
        stacked.append(mapping.astype(jnp.int32))
    return jnp.stack(stacked)


def with_ends(drawn, rng, least, largest):
    shape = drawn.shape
    index_at = [jax.random.randint(jax.random.fold_in(rng, axis), (), 0, shape[axis]) for axis in range(len(shape))]
    drawn = drawn.at[tuple(index_at)].set(least)
    longest = shape.index(max(shape))
    index_at[longest] = (index_at[longest] + 1) % shape[longest]
    return drawn.at[tuple(index_at)].set(largest)


def raised(result, rng, source, target, blocks, factor):
    def block_of(position):
        return (jnp.arange(result.shape[position]) // (result.shape[position] // blocks)).reshape((-1,) + (1,) * (result.ndim - 1 - position))

    first = jax.random.permutation(rng, blocks)[block_of(target)]
    second = (block_of(target) + blocks // 2) % blocks
    return jnp.where((block_of(source) == first) | (block_of(source) == second), factor * result, result)


def block_levels(stream_key, shape, pieces, least, largest):
    loudness, own = 1.0, jax.random.fold_in(stream_key, 6)
    for axis_at, blocks in pieces:
        draws = jnp.exp(jax.random.uniform(jax.random.fold_in(own, axis_at), (blocks,), jnp.float32, least / len(pieces), largest / len(pieces)))
        loudness = loudness * jnp.repeat(draws, shape[axis_at] // blocks).reshape([-1 if axis == axis_at else 1 for axis in range(len(shape))])
    return loudness


def bell_draw(rng, shape, width, reach, shards=(), kind=jnp.bfloat16):
    result = width * jax.random.normal(rng, shape, jnp.float32)
    if shards:
        result = result * block_levels(rng, shape, shards, -0.22, 0.18)
    return jnp.clip(result, -reach, reach).astype(kind)


def heavy_noise(rng, extent, width, reach, shards, heavy, kind=jnp.bfloat16):
    array = width * jax.random.normal(rng, extent, jnp.float32)
    if shards:
        array = array * block_levels(rng, extent, shards, -0.22, 0.18)
    return jnp.clip(raised(array, jax.random.fold_in(rng, 3), *heavy), -reach, reach).astype(kind)


def setup_inputs(seed: int = 0) -> dict:
    splits = jax.random.split(jax.random.key(seed), 13)
    return {
        "states": bell_draw(splits[0], (ROWS_TOTAL, HEADS, DK, DK), 0.5, 4.0, ((0, 64), (1, 8)), jnp.float32),
        "conv_states": bell_draw(splits[1], (ROWS_TOTAL, TAPS - 1, 3, HEADS * DK), 1.0, 6.0, ((0, 64), (3, 8))),
        "projected": bell_draw(splits[2], (STEPS, ROWS_TOTAL, 3, HEADS * DK), 1.0, 6.0, ((1, 64), (3, 8))),
        "conv_weight": bell_draw(splits[3], (TAPS, 3, HEADS * DK), 0.6, 3.0, ((2, 8),), jnp.float32),
        "decay_input": bell_draw(splits[4], (STEPS, ROWS_TOTAL, HEADS * DK), 1.5, 6.0, ((1, 64), (2, 8)), jnp.float32),
        "decay_rate": jnp.clip(jnp.exp(math.log(2.0) - 3.6888794 * jax.random.uniform(splits[5], (HEADS,), jnp.float32) ** block_levels(splits[5], (HEADS,), ((0, 8),), -0.2, 0.2)), 0.05, 2.0),
        "beta_logit": bell_draw(splits[6], (STEPS, ROWS_TOTAL, HEADS), 1.5, 6.0, ((1, 64), (2, 8)), jnp.float32),
        "out_gate": bell_draw(splits[7], (STEPS, ROWS_TOTAL, HEADS * DK), 1.5, 6.0, ((1, 64), (2, 8))),
        "norm_gain": jnp.clip(1.0 + 0.15 * jax.random.normal(splits[8], (DK,), jnp.float32), 0.25, 1.75),
        "out_weight": heavy_noise(splits[9], (HEADS * DK, D), (HEADS * DK) ** -0.5, 0.125, ((0, 8),), (0, 1, 8, 2.0)),
        "destinations": draw_destinations(jax.random.fold_in(splits[12], 71), 0),
        "live_counts": with_ends(jax.random.randint(splits[11], (STEPS, GROUPS), 1, ROWS_DEV + 1), jax.random.fold_in(splits[11], 1), 1, ROWS_DEV).astype(jnp.int32),
    }


EPSILON = 1e-06

def unit_rows(vectors):
    return vectors / jnp.sqrt(lax.optimization_barrier(jnp.sum(vectors * vectors, axis=-1, keepdims=True)) + EPSILON)

def head_update(carried):
    memory, query, key_vec, value_vec, retain, strength = carried
    decayed = retain[:, :, None] * memory
    recalled = lax.optimization_barrier(jnp.sum(key_vec[:, :, None] * decayed, axis=1))
    updated = decayed + strength[:, None, None] * key_vec[:, :, None] * (value_vec - recalled)[:, None, :]
    readout = lax.optimization_barrier(jnp.sum(query[:, :, None] * updated, axis=1)) * DK ** (-0.5)
    return (updated, readout)

def reference(states, conv_states, projected, conv_weight, decay_input, decay_rate, beta_logit, out_gate, norm_gain, out_weight, destinations, live_counts):
    memory = jnp.moveaxis(states, 1, 0)
    history = conv_states
    slot_ids = jnp.arange(ROWS_TOTAL, dtype=jnp.int32)
    results = []
    for step_id in range(STEPS):
        source = jnp.zeros((ROWS_TOTAL,), jnp.int32).at[destinations[step_id]].set(slot_ids)
        memory = memory[:, source]
        history = history[source]
        alive = slot_ids % ROWS_DEV < jnp.repeat(live_counts[step_id], ROWS_DEV)
        window = jnp.concatenate([history.astype(jnp.float32), projected[step_id][:, None].astype(jnp.float32)], axis=1)
        summed = window[:, 0] * conv_weight[0]
        for tap_id in range(1, TAPS):
            summed = summed + window[:, tap_id] * conv_weight[tap_id]
        activated = jax.nn.silu(summed)
        shifted = window[:, 1:].astype(jnp.bfloat16)
        query = unit_rows(activated[:, 0].reshape(ROWS_TOTAL, HEADS, DK))
        key_vec = unit_rows(activated[:, 1].reshape(ROWS_TOTAL, HEADS, DK))
        value_vec = activated[:, 2].reshape(ROWS_TOTAL, HEADS, DK)
        retain = jnp.exp(-decay_rate[None, :, None] * jax.nn.softplus(decay_input[step_id].reshape(ROWS_TOTAL, HEADS, DK)))
        strength = jax.nn.sigmoid(beta_logit[step_id])
        updated, readout = lax.map(head_update, (memory, jnp.moveaxis(query, 1, 0), jnp.moveaxis(key_vec, 1, 0), jnp.moveaxis(value_vec, 1, 0), jnp.moveaxis(retain, 1, 0), jnp.moveaxis(strength, 1, 0)))
        memory = jnp.where(alive[None, :, None, None], updated, memory)
        history = jnp.where(alive[:, None, None, None], shifted, history)
        readout = jnp.moveaxis(readout, 0, 1)
        scaling = lax.rsqrt(lax.optimization_barrier(jnp.mean(readout * readout, axis=-1, keepdims=True)) + EPSILON)
        gates = jax.nn.sigmoid(out_gate[step_id].astype(jnp.float32).reshape(ROWS_TOTAL, HEADS, DK))
        gated = readout * scaling * norm_gain * gates
        gated = jnp.where(alive[:, None, None], gated, jnp.zeros_like(gated)).astype(jnp.bfloat16).reshape(ROWS_TOTAL, HEADS * DK)
        results.append(jnp.dot(gated, out_weight, preferred_element_type=jnp.float32).astype(jnp.bfloat16))
    return (jnp.stack(results), jnp.moveaxis(memory, 0, 1), history)
```

```python
import functools

import jax
import jax.numpy as jnp
from jax import lax
from jax.experimental import pallas as pl
from jax.experimental.pallas import tpu as pltpu
from jax.sharding import PartitionSpec as P

F32, BF16 = jnp.float32, jnp.bfloat16
STEPS, TAPS = 6, 4
HIST = TAPS - 1
GROUPS, HEADS, DK = 64, 4, 128
SLOTS = 2 * GROUPS
JG, JW = 16, 8
WIN = HIST + STEPS
ROW_X = 0
ROW_HI = WIN * 6
ROW_LO = ROW_HI + 2 * STEPS
ROW_MISC = ROW_LO + 2 * STEPS
ROWS = ROW_MISC + 2
CONV = 3 * HIST
BLOCKS = CONV + STEPS
EPS = 1e-6


def piece_of(m):
    return (m // 8) % HEADS, (m // 32) * 8 + m % 8


def holder(h, jg):
    return (jg // 8) * 32 + h * 8 + jg % 8


def iota(shape, dim):
    return lax.broadcasted_iota(jnp.int32, shape, dim)


def contract(a, b, da, db):
    return lax.dot_general(a, b, (((da,), (db,)), ((), ())), preferred_element_type=F32)


def halves(x):
    lead = x.astype(BF16)
    return lead, (x - lead.astype(F32)).astype(BF16)


def sigmoid(x):
    return 1.0 / (1.0 + jnp.exp(-x))


def softplus(x):
    return jnp.maximum(x, 0.0) + jnp.log1p(jnp.exp(-jnp.abs(x)))


def pack(states, conv, proj, decay, beta, live, s1, s2, f):
    for h in range(HEADS):
        cols = slice(h * DK, (h + 1) * DK)
        first, second = states[0, h].T, states[1, h].T
        for jg in range(JG):
            rows = slice(jg * JW, (jg + 1) * JW)
            s1[holder(h, jg)] = jnp.concatenate([first[rows], second[rows]], axis=0).astype(BF16)
        lane = iota((1, DK), 1)
        for slot in range(2):
            row = jnp.zeros((1, DK), F32)
            for t in range(STEPS):
                alive = jnp.where(live[t, 0] > slot, 1.0, 0.0)
                logit = beta[t, slot, h]
                row = jnp.where(lane == t * 8, alive, row)
                row = jnp.where((lane == t * 8 + 1) | (lane == t * 8 + 2), logit, row)
            lead, rest = halves(row)
            f[h, ROW_MISC + slot : ROW_MISC + slot + 1, :] = jnp.where(
                lane % 8 == 2, rest.astype(F32), lead.astype(F32)
            )
    for w in range(WIN):
        for slot in range(2):
            block = (conv[slot, w] if w < HIST else proj[w - HIST, slot]).astype(F32)
            at = ROW_X + (w * 2 + slot) * 3
            for h in range(HEADS):
                f[h, at : at + 3, :] = block[:, h * DK : (h + 1) * DK]
    for t in range(STEPS):
        lead, rest = halves(decay[t])
        for h in range(HEADS):
            cols = slice(h * DK, (h + 1) * DK)
            f[h, ROW_HI + 2 * t : ROW_HI + 2 * t + 2, :] = lead.astype(F32)[:, cols]
            f[h, ROW_LO + 2 * t : ROW_LO + 2 * t + 2, :] = rest.astype(F32)[:, cols]
    for h in range(HEADS):
        s2[h] = f[h].astype(BF16)


def middle(h, jg, r1, r2, weight, rate, targets, b1, b2, f1, f2, mem, xt):
    def widen(i, _):
        f2[pl.ds(pl.multiple_of(i * ROWS, 8), ROWS), :] = r2[i].astype(F32)
        f1[pl.ds(pl.multiple_of(i * 16, 8), 16), :] = r1[i].astype(F32)
        return 0

    lax.fori_loop(0, GROUPS, widen, 0)

    def both(row, step):
        return jnp.concatenate(
            [f2[pl.ds(row + s * step, GROUPS, stride=ROWS), :] for s in range(2)], axis=0
        )

    for j in range(JW):
        rows = [f1[pl.ds(s * JW + j, GROUPS, stride=16), :] for s in range(2)]
        mem[j] = jnp.concatenate(rows, axis=0).T

    taps = weight[...].T
    eye = jnp.where(iota((SLOTS, SLOTS), 0) == iota((SLOTS, SLOTS), 1), 1.0, 0.0).astype(BF16)
    mine = pl.ds(pl.multiple_of(jg * JW, JW), JW)

    def parts_of(w, at):
        x = jnp.concatenate([both(ROW_X + w * 6 + part, 3) for part in range(3)], axis=1)
        return contract(x.astype(BF16), at, 0, 0)

    for w in range(HIST):
        xt[w] = parts_of(w, eye)
    tap_rows = [[taps[:, 3 * n + part : 3 * n + part + 1] for part in range(3)] for n in range(TAPS)]
    xt[HIST, 0:DK, 0 : TAPS * 3] = taps[:, 0 : TAPS * 3]
    value_taps = [
        xt[HIST, mine, 3 * n + 2 : 3 * n + 3] for n in range(TAPS)
    ]

    def split(ref_index):
        return [
            xt[ref_index, 0:DK, :],
            xt[ref_index, DK : 2 * DK, :],
            xt[ref_index, pl.ds(pl.multiple_of(2 * DK + jg * JW, JW), JW), :],
        ]

    hist = [split(w) for w in range(HIST)]
    misc = jnp.concatenate(
        [f2[pl.ds(ROW_MISC + s, GROUPS, stride=ROWS), :] for s in range(2)], axis=0
    ).astype(BF16)
    place = eye
    readouts = []
    for t in range(STEPS):
        move = jnp.where(iota((SLOTS, SLOTS), 0) == targets[t : t + 1, :], 1.0, 0.0).astype(BF16)
        place = move if t == 0 else contract(move, place, 1, 0).astype(BF16)
        xt[HIST] = parts_of(t + HIST, place)
        new = split(HIST)
        lead, rest = both(ROW_HI + 2 * t, 1).astype(BF16), both(ROW_LO + 2 * t, 1).astype(BF16)
        decay = contract(lead, place, 0, 0) + contract(rest, place, 0, 0)
        flags = contract(misc, place, 0, 0)[t * 8 : t * 8 + 8, :]
        alive = flags[0:1] > 0.5
        strength = jnp.where(alive, sigmoid(flags[1:2] + flags[2:3]), 0.0)
        retain = jnp.where(alive, jnp.exp(-rate * softplus(decay)), 1.0)
        window = hist + [new]
        acts = []
        for part in range(3):
            weights = [value_taps[n] if part == 2 else tap_rows[n][part] for n in range(TAPS)]
            total = window[0][part] * weights[0]
            for n in range(1, TAPS):
                total = total + window[n][part] * weights[n]
            acts.append(total / (1.0 + jnp.exp(-total)))
        hist = [
            [jnp.where(alive, window[n + 1][part], window[n][part]) for part in range(3)]
            for n in range(HIST)
        ]
        query, key, value = acts
        query = query / jnp.sqrt(jnp.sum(query * query, axis=0, keepdims=True) + EPS)
        key = key / jnp.sqrt(jnp.sum(key * key, axis=0, keepdims=True) + EPS)
        rows = []
        for j in range(JW):
            decayed = retain * mem[j]
            recalled = jnp.sum(key * decayed, axis=0, keepdims=True)
            updated = decayed + key * (strength * (value[j : j + 1] - recalled))
            mem[j] = updated
            rows.append(jnp.sum(query * updated, axis=0, keepdims=True) * DK**-0.5)
        lead, rest = halves(jnp.concatenate(rows, axis=0))
        readouts.append(contract(place, lead, 1, 1) + contract(place, rest, 1, 1))

    for j in range(JW):
        final = contract(place, mem[j].astype(BF16), 1, 1)
        for s in range(2):
            f1[pl.ds(s * JW + j, GROUPS, stride=16), :] = final[s * GROUPS : (s + 1) * GROUPS]
    xt[HIST, 0:DK, :] = jnp.zeros((DK, SLOTS), F32)
    for n in range(HIST):
        for part in range(3):
            block = hist[n][part]
            if part < 2:
                xt[HIST, DK * (part + 1) : DK * (part + 2), :] = block
                block = xt[HIST, pl.ds(pl.multiple_of(DK * (part + 1) + jg * JW, JW), JW), :]
            at = (n * 3 + part) * JW
            xt[HIST, at : at + JW, :] = block
    kept = contract(place, xt[HIST, 0:DK, :].astype(BF16), 1, 1)
    tail = jnp.concatenate(readouts + [jnp.zeros((SLOTS, DK - BLOCKS * JW), F32)], axis=1)
    xt[HIST, 0:SLOTS, :] = kept
    xt[HIST, 0:SLOTS, CONV * JW : DK] = tail
    for s in range(2):
        b2[pl.ds(s, GROUPS, stride=2), :] = xt[HIST, s * GROUPS : (s + 1) * GROUPS, :]

    def narrow(i, _):
        b1[i] = f1[pl.ds(pl.multiple_of(i * 16, 8), 16), :].astype(BF16)
        return 0

    lax.fori_loop(0, GROUPS, narrow, 0)


def finish(a1, a2, gate, gain, live, weight, states, conv, partial, fc, fg):
    for h in range(HEADS):
        pieces = [a1[holder(h, jg)].astype(F32) for jg in range(JG)]
        for s in range(2):
            states[s, h] = jnp.concatenate([p[s * JW : (s + 1) * JW] for p in pieces], axis=0).T
    both = jnp.concatenate([a2[pl.ds(s, GROUPS, stride=2), :] for s in range(2)], axis=0)
    lead, rest = halves(both)
    wide = (DK, BLOCKS * DK)
    source = (iota(wide, 1) // DK) * JW + iota(wide, 1) % JW
    spread = jnp.where(iota(wide, 0) == source, 1.0, 0.0).astype(BF16)
    every = contract(lead, spread, 1, 0) + contract(rest, spread, 1, 0)
    own = iota((SLOTS, DK), 0) % GROUPS
    own = (own // 32) * 8 + own % 8
    own = jnp.where(own == iota((SLOTS, DK), 1) // JW, 1.0, 0.0)

    def block(b):
        picked = every[:, b * DK : (b + 1) * DK] * own
        rows = []
        for s in range(2):
            for h in range(HEADS):
                at = s * GROUPS + h * 8
                rows.append(
                    jnp.sum(picked[at : at + 8] + picked[at + 32 : at + 40], axis=0, keepdims=True)
                )
        return jnp.concatenate(rows, axis=0)

    for n in range(HIST):
        for part in range(3):
            kept = block(n * 3 + part)
            for s in range(2):
                for h in range(HEADS):
                    r = s * HEADS + h
                    fc[s, n, part : part + 1, h * DK : (h + 1) * DK] = kept[r : r + 1]
    conv[...] = fc[...].astype(BF16)

    fg[...] = jnp.zeros_like(fg)
    for t in range(STEPS):
        readout = block(CONV + t)
        scaling = lax.rsqrt(jnp.sum(readout * readout, axis=1, keepdims=True) / DK + EPS)
        logits = gate[t].astype(F32)
        gates = sigmoid(
            jnp.concatenate(
                [logits[s : s + 1, h * DK : (h + 1) * DK] for s in range(2) for h in range(HEADS)],
                axis=0,
            )
        )
        gated = readout * scaling * gain[...] * gates
        for s in range(2):
            alive = jnp.where(live[t, 0] > s, 1.0, 0.0)
            for h in range(HEADS):
                r = s * HEADS + h
                fg[2 * t + s : 2 * t + s + 1, h * DK : (h + 1) * DK] = gated[r : r + 1] * alive
    total = jnp.dot(fg[...].astype(BF16), weight[...], preferred_element_type=F32)
    width = partial.shape[2]
    share = total.shape[1] // partial.shape[0]
    for d in range(partial.shape[0]):
        turned = total if d == 0 else pltpu.roll(total, total.shape[1] - d * share, 1)
        partial[d] = turned[:, :width].astype(BF16)


def greet(axis, count):
    me = lax.axis_index(axis)
    barrier = pltpu.get_barrier_semaphore()

    def signal(k, _):
        pl.semaphore_signal(
            barrier,
            inc=1,
            device_id={axis: lax.rem(me + k, count)},
            device_id_type=pl.DeviceIdType.MESH,
        )
        return 0

    lax.fori_loop(1, count, signal, 0)
    pl.semaphore_wait(barrier, count - 1)
    return me


def remote(axis, peer, src, dst, send, recv):
    return pltpu.make_async_remote_copy(
        src_ref=src,
        dst_ref=dst,
        send_sem=send,
        recv_sem=recv,
        device_id={axis: peer},
        device_id_type=pl.DeviceIdType.MESH,
    )


def spread_kernel(s1, s2, r1, r2, sems, own):
    me = greet("rep", GROUPS)
    head = piece_of(me)[0]
    keep = [
        pltpu.make_async_copy(s1.at[me], r1.at[me], own.at[0]),
        pltpu.make_async_copy(s2.at[head], r2.at[me], own.at[1]),
    ]
    for copy in keep:
        copy.start()

    def send(k, _):
        p = lax.rem(me + k, GROUPS)
        remote("rep", p, s2.at[piece_of(p)[0]], r2.at[me], sems.at[2], sems.at[3]).start()
        remote("rep", p, s1.at[p], r1.at[me], sems.at[0], sems.at[1]).start()
        return 0

    lax.fori_loop(1, GROUPS, send, 0)
    for copy in keep:
        copy.wait()
    most = pl.ds(0, GROUPS - 1)
    for buf, n in ((r1, 0), (r2, 2)):
        done = remote("rep", me, buf.at[most], buf.at[most], sems.at[n], sems.at[n + 1])
        done.wait_send()
        done.wait_recv()


def swap_kernel(axis, count, *refs):
    pairs = (len(refs) - 2) // 2
    sources, lands, sems, own = refs[:pairs], refs[pairs : 2 * pairs], refs[-2], refs[-1]
    me = greet(axis, count)
    keep = [
        pltpu.make_async_copy(s.at[me], d.at[me], own.at[n])
        for n, (s, d) in enumerate(zip(sources, lands))
    ]
    for copy in keep:
        copy.start()

    def send(k, _):
        p = lax.rem(me + k, count)
        for n, (s, d) in enumerate(zip(sources, lands)):
            remote(axis, p, s.at[p], d.at[me], sems.at[2 * n], sems.at[2 * n + 1]).start()
        return 0

    lax.fori_loop(1, count, send, 0)
    for copy in keep:
        copy.wait()
    most = pl.ds(0, count - 1)
    for n, d in enumerate(lands):
        done = remote(axis, me, d.at[most], d.at[most], sems.at[2 * n], sems.at[2 * n + 1])
        done.wait_send()
        done.wait_recv()


VMEM = pl.BlockSpec(memory_space=pltpu.VMEM)
SMEM = pl.BlockSpec(memory_space=pltpu.SMEM)
ANY = pl.BlockSpec(memory_space=pl.ANY)
BIG = 48 * 1024 * 1024


def shape(dims, kind):
    return jax.ShapeDtypeStruct(dims, kind)


def do_pack(states, conv, proj, decay, beta, live):
    return pl.pallas_call(
        pack,
        out_shape=(shape((GROUPS, 16, DK), BF16), shape((HEADS, ROWS, DK), BF16)),
        in_specs=[VMEM] * 4 + [SMEM] * 2,
        out_specs=(VMEM, VMEM),
        scratch_shapes=[pltpu.VMEM((HEADS, ROWS, DK), F32)],
        compiler_params=pltpu.CompilerParams(vmem_limit_bytes=BIG),
        name="pack",
    )(states, conv, proj, decay, beta, live)


def do_spread(s1, s2):
    return pl.pallas_call(
        spread_kernel,
        out_shape=(shape((GROUPS, 16, DK), BF16), shape((GROUPS, ROWS, DK), BF16)),
        in_specs=[ANY] * 2,
        out_specs=(ANY, ANY),
        scratch_shapes=[pltpu.SemaphoreType.DMA((4,)), pltpu.SemaphoreType.DMA((2,))],
        compiler_params=pltpu.CompilerParams(collective_id=0, has_side_effects=True),
        name="spread",
    )(s1, s2)


def middle_kernel(where, r1, r2, weight, rate, targets, *rest):
    middle(where[0], where[1], r1, r2, weight, rate[where[0]], targets, *rest)


def do_middle(where, r1, r2, weight, rate, targets):
    return pl.pallas_call(
        middle_kernel,
        out_shape=(shape((GROUPS, 16, DK), BF16), shape((GROUPS * 2, DK), F32)),
        in_specs=[SMEM, VMEM, VMEM, VMEM, SMEM, VMEM],
        out_specs=(VMEM, VMEM),
        scratch_shapes=[
            pltpu.VMEM((GROUPS * 16, DK), F32),
            pltpu.VMEM((GROUPS * ROWS, DK), F32),
            pltpu.VMEM((JW, DK, SLOTS), F32),
            pltpu.VMEM((HIST + 1, 3 * DK, SLOTS), F32),
        ],
        compiler_params=pltpu.CompilerParams(vmem_limit_bytes=BIG),
        name="middle",
    )(where, r1, r2, weight, rate, targets)


def do_finish(a1, a2, gate, gain, live, weight, heads_axis):
    width = -(-(weight.shape[1] // heads_axis) // DK) * DK
    return pl.pallas_call(
        finish,
        out_shape=(
            shape((2, HEADS, DK, DK), F32),
            shape((2, HIST, 3, HEADS * DK), BF16),
            shape((heads_axis, 16, width), BF16),
        ),
        in_specs=[VMEM] * 4 + [SMEM] + [VMEM],
        out_specs=(VMEM, VMEM, VMEM),
        scratch_shapes=[
            pltpu.VMEM((2, HIST, 3, HEADS * DK), F32),
            pltpu.VMEM((16, HEADS * DK), F32),
        ],
        compiler_params=pltpu.CompilerParams(vmem_limit_bytes=BIG),
        name="finish",
    )(a1, a2, gate, gain, live, weight)


def do_swap(axis, count, tag, *sources):
    return pl.pallas_call(
        functools.partial(swap_kernel, axis, count),
        out_shape=tuple(shape(s.shape, s.dtype) for s in sources),
        in_specs=[ANY] * len(sources),
        out_specs=tuple([ANY] * len(sources)),
        scratch_shapes=[
            pltpu.SemaphoreType.DMA((2 * len(sources),)),
            pltpu.SemaphoreType.DMA((len(sources),)),
        ],
        compiler_params=pltpu.CompilerParams(collective_id=tag, has_side_effects=True),
        name="swap%d" % tag,
    )(*sources)


def local(
    heads_axis,
    states,
    conv_states,
    projected,
    conv_weight,
    decay_input,
    decay_rate,
    beta_logit,
    out_gate,
    norm_gain,
    out_weight,
    destinations,
    live_counts,
):
    me = lax.axis_index("rep")
    head, jg = piece_of(me)
    s1, s2 = do_pack(states, conv_states, projected, decay_input, beta_logit, live_counts)
    r1, r2 = do_spread(s1, s2)
    targets = destinations.reshape(STEPS, GROUPS, 2).transpose(0, 2, 1).reshape(STEPS, SLOTS)
    targets = (targets % 2) * GROUPS + targets // 2
    weight = lax.dynamic_slice_in_dim(conv_weight, head * DK, DK, axis=2).reshape(TAPS * 3, DK)
    weight = jnp.pad(weight, ((0, 16 - TAPS * 3), (0, 0)))
    where = jnp.stack([head, jg]).astype(jnp.int32)
    b1, b2 = do_middle(where, r1, r2, weight, decay_rate, targets)
    a1, a2 = do_swap("rep", GROUPS, 1, b1, b2.reshape(GROUPS, 2, DK))
    states_out, conv_out, partial = do_finish(
        a1,
        a2.reshape(GROUPS * 2, DK),
        out_gate,
        norm_gain.reshape(1, DK),
        live_counts,
        out_weight,
        heads_axis,
    )
    (shares,) = do_swap("head", heads_axis, 2, partial)
    share = out_weight.shape[1] // heads_axis
    out = jnp.sum(shares.astype(F32), axis=0)[: 2 * STEPS, :share].astype(BF16)
    return out.reshape(STEPS, 2, share), states_out, conv_out


def solution(mesh):
    placed = (
        P("rep", "head", None, None),
        P("rep", None, None, "head"),
        P(None, "rep", None, "head"),
        P(None, None, "head"),
        P(None, "rep", "head"),
        P("head"),
        P(None, "rep", "head"),
        P(None, "rep", "head"),
        P(),
        P("head", None),
        P(),
        P(None, "rep"),
    )
    return jax.shard_map(
        functools.partial(local, mesh.shape["head"]),
        mesh=mesh,
        in_specs=placed,
        out_specs=(
            P(None, "rep", "head"),
            P("rep", "head", None, None),
            P("rep", None, None, "head"),
        ),
        check_vma=False,
    )
```

```python
import functools

import jax
import jax.numpy as jnp
from jax import lax
from jax.experimental import pallas as pl
from jax.experimental.pallas import tpu as pltpu
from jax.sharding import PartitionSpec as P

F32, BF16 = jnp.float32, jnp.bfloat16
STEPS, TAPS = 6, 4
HIST = TAPS - 1
ZS, XS, CS = 8, 4, 2
GROUPS, HEADS, DK = 64, 4, 128
SLOTS = 2 * GROUPS
JG, JW = 16, 8
WIN = HIST + STEPS
ROW_HI = WIN * 4
ROW_LO = ROW_HI + 2 * STEPS
ROWS = 64
LANE_ALIVE = WIN * JW
LANE_BETA = LANE_ALIVE + 8
CONV = 3 * HIST
BLOCKS = CONV + STEPS
EPS = 1e-6


def holder(h, jg):
    return (jg % 8) * ZS + (jg // 8) * HEADS + h


def iota(shape, dim):
    return lax.broadcasted_iota(jnp.int32, shape, dim)


def contract(a, b, da, db):
    return lax.dot_general(a, b, (((da,), (db,)), ((), ())), preferred_element_type=F32)


def halves(x):
    lead = x.astype(BF16)
    return lead, (x - lead.astype(F32)).astype(BF16)


def sigmoid(x):
    return 1.0 / (1.0 + jnp.exp(-x))


def softplus(x):
    return jnp.maximum(x, 0.0) + jnp.log1p(jnp.exp(-jnp.abs(x)))


def inner(slot):
    group = slot >> 1
    return ((slot & 1) << 6) + ((group & 1) << 5) + (((group >> 1) & 3) << 3) + (group >> 3)


def own_lanes():
    group = iota((SLOTS, DK), 0) & 63
    piece = (group >> 3) + ((group & 4) << 1)
    return jnp.where(piece == iota((SLOTS, DK), 1) >> 3, 1.0, 0.0)


def by_head(x):
    return [
        jnp.concatenate([x[s : s + 1, h * DK : (h + 1) * DK] for h in range(HEADS)], axis=0)
        for s in range(2)
    ]


def pack_inputs(conv, proj, decay, s2, f):
    for w in range(WIN):
        for part in range(2):
            block = (conv[w, part] if w < HIST else proj[w - HIST, part]).astype(F32)
            at = (w * 2 + part) * 2
            for h in range(HEADS):
                f[h, at : at + 2, :] = block[:, h * DK : (h + 1) * DK]
    for t in range(STEPS):
        lead, rest = halves(decay[t])
        lead, rest = lead.astype(F32), rest.astype(F32)
        for h in range(HEADS):
            cols = slice(h * DK, (h + 1) * DK)
            f[h, ROW_HI + 2 * t : ROW_HI + 2 * t + 2, :] = lead[:, cols]
            f[h, ROW_LO + 2 * t : ROW_LO + 2 * t + 2, :] = rest[:, cols]
    for h in range(HEADS):
        f[h, ROW_LO + 2 * STEPS : ROWS, :] = jnp.zeros((ROWS - ROW_LO - 2 * STEPS, DK), F32)
        s2[h] = f[h].astype(BF16)


def pack_values(conv, proj, beta, live, s3):
    mask = own_lanes()
    parts = []
    for w in range(WIN):
        block = (conv[w, 2] if w < HIST else proj[w - HIST, 2]).astype(F32)
        rows = []
        for four in by_head(block):
            rows += [four] * (2 * ZS)
        parts.append((jnp.concatenate(rows, axis=0) * mask).astype(BF16))
    shape = (WIN * DK, DK)
    place = jnp.where(((iota(shape, 0) >> 7) << 3) + (iota(shape, 0) & 7) == iota(shape, 1), 1.0, 0.0)
    packed = contract(jnp.concatenate(parts, axis=1), place.astype(BF16), 1, 0)
    for s in range(2):
        alive = jnp.where(live[...] > s, 1.0, 0.0)
        row = jnp.concatenate(
            [
                jnp.zeros((HEADS, LANE_ALIVE), F32),
                jnp.broadcast_to(alive, (HEADS, STEPS)),
                jnp.zeros((HEADS, 8 - STEPS), F32),
                beta[s],
                jnp.zeros((HEADS, DK - LANE_BETA - STEPS), F32),
            ],
            axis=1,
        )
        rest = jnp.concatenate([row] * (2 * ZS), axis=0)
        s3[:, s, :] = packed[s * GROUPS : (s + 1) * GROUPS] + rest


def pack_states(states, s1):
    for h in range(HEADS):
        first, second = states[0, h].T, states[1, h].T
        for jg in range(JG):
            rows = slice(jg * JW, (jg + 1) * JW)
            s1[holder(h, jg)] = jnp.concatenate([first[rows], second[rows]], axis=0).astype(BF16)


def widen_inputs(r2, f2, core, x):
    def one(i, _):
        at = pl.multiple_of(((core * XS + x) * ZS + i) * ROWS, ROWS)
        f2[pl.ds(at, ROWS), :] = r2[core, x, i].astype(F32)
        return 0

    lax.fori_loop(0, ZS, one, 0)


def enter_states(r1, f1, mem):
    def one(i, _):
        f1[pl.ds(pl.multiple_of(i * 16, 16), 16), :] = r1[i].astype(F32)
        return 0

    lax.fori_loop(0, GROUPS, one, 0)
    for j in range(JW):
        rows = [f1[pl.ds(s * JW + j, GROUPS, stride=16), :] for s in range(2)]
        mem[j] = jnp.concatenate(rows, axis=0).T


def find_places(targets, places):
    square = (SLOTS, SLOTS)
    back = jnp.where(inner(iota(square, 0)) == iota(square, 1), 1.0, 0.0).astype(BF16)
    held = back
    for t in range(STEPS):
        move = jnp.where(iota(square, 0) == inner(targets[t : t + 1, :]), 1.0, 0.0).astype(BF16)
        place = contract(move, held, 1, 0).astype(BF16)
        places[t] = place
        if t < STEPS - 1:
            held = contract(back, place, 1, 0).astype(BF16)


def run_steps(jg, f2, r3, weight, rate, places, mem, xt):
    def both(row):
        return jnp.concatenate(
            [f2[pl.ds(row + s, GROUPS, stride=ROWS), :] for s in range(2)], axis=0
        )

    square = (SLOTS, SLOTS)
    eye = jnp.where(iota(square, 0) == iota(square, 1), 1.0, 0.0).astype(BF16)
    taps = [weight[part].T for part in range(3)]
    xt[0:DK, 0:TAPS] = taps[2]
    mine = pl.ds(pl.multiple_of(jg * JW, JW), JW)
    value_taps = xt[mine, 0:TAPS]
    values = jnp.concatenate([r3[:, s, :] for s in range(2)], axis=0)
    lead3, rest3 = halves(values)

    def pair(w, extra, at):
        x = jnp.concatenate([both(w * 4), both(w * 4 + 2)] + extra, axis=1)
        return contract(x.astype(BF16), at, 0, 0)

    start = contract(lead3, eye, 0, 0)
    hist = []
    for w in range(HIST):
        two = pair(w, [], eye)
        hist.append([two[:DK], two[DK:], start[w * JW : (w + 1) * JW]])
    readouts = []
    for t in range(STEPS):
        place = places[t]
        four = pair(t + HIST, [both(ROW_HI + 2 * t), both(ROW_LO + 2 * t)], place)
        decay = four[2 * DK : 3 * DK] + four[3 * DK :]
        small = contract(lead3, place, 0, 0) + contract(rest3, place, 0, 0)
        new = [four[:DK], four[DK : 2 * DK], small[(t + HIST) * JW : (t + HIST + 1) * JW]]
        alive = small[LANE_ALIVE + t : LANE_ALIVE + t + 1] > 0.5
        logit = small[LANE_BETA + t : LANE_BETA + t + 1]
        strength = jnp.where(alive, sigmoid(logit), 0.0)
        retain = jnp.where(alive, jnp.exp(-rate * softplus(decay)), 1.0)
        window = hist + [new]
        acts = []
        for part in range(3):
            cols = value_taps if part == 2 else taps[part]
            total = window[0][part] * cols[:, 0:1]
            for n in range(1, TAPS):
                total = total + window[n][part] * cols[:, n : n + 1]
            acts.append(total / (1.0 + jnp.exp(-total)))
        hist = [
            [jnp.where(alive, window[n + 1][part], window[n][part]) for part in range(3)]
            for n in range(HIST)
        ]
        query, key, value = acts
        query = query / jnp.sqrt(jnp.sum(query * query, axis=0, keepdims=True) + EPS)
        key = key / jnp.sqrt(jnp.sum(key * key, axis=0, keepdims=True) + EPS)
        rows = []
        for j in range(JW):
            decayed = retain * mem[j]
            recalled = jnp.sum(key * decayed, axis=0, keepdims=True)
            updated = decayed + key * (strength * (value[j : j + 1] - recalled))
            mem[j] = updated
            rows.append(jnp.sum(query * updated, axis=0, keepdims=True) * DK**-0.5)
        lead, rest = halves(jnp.concatenate(rows, axis=0))
        readouts.append(contract(place, lead, 1, 1) + contract(place, rest, 1, 1))
    kept = []
    for n in range(HIST):
        for part in range(3):
            block = hist[n][part]
            if part < 2:
                xt[...] = block
                block = xt[mine, :]
            kept.append(block)
    kept = jnp.concatenate(kept, axis=0).astype(BF16)
    kept = contract(places[STEPS - 1], kept, 1, 1)
    pad = jnp.zeros((SLOTS, DK - BLOCKS * JW), F32)
    return jnp.concatenate([kept] + readouts + [pad], axis=1)


def leave_states(place, mem, f1, b1):
    for j in range(JW):
        final = contract(place, mem[j].astype(BF16), 1, 1)
        for s in range(2):
            f1[pl.ds(s * JW + j, GROUPS, stride=16), :] = final[s * GROUPS : (s + 1) * GROUPS]

    def one(i, _):
        b1[i] = f1[pl.ds(pl.multiple_of(i * 16, 16), 16), :].astype(BF16)
        return 0

    lax.fori_loop(0, GROUPS, one, 0)


def finish_rows(a2, gate, gain, live, weight, conv, partial, fc, fg):
    lead, rest = halves(jnp.concatenate([a2[:, s, :] for s in range(2)], axis=0))
    wide = (DK, BLOCKS * DK)
    source = ((iota(wide, 1) >> 7) << 3) + (iota(wide, 1) & 7)
    spread = jnp.where(iota(wide, 0) == source, 1.0, 0.0).astype(BF16)
    every = contract(lead, spread, 1, 0) + contract(rest, spread, 1, 0)
    mask = own_lanes()

    def block(b):
        picked = every[:, b * DK : (b + 1) * DK] * mask
        rows = []
        for s in range(2):
            total = picked[s * GROUPS : s * GROUPS + ZS]
            for n in range(1, GROUPS // ZS):
                total = total + picked[s * GROUPS + n * ZS : s * GROUPS + (n + 1) * ZS]
            rows.append(total[:HEADS] + total[HEADS:])
        return jnp.concatenate(rows, axis=0)

    fg[...] = jnp.zeros_like(fg)
    second = iota((2 * HEADS, DK), 0) >> 2
    for t in range(STEPS):
        readout = block(CONV + t)
        scaling = lax.rsqrt(jnp.sum(readout * readout, axis=1, keepdims=True) / DK + EPS)
        gates = sigmoid(jnp.concatenate(by_head(gate[t].astype(F32)), axis=0))
        gated = readout * scaling * gain[...] * gates
        gated = jnp.where(live[0:1, t : t + 1] > second, gated, 0.0)
        for s in range(2):
            for h in range(HEADS):
                r = s * HEADS + h
                fg[2 * t + s : 2 * t + s + 1, h * DK : (h + 1) * DK] = gated[r : r + 1]
    total = jnp.dot(fg[...].astype(BF16), weight[...], preferred_element_type=F32)
    width = partial.shape[2]
    share = total.shape[1] // partial.shape[0]
    for d in range(partial.shape[0]):
        turned = total if d == 0 else pltpu.roll(total, total.shape[1] - d * share, 1)
        partial[d] = turned[:, :width].astype(BF16)
    for n in range(HIST):
        for part in range(3):
            kept = block(n * 3 + part)
            for s in range(2):
                for h in range(HEADS):
                    r = s * HEADS + h
                    fc[n, part, s : s + 1, h * DK : (h + 1) * DK] = kept[r : r + 1]
    conv[...] = fc[...].astype(BF16)


def finish_states(a1, states):
    for h in range(HEADS):
        pieces = [a1[holder(h, jg)].astype(F32) for jg in range(JG)]
        for s in range(2):
            states[s, h] = jnp.concatenate([p[s * JW : (s + 1) * JW] for p in pieces], axis=0).T


def remote(axis, peer, src, dst, sems, n):
    return pltpu.make_async_remote_copy(
        src_ref=src,
        dst_ref=dst,
        send_sem=sems.at[0, n],
        recv_sem=sems.at[1, n],
        device_id={axis: peer},
        device_id_type=pl.DeviceIdType.MESH,
    )


def whole(
    columns,
    states_in,
    conv_in,
    proj_in,
    taps_in,
    decay_in,
    rate_in,
    beta_in,
    gate_in,
    gain_in,
    weight_in,
    targets_in,
    live_in,
    out_to,
    states_to,
    conv_to,
    states,
    conv,
    proj,
    taps,
    decay,
    rate,
    beta,
    gate,
    gain,
    weight,
    targets,
    live,
    out,
    conv_out,
    s1,
    s2,
    s3,
    r1,
    r2,
    r3,
    b1,
    b2,
    a1,
    a2,
    partial,
    shares,
    f,
    f1,
    f2,
    mem,
    places,
    xt,
    fc,
    fg,
    local,
    sems,
):
    me = lax.axis_index("rep")
    col = lax.axis_index("head")
    z, x, core = me // (XS * CS), (me // CS) % XS, me % CS
    mine = (core * XS + x) * ZS + z
    head, jg = z % HEADS, (z // HEADS) * 8 + core * XS + x

    barrier = pltpu.get_barrier_semaphore()

    def greet(k, _):
        pl.semaphore_signal(
            barrier,
            inc=1,
            device_id={"rep": lax.rem(me + k, GROUPS)},
            device_id_type=pl.DeviceIdType.MESH,
        )
        return 0

    lax.fori_loop(1, GROUPS, greet, 0)
    for k in range(1, columns):
        pl.semaphore_signal(
            barrier,
            inc=1,
            device_id={"head": lax.rem(col + k, columns)},
            device_id_type=pl.DeviceIdType.MESH,
        )

    loads = [
        pltpu.make_async_copy(src, dst, local.at[n])
        for n, (src, dst) in enumerate(
            [
                (conv_in, conv),
                (proj_in, proj),
                (decay_in, decay),
                (beta_in, beta),
                (live_in, live),
                (states_in, states),
                (targets_in, targets),
                (taps_in, taps),
                (rate_in, rate),
                (gate_in, gate),
                (gain_in, gain),
                (weight_in, weight),
            ]
        )
    ]
    for load in loads:
        load.start()
    for load in loads[:3]:
        load.wait()
    pack_inputs(conv, proj, decay, s2, f)
    pl.semaphore_wait(barrier, GROUPS - 1 + columns - 1)

    keep = pltpu.make_async_copy(s2.at[head], r2.at[core, x, z], local.at[12])
    keep.start()
    for k in (4, 3, 5, 2, 6, 1, 7):
        to = lax.rem(z + k, ZS)
        peer = (to * XS + x) * CS + core
        remote("rep", peer, s2.at[lax.rem(to, HEADS)], r2.at[core, x, z], sems, 0).start()

    for load in loads[3:6]:
        load.wait()
    pack_values(conv, proj, beta, live, s3)
    pack_states(states, s1)

    keep.wait()
    done = remote("rep", me, r2.at[0, 0, pl.ds(0, ZS - 1)], r2.at[0, 0, pl.ds(0, ZS - 1)], sems, 0)
    done.wait_send()
    done.wait_recv()
    across = []
    for k in (2, 1, 3):
        to = lax.rem(x + k, XS)
        across.append(
            remote("rep", (z * XS + to) * CS + core, r2.at[core, x], r2.at[core, x], sems, k)
        )
        across[-1].start()
    other = me + 1 - 2 * core
    remote("rep", other, r2.at[core, x], r2.at[core, x], sems, 4).start()

    keep = [
        pltpu.make_async_copy(s1.at[mine], r1.at[mine], local.at[13]),
        pltpu.make_async_copy(s3.at[mine], r3.at[mine], local.at[14]),
    ]
    for copy in keep:
        copy.start()

    def to_all(pairs):
        def one(p):
            at = ((p % CS) * XS + (p // CS) % XS) * ZS + p // (XS * CS)
            for src, dst, n in pairs:
                remote("rep", p, src.at[at], dst.at[mine], sems, n).start()

        def send(i, _):
            one(lax.rem(me + 31 - i, GROUPS))
            one(lax.rem(me + GROUPS - 31 + i, GROUPS))
            return 0

        one(lax.rem(me + GROUPS // 2, GROUPS))
        lax.fori_loop(0, GROUPS // 2 - 1, send, 0)

    def from_all(dst, n):
        most = dst.at[pl.ds(0, GROUPS - 1)]
        done = remote("rep", me, most, most, sems, n)
        done.wait_send()
        done.wait_recv()

    to_all([(s3, r3, 5), (s1, r1, 6)])

    widen_inputs(r2, f2, core, x)
    for load in loads[6:9]:
        load.wait()
    find_places(targets, places)
    for n, k in enumerate((2, 1, 3)):
        origin = lax.rem(x + XS - k, XS)
        across[n].wait_recv()
        remote("rep", other, r2.at[core, origin], r2.at[core, origin], sems, 4).start()
        widen_inputs(r2, f2, core, origin)
    for copy in keep:
        copy.wait()
    from_all(r1, 6)
    enter_states(r1, f1, mem)
    for copy in across:
        copy.wait_send()
    done = remote("rep", me, r2.at[0], r2.at[0], sems, 4)
    done.wait_send()
    done.wait_recv()
    for n in range(XS):
        widen_inputs(r2, f2, 1 - core, n)
    from_all(r3, 5)

    rate_here = jnp.sum(
        jnp.where(iota((1, HEADS), 1) == head, rate[...], 0.0), axis=1, keepdims=True
    )
    cols = pl.ds(pl.multiple_of(head * DK, DK), DK)
    returned = run_steps(jg, f2, r3, taps.at[:, :, cols], rate_here, places, mem, xt)
    for s in range(2):
        b2[:, s, :] = returned[s * GROUPS : (s + 1) * GROUPS]
    keep = pltpu.make_async_copy(b2.at[mine], a2.at[mine], local.at[12])
    keep.start()
    to_all([(b2, a2, 7)])
    leave_states(places[STEPS - 1], mem, f1, b1)
    keep_states = pltpu.make_async_copy(b1.at[mine], a1.at[mine], local.at[13])
    keep_states.start()
    to_all([(b1, a1, 8)])

    for load in loads[9:]:
        load.wait()
    keep.wait()
    from_all(a2, 7)
    finish_rows(a2, gate, gain, live, weight, conv_out, partial, fc, fg)
    keep = pltpu.make_async_copy(partial.at[col], shares.at[col], local.at[12])
    keep.start()
    for k in (4, 3, 5, 2, 6, 1, 7):
        to = lax.rem(col + k, columns)
        remote("head", to, partial.at[to], shares.at[col], sems, 9).start()
    stores = [pltpu.make_async_copy(conv_out, conv_to, local.at[14])]
    stores[0].start()

    keep_states.wait()
    from_all(a1, 8)
    finish_states(a1, states)
    stores.append(pltpu.make_async_copy(states, states_to, local.at[13]))
    stores[1].start()

    keep.wait()
    most = shares.at[pl.ds(0, columns - 1)]
    done = remote("head", col, most, most, sems, 9)
    done.wait_send()
    done.wait_recv()
    total = shares[0].astype(F32)
    for n in range(1, columns):
        total = total + shares[n].astype(F32)
    for t in range(STEPS):
        out[t] = total[2 * t : 2 * t + 2, : out.shape[2]].astype(BF16)
    stores.append(pltpu.make_async_copy(out, out_to, local.at[12]))
    stores[2].start()
    for store in stores:
        store.wait()


def shape(dims, kind):
    return jax.ShapeDtypeStruct(dims, kind)


def local(columns, *args):
    (
        states,
        conv_states,
        projected,
        conv_weight,
        decay_input,
        decay_rate,
        beta_logit,
        out_gate,
        norm_gain,
        out_weight,
        destinations,
        live_counts,
    ) = args
    operands = (
        states,
        conv_states.transpose(1, 2, 0, 3),
        projected.transpose(0, 2, 1, 3),
        conv_weight.transpose(1, 0, 2),
        decay_input,
        decay_rate.reshape(1, HEADS),
        beta_logit.transpose(1, 2, 0),
        out_gate,
        norm_gain.reshape(1, DK),
        out_weight,
        destinations,
        live_counts.transpose(1, 0),
    )
    share = out_weight.shape[1] // columns
    width = -(-share // DK) * DK
    block = pltpu.VMEM((GROUPS, 16, DK), BF16)
    small = pltpu.VMEM((GROUPS, 2, DK), F32)
    any_ = pl.BlockSpec(memory_space=pl.ANY)
    out, states_out, conv_out = pl.pallas_call(
        functools.partial(whole, columns),
        out_shape=(
            shape((STEPS, 2, share), BF16),
            shape(states.shape, F32),
            shape(operands[1].shape, BF16),
        ),
        in_specs=[any_] * len(operands),
        out_specs=(any_,) * 3,
        scratch_shapes=[pltpu.VMEM(a.shape, a.dtype) for a in operands]
        + [
            pltpu.VMEM((STEPS, 2, share), BF16),
            pltpu.VMEM(operands[1].shape, BF16),
            block,
            pltpu.VMEM((HEADS, ROWS, DK), BF16),
            small,
            block,
            pltpu.VMEM((CS, XS, ZS, ROWS, DK), BF16),
            small,
            block,
            small,
            block,
            small,
            pltpu.VMEM((columns, 16, width), BF16),
            pltpu.VMEM((columns, 16, width), BF16),
            pltpu.VMEM((HEADS, ROWS, DK), F32),
            pltpu.VMEM((GROUPS * 16, DK), F32),
            pltpu.VMEM((GROUPS * ROWS, DK), F32),
            pltpu.VMEM((JW, DK, SLOTS), F32),
            pltpu.VMEM((STEPS, SLOTS, SLOTS), BF16),
            pltpu.VMEM((DK, SLOTS), F32),
            pltpu.VMEM(operands[1].shape, F32),
            pltpu.VMEM((16, HEADS * DK), F32),
            pltpu.SemaphoreType.DMA((15,)),
            pltpu.SemaphoreType.DMA((2, 10)),
        ],
        compiler_params=pltpu.CompilerParams(
            collective_id=0, has_side_effects=True, vmem_limit_bytes=48 * 1024 * 1024
        ),
        name="kda_steps",
    )(*operands)
    return out, states_out, conv_out.transpose(2, 0, 1, 3)


def solution(mesh):
    placed = (
        P("rep", "head", None, None),
        P("rep", None, None, "head"),
        P(None, "rep", None, "head"),
        P(None, None, "head"),
        P(None, "rep", "head"),
        P("head"),
        P(None, "rep", "head"),
        P(None, "rep", "head"),
        P(),
        P("head", None),
        P(),
        P(None, "rep"),
    )
    return jax.shard_map(
        functools.partial(local, mesh.shape["head"]),
        mesh=mesh,
        in_specs=placed,
        out_specs=(
            P(None, "rep", "head"),
            P("rep", "head", None, None),
            P("rep", None, None, "head"),
        ),
        check_vma=False,
    )
```

```python
import functools

import jax
import jax.numpy as jnp
from jax import lax
from jax.experimental import pallas as pl
from jax.experimental.pallas import tpu as pltpu
from jax.sharding import PartitionSpec as P

F32, BF16 = jnp.float32, jnp.bfloat16
STEPS, TAPS = 6, 4
HIST = TAPS - 1
ZS, XS, CS = 8, 4, 2
GROUPS, HEADS, DK = 64, 4, 128
SLOTS = 2 * GROUPS
JG, JW = 16, 8
WIN = HIST + STEPS
ROW_DECAY = WIN * 4
ROWS = ROW_DECAY + 2 * STEPS
LANE_ALIVE = WIN * JW
LANE_BETA = LANE_ALIVE + 8
CONV = 3 * HIST
BLOCKS = CONV + STEPS
EPS = 1e-6


def holder(h, jg):
    return (jg % 8) * ZS + (jg // 8) * HEADS + h


def iota(shape, dim):
    return lax.broadcasted_iota(jnp.int32, shape, dim)


def contract(a, b, da, db):
    return lax.dot_general(a, b, (((da,), (db,)), ((), ())), preferred_element_type=F32)


def halves(x):
    lead = x.astype(BF16)
    return lead, (x - lead.astype(F32)).astype(BF16)


def sigmoid(x):
    return 1.0 / (1.0 + jnp.exp(-x))


def softplus(x):
    return jnp.maximum(x, 0.0) + jnp.log1p(jnp.exp(-jnp.abs(x)))


def inner(slot):
    group = slot >> 1
    return ((slot & 1) << 6) + ((group & 1) << 5) + (((group >> 1) & 3) << 3) + (group >> 3)


def own_lanes():
    group = iota((SLOTS, DK), 0) & 63
    piece = (group >> 3) + ((group & 4) << 1)
    return jnp.where(piece == iota((SLOTS, DK), 1) >> 3, 1.0, 0.0)


def by_head(x):
    return [
        jnp.concatenate([x[s : s + 1, h * DK : (h + 1) * DK] for h in range(HEADS)], axis=0)
        for s in range(2)
    ]


def pack_inputs(conv, proj, decay, rate, s2, f):
    for w in range(WIN):
        for part in range(2):
            block = (conv[w, part] if w < HIST else proj[w - HIST, part]).astype(F32)
            at = (w * 2 + part) * 2
            for h in range(HEADS):
                f[h, at : at + 2, :] = block[:, h * DK : (h + 1) * DK]
    for t in range(STEPS):
        exponent = softplus(decay[t])
        for h in range(HEADS):
            at = ROW_DECAY + 2 * t
            f[h, at : at + 2, :] = exponent[:, h * DK : (h + 1) * DK] * rate[0:1, h : h + 1]
    for h in range(HEADS):
        s2[h] = f[h].astype(BF16)


def pack_values(conv, proj, beta, live, s3):
    mask = own_lanes()
    parts = []
    for w in range(WIN):
        block = (conv[w, 2] if w < HIST else proj[w - HIST, 2]).astype(F32)
        rows = []
        for four in by_head(block):
            rows += [four] * (2 * ZS)
        parts.append((jnp.concatenate(rows, axis=0) * mask).astype(BF16))
    shape = (WIN * DK, DK)
    place = jnp.where(((iota(shape, 0) >> 7) << 3) + (iota(shape, 0) & 7) == iota(shape, 1), 1.0, 0.0)
    packed = contract(jnp.concatenate(parts, axis=1), place.astype(BF16), 1, 0)
    for s in range(2):
        alive = jnp.where(live[...] > s, 1.0, 0.0)
        row = jnp.concatenate(
            [
                jnp.zeros((HEADS, LANE_ALIVE), F32),
                jnp.broadcast_to(alive, (HEADS, STEPS)),
                jnp.zeros((HEADS, 8 - STEPS), F32),
                beta[s],
                jnp.zeros((HEADS, DK - LANE_BETA - STEPS), F32),
            ],
            axis=1,
        )
        rest = jnp.concatenate([row] * (2 * ZS), axis=0)
        s3[:, s, :] = packed[s * GROUPS : (s + 1) * GROUPS] + rest


def pack_states(states, s1):
    for h in range(HEADS):
        first, second = states[0, h].T, states[1, h].T
        for jg in range(JG):
            rows = slice(jg * JW, (jg + 1) * JW)
            s1[holder(h, jg)] = jnp.concatenate([first[rows], second[rows]], axis=0).astype(BF16)


def widen_inputs(r2, f2, core, x, first, last):
    def one(i, _):
        at = pl.multiple_of(((core * XS + x) * ZS + i) * ROWS, ROWS)
        f2[pl.ds(at, ROWS), :] = r2[core, x, i].astype(F32)
        return 0

    lax.fori_loop(first, last, one, 0)


def enter_states(r1, f1, mem):
    def one(i, _):
        f1[pl.ds(pl.multiple_of(i * 16, 16), 16), :] = r1[i].astype(F32)
        return 0

    lax.fori_loop(0, GROUPS, one, 0)
    for j in range(JW):
        rows = [f1[pl.ds(s * JW + j, GROUPS, stride=16), :] for s in range(2)]
        mem[j] = jnp.concatenate(rows, axis=0).T


def find_places(targets, places):
    square = (SLOTS, SLOTS)
    back = jnp.where(inner(iota(square, 0)) == iota(square, 1), 1.0, 0.0).astype(BF16)
    held = back
    for t in range(STEPS):
        move = jnp.where(iota(square, 0) == inner(targets[t : t + 1, :]), 1.0, 0.0).astype(BF16)
        place = contract(move, held, 1, 0).astype(BF16)
        places[t] = place
        if t < STEPS - 1:
            held = contract(back, place, 1, 0).astype(BF16)


def run_steps(jg, f2, r3, weight, places, mem, xt):
    def both(row):
        return jnp.concatenate(
            [f2[pl.ds(row + s, GROUPS, stride=ROWS), :] for s in range(2)], axis=0
        )

    square = (SLOTS, SLOTS)
    eye = jnp.where(iota(square, 0) == iota(square, 1), 1.0, 0.0).astype(BF16)
    taps = [weight[part].T for part in range(3)]
    xt[0:DK, 0:TAPS] = taps[2]
    mine = pl.ds(pl.multiple_of(jg * JW, JW), JW)
    value_taps = xt[mine, 0:TAPS]
    values = jnp.concatenate([r3[:, s, :] for s in range(2)], axis=0)
    lead3, rest3 = halves(values)

    def pair(w, extra, at):
        x = jnp.concatenate([both(w * 4), both(w * 4 + 2)] + extra, axis=1)
        return contract(x.astype(BF16), at, 0, 0)

    start = contract(lead3, eye, 0, 0)
    hist = []
    for w in range(HIST):
        two = pair(w, [], eye)
        hist.append([two[:DK], two[DK:], start[w * JW : (w + 1) * JW]])
    readouts = []
    for t in range(STEPS):
        place = places[t]
        three = pair(t + HIST, [both(ROW_DECAY + 2 * t)], place)
        small = contract(lead3, place, 0, 0) + contract(rest3, place, 0, 0)
        new = [three[:DK], three[DK : 2 * DK], small[(t + HIST) * JW : (t + HIST + 1) * JW]]
        alive = small[LANE_ALIVE + t : LANE_ALIVE + t + 1] > 0.5
        logit = small[LANE_BETA + t : LANE_BETA + t + 1]
        strength = jnp.where(alive, sigmoid(logit), 0.0)
        retain = jnp.where(alive, jnp.exp(-three[2 * DK :]), 1.0)
        window = hist + [new]
        acts = []
        for part in range(3):
            cols = value_taps if part == 2 else taps[part]
            total = window[0][part] * cols[:, 0:1]
            for n in range(1, TAPS):
                total = total + window[n][part] * cols[:, n : n + 1]
            acts.append(total / (1.0 + jnp.exp(-total)))
        hist = [
            [jnp.where(alive, window[n + 1][part], window[n][part]) for part in range(3)]
            for n in range(HIST)
        ]
        query, key, value = acts
        query = query / jnp.sqrt(jnp.sum(query * query, axis=0, keepdims=True) + EPS)
        key = key / jnp.sqrt(jnp.sum(key * key, axis=0, keepdims=True) + EPS)
        rows = []
        for j in range(JW):
            decayed = retain * mem[j]
            recalled = jnp.sum(key * decayed, axis=0, keepdims=True)
            updated = decayed + key * (strength * (value[j : j + 1] - recalled))
            mem[j] = updated
            rows.append(jnp.sum(query * updated, axis=0, keepdims=True) * DK**-0.5)
        lead, rest = halves(jnp.concatenate(rows, axis=0))
        readouts.append(contract(place, lead, 1, 1) + contract(place, rest, 1, 1))
    kept = []
    for n in range(HIST):
        for part in range(3):
            block = hist[n][part]
            if part < 2:
                xt[...] = block
                block = xt[mine, :]
            kept.append(block)
    kept = jnp.concatenate(kept, axis=0).astype(BF16)
    kept = contract(places[STEPS - 1], kept, 1, 1)
    pad = jnp.zeros((SLOTS, DK - BLOCKS * JW), F32)
    return jnp.concatenate([kept] + readouts + [pad], axis=1)


def leave_states(place, mem, f1, b1):
    for j in range(JW):
        final = contract(place, mem[j].astype(BF16), 1, 1)
        for s in range(2):
            f1[pl.ds(s * JW + j, GROUPS, stride=16), :] = final[s * GROUPS : (s + 1) * GROUPS]

    def one(i, _):
        b1[i] = f1[pl.ds(pl.multiple_of(i * 16, 16), 16), :].astype(BF16)
        return 0

    lax.fori_loop(0, GROUPS, one, 0)


def finish_rows(a2, gate, gain, live, weight, conv, partial, fc, fg):
    lead, rest = halves(jnp.concatenate([a2[:, s, :] for s in range(2)], axis=0))
    wide = (DK, BLOCKS * DK)
    source = ((iota(wide, 1) >> 7) << 3) + (iota(wide, 1) & 7)
    spread = jnp.where(iota(wide, 0) == source, 1.0, 0.0).astype(BF16)
    every = contract(lead, spread, 1, 0) + contract(rest, spread, 1, 0)
    mask = own_lanes()

    def block(b):
        picked = every[:, b * DK : (b + 1) * DK] * mask
        rows = []
        for s in range(2):
            total = picked[s * GROUPS : s * GROUPS + ZS]
            for n in range(1, GROUPS // ZS):
                total = total + picked[s * GROUPS + n * ZS : s * GROUPS + (n + 1) * ZS]
            rows.append(total[:HEADS] + total[HEADS:])
        return jnp.concatenate(rows, axis=0)

    fg[...] = jnp.zeros_like(fg)
    second = iota((2 * HEADS, DK), 0) >> 2
    for t in range(STEPS):
        readout = block(CONV + t)
        scaling = lax.rsqrt(jnp.sum(readout * readout, axis=1, keepdims=True) / DK + EPS)
        gates = sigmoid(jnp.concatenate(by_head(gate[t].astype(F32)), axis=0))
        gated = readout * scaling * gain[...] * gates
        gated = jnp.where(live[0:1, t : t + 1] > second, gated, 0.0)
        for s in range(2):
            for h in range(HEADS):
                r = s * HEADS + h
                fg[2 * t + s : 2 * t + s + 1, h * DK : (h + 1) * DK] = gated[r : r + 1]
    total = jnp.dot(fg[...].astype(BF16), weight[...], preferred_element_type=F32)
    width = partial.shape[2]
    share = total.shape[1] // partial.shape[0]
    for d in range(partial.shape[0]):
        turned = total if d == 0 else pltpu.roll(total, total.shape[1] - d * share, 1)
        partial[d] = turned[:, :width].astype(BF16)
    for n in range(HIST):
        for part in range(3):
            kept = block(n * 3 + part)
            for s in range(2):
                for h in range(HEADS):
                    r = s * HEADS + h
                    fc[n, part, s : s + 1, h * DK : (h + 1) * DK] = kept[r : r + 1]
    conv[...] = fc[...].astype(BF16)


def finish_states(a1, states):
    for h in range(HEADS):
        pieces = [a1[holder(h, jg)].astype(F32) for jg in range(JG)]
        for s in range(2):
            states[s, h] = jnp.concatenate([p[s * JW : (s + 1) * JW] for p in pieces], axis=0).T


def remote(axis, peer, src, dst, sems, n):
    return pltpu.make_async_remote_copy(
        src_ref=src,
        dst_ref=dst,
        send_sem=sems.at[0, n],
        recv_sem=sems.at[1, n],
        device_id={axis: peer},
        device_id_type=pl.DeviceIdType.MESH,
    )


def whole(
    columns,
    states_in,
    conv_in,
    proj_in,
    taps_in,
    decay_in,
    rate_in,
    beta_in,
    gate_in,
    gain_in,
    weight_in,
    targets_in,
    live_in,
    out_to,
    states_to,
    conv_to,
    states,
    conv,
    proj,
    taps,
    decay,
    rate,
    beta,
    gate,
    gain,
    weight,
    targets,
    live,
    out,
    conv_out,
    s1,
    s2,
    s3,
    r1,
    r2,
    r3,
    b1,
    b2,
    a1,
    a2,
    partial,
    shares,
    f,
    f1,
    f2,
    mem,
    places,
    xt,
    fc,
    fg,
    local,
    sems,
):
    me = lax.axis_index("rep")
    col = lax.axis_index("head")
    z, x, core = me // (XS * CS), (me // CS) % XS, me % CS
    mine = (core * XS + x) * ZS + z
    head, jg = z % HEADS, (z // HEADS) * 8 + core * XS + x

    barrier = pltpu.get_barrier_semaphore()

    def greet(k, _):
        pl.semaphore_signal(
            barrier,
            inc=1,
            device_id={"rep": lax.rem(me + k, GROUPS)},
            device_id_type=pl.DeviceIdType.MESH,
        )
        return 0

    lax.fori_loop(1, GROUPS, greet, 0)
    for k in range(1, columns):
        pl.semaphore_signal(
            barrier,
            inc=1,
            device_id={"head": lax.rem(col + k, columns)},
            device_id_type=pl.DeviceIdType.MESH,
        )

    loads = [
        pltpu.make_async_copy(src, dst, local.at[n])
        for n, (src, dst) in enumerate(
            [
                (conv_in, conv),
                (proj_in, proj),
                (decay_in, decay),
                (rate_in, rate),
                (beta_in, beta),
                (live_in, live),
                (states_in, states),
                (targets_in, targets),
                (taps_in, taps),
                (gate_in, gate),
                (gain_in, gain),
                (weight_in, weight),
            ]
        )
    ]
    for load in loads:
        load.start()
    for load in loads[:4]:
        load.wait()
    pack_inputs(conv, proj, decay, rate, s2, f)
    pl.semaphore_wait(barrier, GROUPS - 1 + columns - 1)

    keep = pltpu.make_async_copy(s2.at[head], r2.at[core, x, z], local.at[12])
    keep.start()
    for k in (4, 3, 5, 2, 6, 1, 7):
        to = lax.rem(z + k, ZS)
        peer = (to * XS + x) * CS + core
        remote("rep", peer, s2.at[lax.rem(to, HEADS)], r2.at[core, x, z], sems, 0).start()

    for load in loads[4:7]:
        load.wait()
    pack_values(conv, proj, beta, live, s3)
    pack_states(states, s1)

    keep.wait()
    done = remote("rep", me, r2.at[0, 0, pl.ds(0, ZS - 1)], r2.at[0, 0, pl.ds(0, ZS - 1)], sems, 0)
    done.wait_send()
    done.wait_recv()
    right = (z * XS + lax.rem(x + 1, XS)) * CS + core
    left = (z * XS + lax.rem(x + XS - 1, XS)) * CS + core
    other = me + 1 - 2 * core
    half = ZS // 2
    behind, ahead = lax.rem(x + XS - 1, XS), lax.rem(x + 1, XS)

    def part(origin, n):
        return r2.at[core, origin, pl.ds(n * half, half)]

    def pass_on(peer, origin, n, sem):
        copy = remote("rep", peer, part(origin, n), part(origin, n), sems, sem)
        copy.start()
        return copy

    ring = [
        pass_on(right, x, 0, 1),
        pass_on(left, x, 1, 2),
        pass_on(right, x, 1, 3),
        pass_on(left, x, 0, 4),
    ]
    remote("rep", other, r2.at[core, x], r2.at[core, x], sems, 10).start()

    keep = [
        pltpu.make_async_copy(s1.at[mine], r1.at[mine], local.at[13]),
        pltpu.make_async_copy(s3.at[mine], r3.at[mine], local.at[14]),
    ]
    for copy in keep:
        copy.start()

    def to_all(pairs):
        def one(p):
            at = ((p % CS) * XS + (p // CS) % XS) * ZS + p // (XS * CS)
            for src, dst, n in pairs:
                remote("rep", p, src.at[at], dst.at[mine], sems, n).start()

        def send(i, _):
            one(lax.rem(me + 31 - i, GROUPS))
            one(lax.rem(me + GROUPS - 31 + i, GROUPS))
            return 0

        one(lax.rem(me + GROUPS // 2, GROUPS))
        lax.fori_loop(0, GROUPS // 2 - 1, send, 0)

    def from_all(dst, n):
        most = dst.at[pl.ds(0, GROUPS - 1)]
        done = remote("rep", me, most, most, sems, n)
        done.wait_send()
        done.wait_recv()

    to_all([(s3, r3, 5), (s1, r1, 6)])

    widen_inputs(r2, f2, core, x, 0, ZS)

    def arrived(copy, origin, n):
        copy.wait_recv()
        pass_on(other, origin, n, 10)
        widen_inputs(r2, f2, core, origin, n * half, (n + 1) * half)

    ring[0].wait_recv()
    ring.append(pass_on(right, behind, 0, 11))
    pass_on(other, behind, 0, 10)
    ring[1].wait_recv()
    ring.append(pass_on(left, ahead, 1, 12))
    pass_on(other, ahead, 1, 10)
    for load in loads[7:9]:
        load.wait()
    find_places(targets, places)
    widen_inputs(r2, f2, core, behind, 0, half)
    widen_inputs(r2, f2, core, ahead, half, ZS)
    arrived(ring[2], behind, 1)
    arrived(ring[3], ahead, 0)
    opposite = lax.rem(x + 2, XS)
    arrived(ring[4], opposite, 0)
    arrived(ring[5], opposite, 1)
    for copy in keep:
        copy.wait()
    from_all(r1, 6)
    enter_states(r1, f1, mem)
    for copy in ring:
        copy.wait_send()
    done = remote("rep", me, r2.at[0], r2.at[0], sems, 10)
    done.wait_send()
    done.wait_recv()
    for n in range(XS):
        widen_inputs(r2, f2, 1 - core, n, 0, ZS)
    from_all(r3, 5)

    cols = pl.ds(pl.multiple_of(head * DK, DK), DK)
    returned = run_steps(jg, f2, r3, taps.at[:, :, cols], places, mem, xt)
    for s in range(2):
        b2[:, s, :] = returned[s * GROUPS : (s + 1) * GROUPS]
    keep = pltpu.make_async_copy(b2.at[mine], a2.at[mine], local.at[12])
    keep.start()
    to_all([(b2, a2, 7)])
    leave_states(places[STEPS - 1], mem, f1, b1)
    keep_states = pltpu.make_async_copy(b1.at[mine], a1.at[mine], local.at[13])
    keep_states.start()
    to_all([(b1, a1, 8)])

    for load in loads[9:]:
        load.wait()
    keep.wait()
    from_all(a2, 7)
    finish_rows(a2, gate, gain, live, weight, conv_out, partial, fc, fg)
    keep = pltpu.make_async_copy(partial.at[col], shares.at[col], local.at[12])
    keep.start()
    for k in (4, 3, 5, 2, 6, 1, 7):
        to = lax.rem(col + k, columns)
        remote("head", to, partial.at[to], shares.at[col], sems, 9).start()
    stores = [pltpu.make_async_copy(conv_out, conv_to, local.at[14])]
    stores[0].start()

    keep_states.wait()
    from_all(a1, 8)
    finish_states(a1, states)
    stores.append(pltpu.make_async_copy(states, states_to, local.at[13]))
    stores[1].start()

    keep.wait()
    most = shares.at[pl.ds(0, columns - 1)]
    done = remote("head", col, most, most, sems, 9)
    done.wait_send()
    done.wait_recv()
    total = shares[0].astype(F32)
    for n in range(1, columns):
        total = total + shares[n].astype(F32)
    for t in range(STEPS):
        out[t] = total[2 * t : 2 * t + 2, : out.shape[2]].astype(BF16)
    stores.append(pltpu.make_async_copy(out, out_to, local.at[12]))
    stores[2].start()
    for store in stores:
        store.wait()


def shape(dims, kind):
    return jax.ShapeDtypeStruct(dims, kind)


def local(columns, *args):
    (
        states,
        conv_states,
        projected,
        conv_weight,
        decay_input,
        decay_rate,
        beta_logit,
        out_gate,
        norm_gain,
        out_weight,
        destinations,
        live_counts,
    ) = args
    operands = (
        states,
        conv_states.transpose(1, 2, 0, 3),
        projected.transpose(0, 2, 1, 3),
        conv_weight.transpose(1, 0, 2),
        decay_input,
        decay_rate.reshape(1, HEADS),
        beta_logit.transpose(1, 2, 0),
        out_gate,
        norm_gain.reshape(1, DK),
        out_weight,
        destinations,
        live_counts.transpose(1, 0),
    )
    share = out_weight.shape[1] // columns
    width = -(-share // DK) * DK
    block = pltpu.VMEM((GROUPS, 16, DK), BF16)
    small = pltpu.VMEM((GROUPS, 2, DK), F32)
    any_ = pl.BlockSpec(memory_space=pltpu.HBM)
    out, states_out, conv_out = pl.pallas_call(
        functools.partial(whole, columns),
        out_shape=(
            shape((STEPS, 2, share), BF16),
            shape(states.shape, F32),
            shape(operands[1].shape, BF16),
        ),
        in_specs=[any_] * len(operands),
        out_specs=(any_,) * 3,
        scratch_shapes=[pltpu.VMEM(a.shape, a.dtype) for a in operands]
        + [
            pltpu.VMEM((STEPS, 2, share), BF16),
            pltpu.VMEM(operands[1].shape, BF16),
            block,
            pltpu.VMEM((HEADS, ROWS, DK), BF16),
            small,
            block,
            pltpu.VMEM((CS, XS, ZS, ROWS, DK), BF16),
            small,
            block,
            small,
            block,
            small,
            pltpu.VMEM((columns, 16, width), BF16),
            pltpu.VMEM((columns, 16, width), BF16),
            pltpu.VMEM((HEADS, ROWS, DK), F32),
            pltpu.VMEM((GROUPS * 16, DK), F32),
            pltpu.VMEM((GROUPS * ROWS, DK), F32),
            pltpu.VMEM((JW, DK, SLOTS), F32),
            pltpu.VMEM((STEPS, SLOTS, SLOTS), BF16),
            pltpu.VMEM((DK, SLOTS), F32),
            pltpu.VMEM(operands[1].shape, F32),
            pltpu.VMEM((16, HEADS * DK), F32),
            pltpu.SemaphoreType.DMA((15,)),
            pltpu.SemaphoreType.DMA((2, 13)),
        ],
        compiler_params=pltpu.CompilerParams(
            collective_id=0, has_side_effects=True, vmem_limit_bytes=60 * 1024 * 1024
        ),
        name="kda_steps",
    )(*operands)
    return out, states_out, conv_out.transpose(2, 0, 1, 3)


def solution(mesh):
    placed = (
        P("rep", "head", None, None),
        P("rep", None, None, "head"),
        P(None, "rep", None, "head"),
        P(None, None, "head"),
        P(None, "rep", "head"),
        P("head"),
        P(None, "rep", "head"),
        P(None, "rep", "head"),
        P(),
        P("head", None),
        P(),
        P(None, "rep"),
    )
    return jax.shard_map(
        functools.partial(local, mesh.shape["head"]),
        mesh=mesh,
        in_specs=placed,
        out_specs=(
            P(None, "rep", "head"),
            P("rep", "head", None, None),
            P("rep", None, None, "head"),
        ),
        check_vma=False,
    )
```

```python
import functools

import jax
import jax.numpy as jnp
from jax import lax
from jax.experimental import pallas as pl
from jax.experimental.pallas import tpu as pltpu
from jax.sharding import PartitionSpec as P

F32, BF16 = jnp.float32, jnp.bfloat16
STEPS, TAPS = 6, 4
HIST = TAPS - 1
ZS, XS, CS = 8, 4, 2
GROUPS, HEADS, DK = 64, 4, 128
SLOTS = 2 * GROUPS
JG, JW = 16, 8
WIN = HIST + STEPS
ROW_DECAY = WIN * 4
ROWS = ROW_DECAY + 2 * STEPS
LANE_ALIVE = WIN * JW
LANE_BETA = LANE_ALIVE + 8
CONV = 3 * HIST
BLOCKS = CONV + STEPS
EPS = 1e-6


def holder(h, jg):
    return (jg % 8) * ZS + (jg // 8) * HEADS + h


def iota(shape, dim):
    return lax.broadcasted_iota(jnp.int32, shape, dim)


def contract(a, b, da, db):
    return lax.dot_general(a, b, (((da,), (db,)), ((), ())), preferred_element_type=F32)


def halves(x):
    lead = x.astype(BF16)
    return lead, (x - lead.astype(F32)).astype(BF16)


def sigmoid(x):
    return 1.0 / (1.0 + jnp.exp(-x))


def softplus(x):
    return jnp.maximum(x, 0.0) + jnp.log1p(jnp.exp(-jnp.abs(x)))


def inner(slot):
    group = slot >> 1
    return ((slot & 1) << 6) + ((group & 1) << 5) + (((group >> 1) & 3) << 3) + (group >> 3)


def own_lanes():
    group = iota((SLOTS, DK), 0) & 63
    piece = (group >> 3) + ((group & 4) << 1)
    return jnp.where(piece == iota((SLOTS, DK), 1) >> 3, 1.0, 0.0)


def by_head(x):
    return [
        jnp.concatenate([x[s : s + 1, h * DK : (h + 1) * DK] for h in range(HEADS)], axis=0)
        for s in range(2)
    ]


def pack_inputs(conv, proj, decay, rate, s2, f):
    for w in range(WIN):
        for part in range(2):
            block = (conv[w, part] if w < HIST else proj[w - HIST, part]).astype(F32)
            at = (w * 2 + part) * 2
            for h in range(HEADS):
                f[h, at : at + 2, :] = block[:, h * DK : (h + 1) * DK]
    for t in range(STEPS):
        exponent = softplus(decay[t])
        for h in range(HEADS):
            at = ROW_DECAY + 2 * t
            f[h, at : at + 2, :] = exponent[:, h * DK : (h + 1) * DK] * rate[0:1, h : h + 1]
    for h in range(HEADS):
        s2[h] = f[h].astype(BF16)


def pack_values(conv, proj, beta, live, s3):
    mask = own_lanes()
    parts = []
    for w in range(WIN):
        block = (conv[w, 2] if w < HIST else proj[w - HIST, 2]).astype(F32)
        rows = []
        for four in by_head(block):
            rows += [four] * (2 * ZS)
        parts.append((jnp.concatenate(rows, axis=0) * mask).astype(BF16))
    shape = (WIN * DK, DK)
    place = jnp.where(((iota(shape, 0) >> 7) << 3) + (iota(shape, 0) & 7) == iota(shape, 1), 1.0, 0.0)
    packed = contract(jnp.concatenate(parts, axis=1), place.astype(BF16), 1, 0)
    for s in range(2):
        alive = jnp.where(live[...] > s, 1.0, 0.0)
        row = jnp.concatenate(
            [
                jnp.zeros((HEADS, LANE_ALIVE), F32),
                jnp.broadcast_to(alive, (HEADS, STEPS)),
                jnp.zeros((HEADS, 8 - STEPS), F32),
                beta[s],
                jnp.zeros((HEADS, DK - LANE_BETA - STEPS), F32),
            ],
            axis=1,
        )
        rest = jnp.concatenate([row] * (2 * ZS), axis=0)
        s3[:, s, :] = packed[s * GROUPS : (s + 1) * GROUPS] + rest


def pack_states(states, s1):
    for h in range(HEADS):
        first, second = states[0, h].T, states[1, h].T
        for jg in range(JG):
            rows = slice(jg * JW, (jg + 1) * JW)
            s1[holder(h, jg)] = jnp.concatenate([first[rows], second[rows]], axis=0).astype(BF16)


def widen_inputs(r2, f2, core, x, first, last):
    def one(i, _):
        at = pl.multiple_of(((core * XS + x) * ZS + i) * ROWS, ROWS)
        f2[pl.ds(at, ROWS), :] = r2[core, x, i].astype(F32)
        return 0

    lax.fori_loop(first, last, one, 0)


def enter_states(r1, f1, mem):
    def one(i, _):
        f1[pl.ds(pl.multiple_of(i * 16, 16), 16), :] = r1[i].astype(F32)
        return 0

    lax.fori_loop(0, GROUPS, one, 0)
    for j in range(JW):
        rows = [f1[pl.ds(s * JW + j, GROUPS, stride=16), :] for s in range(2)]
        mem[j] = jnp.concatenate(rows, axis=0).T


def find_places(targets, places):
    square = (SLOTS, SLOTS)
    back = jnp.where(inner(iota(square, 0)) == iota(square, 1), 1.0, 0.0).astype(BF16)
    held = back
    for t in range(STEPS):
        move = jnp.where(iota(square, 0) == inner(targets[t : t + 1, :]), 1.0, 0.0).astype(BF16)
        place = contract(move, held, 1, 0).astype(BF16)
        places[t] = place
        if t < STEPS - 1:
            held = contract(back, place, 1, 0).astype(BF16)


def run_steps(jg, f2, r3, weight, places, mem, xt):
    def both(row):
        return jnp.concatenate(
            [f2[pl.ds(row + s, GROUPS, stride=ROWS), :] for s in range(2)], axis=0
        )

    square = (SLOTS, SLOTS)
    eye = jnp.where(iota(square, 0) == iota(square, 1), 1.0, 0.0).astype(BF16)
    taps = [weight[part].T for part in range(3)]
    xt[0:DK, 0:TAPS] = taps[2]
    mine = pl.ds(pl.multiple_of(jg * JW, JW), JW)
    value_taps = xt[mine, 0:TAPS]
    values = jnp.concatenate([r3[:, s, :] for s in range(2)], axis=0)
    lead3, rest3 = halves(values)

    def pair(w, extra, at):
        x = jnp.concatenate([both(w * 4), both(w * 4 + 2)] + extra, axis=1)
        return contract(x.astype(BF16), at, 0, 0)

    start = contract(lead3, eye, 0, 0)
    hist = []
    for w in range(HIST):
        two = pair(w, [], eye)
        hist.append([two[:DK], two[DK:], start[w * JW : (w + 1) * JW]])
    readouts = []
    for t in range(STEPS):
        place = places[t]
        three = pair(t + HIST, [both(ROW_DECAY + 2 * t)], place)
        small = contract(lead3, place, 0, 0) + contract(rest3, place, 0, 0)
        new = [three[:DK], three[DK : 2 * DK], small[(t + HIST) * JW : (t + HIST + 1) * JW]]
        alive = small[LANE_ALIVE + t : LANE_ALIVE + t + 1] > 0.5
        logit = small[LANE_BETA + t : LANE_BETA + t + 1]
        strength = jnp.where(alive, sigmoid(logit), 0.0)
        retain = jnp.where(alive, jnp.exp(-three[2 * DK :]), 1.0)
        window = hist + [new]
        acts = []
        for part in range(3):
            cols = value_taps if part == 2 else taps[part]
            total = window[0][part] * cols[:, 0:1]
            for n in range(1, TAPS):
                total = total + window[n][part] * cols[:, n : n + 1]
            acts.append(total / (1.0 + jnp.exp(-total)))
        hist = [
            [jnp.where(alive, window[n + 1][part], window[n][part]) for part in range(3)]
            for n in range(HIST)
        ]
        query, key, value = acts
        query = query / jnp.sqrt(jnp.sum(query * query, axis=0, keepdims=True) + EPS)
        key = key / jnp.sqrt(jnp.sum(key * key, axis=0, keepdims=True) + EPS)
        rows = []
        for j in range(JW):
            decayed = retain * mem[j]
            recalled = jnp.sum(key * decayed, axis=0, keepdims=True)
            updated = decayed + key * (strength * (value[j : j + 1] - recalled))
            mem[j] = updated
            rows.append(jnp.sum(query * updated, axis=0, keepdims=True) * DK**-0.5)
        lead, rest = halves(jnp.concatenate(rows, axis=0))
        readouts.append(contract(place, lead, 1, 1) + contract(place, rest, 1, 1))
    kept = []
    for n in range(HIST):
        for part in range(3):
            block = hist[n][part]
            if part < 2:
                xt[...] = block
                block = xt[mine, :]
            kept.append(block)
    kept = jnp.concatenate(kept, axis=0).astype(BF16)
    kept = contract(places[STEPS - 1], kept, 1, 1)
    pad = jnp.zeros((SLOTS, DK - BLOCKS * JW), F32)
    return jnp.concatenate([kept] + readouts + [pad], axis=1)


def leave_states(place, mem, f1, b1):
    for j in range(JW):
        final = contract(place, mem[j].astype(BF16), 1, 1)
        for s in range(2):
            f1[pl.ds(s * JW + j, GROUPS, stride=16), :] = final[s * GROUPS : (s + 1) * GROUPS]

    def one(i, _):
        b1[i] = f1[pl.ds(pl.multiple_of(i * 16, 16), 16), :].astype(BF16)
        return 0

    lax.fori_loop(0, GROUPS, one, 0)


def finish_rows(a2, gate, gain, live, weight, conv, partial, fc, fg):
    lead, rest = halves(jnp.concatenate([a2[:, s, :] for s in range(2)], axis=0))
    wide = (DK, BLOCKS * DK)
    source = ((iota(wide, 1) >> 7) << 3) + (iota(wide, 1) & 7)
    spread = jnp.where(iota(wide, 0) == source, 1.0, 0.0).astype(BF16)
    every = contract(lead, spread, 1, 0) + contract(rest, spread, 1, 0)
    mask = own_lanes()

    def block(b):
        picked = every[:, b * DK : (b + 1) * DK] * mask
        rows = []
        for s in range(2):
            total = picked[s * GROUPS : s * GROUPS + ZS]
            for n in range(1, GROUPS // ZS):
                total = total + picked[s * GROUPS + n * ZS : s * GROUPS + (n + 1) * ZS]
            rows.append(total[:HEADS] + total[HEADS:])
        return jnp.concatenate(rows, axis=0)

    fg[...] = jnp.zeros_like(fg)
    second = iota((2 * HEADS, DK), 0) >> 2
    for t in range(STEPS):
        readout = block(CONV + t)
        scaling = lax.rsqrt(jnp.sum(readout * readout, axis=1, keepdims=True) / DK + EPS)
        gates = sigmoid(jnp.concatenate(by_head(gate[t].astype(F32)), axis=0))
        gated = readout * scaling * gain[...] * gates
        gated = jnp.where(live[0:1, t : t + 1] > second, gated, 0.0)
        for s in range(2):
            for h in range(HEADS):
                r = s * HEADS + h
                fg[2 * t + s : 2 * t + s + 1, h * DK : (h + 1) * DK] = gated[r : r + 1]
    total = jnp.dot(fg[...].astype(BF16), weight[...], preferred_element_type=F32)
    width = partial.shape[2]
    share = total.shape[1] // partial.shape[0]
    for d in range(partial.shape[0]):
        turned = total if d == 0 else pltpu.roll(total, total.shape[1] - d * share, 1)
        partial[d] = turned[:, :width].astype(BF16)
    for n in range(HIST):
        for part in range(3):
            kept = block(n * 3 + part)
            for s in range(2):
                for h in range(HEADS):
                    r = s * HEADS + h
                    fc[n, part, s : s + 1, h * DK : (h + 1) * DK] = kept[r : r + 1]
    conv[...] = fc[...].astype(BF16)


def remote(axis, peer, src, dst, sems, n):
    return pltpu.make_async_remote_copy(
        src_ref=src,
        dst_ref=dst,
        send_sem=sems.at[0, n],
        recv_sem=sems.at[1, n],
        device_id={axis: peer},
        device_id_type=pl.DeviceIdType.MESH,
    )


def peers_far_first(me, act):
    act(lax.rem(me + GROUPS // 2, GROUPS))

    def two(i, _):
        act(lax.rem(me + 31 - i, GROUPS))
        act(lax.rem(me + GROUPS - 31 + i, GROUPS))
        return 0

    lax.fori_loop(0, GROUPS // 2 - 1, two, 0)


def whole(
    columns,
    states_in,
    conv_in,
    proj_in,
    taps_in,
    decay_in,
    rate_in,
    beta_in,
    gate_in,
    gain_in,
    weight_in,
    targets_in,
    live_in,
    a1,
    shares,
    conv_to,
    states,
    conv,
    proj,
    taps,
    decay,
    rate,
    beta,
    gate,
    gain,
    weight,
    targets,
    live,
    conv_out,
    s1,
    s2,
    s3,
    r1,
    r2,
    r3,
    b1,
    b2,
    a2,
    partial,
    f,
    f1,
    f2,
    mem,
    places,
    xt,
    fc,
    fg,
    local,
    sems,
):
    me = lax.axis_index("rep")
    col = lax.axis_index("head")
    z, x, core = me // (XS * CS), (me // CS) % XS, me % CS
    mine = (core * XS + x) * ZS + z
    head, jg = z % HEADS, (z // HEADS) * 8 + core * XS + x

    barrier = pltpu.get_barrier_semaphore()

    def greet(axis, peer):
        pl.semaphore_signal(
            barrier, inc=1, device_id={axis: peer}, device_id_type=pl.DeviceIdType.MESH
        )

    peers_far_first(me, functools.partial(greet, "rep"))
    for k in range(1, columns):
        greet("head", lax.rem(col + k, columns))

    loads = [
        pltpu.make_async_copy(src, dst, local.at[n])
        for n, (src, dst) in enumerate(
            [
                (conv_in, conv),
                (proj_in, proj),
                (decay_in, decay),
                (rate_in, rate),
                (beta_in, beta),
                (live_in, live),
                (states_in, states),
                (targets_in, targets),
                (taps_in, taps),
                (gate_in, gate),
                (gain_in, gain),
                (weight_in, weight),
            ]
        )
    ]
    for load in loads:
        load.start()
    for load in loads[:4]:
        load.wait()
    pack_inputs(conv, proj, decay, rate, s2, f)
    pl.semaphore_wait(barrier, GROUPS - 1 + columns - 1)

    keep = pltpu.make_async_copy(s2.at[head], r2.at[core, x, z], local.at[12])
    keep.start()
    for k in (4, 3, 5, 2, 6, 1, 7):
        to = lax.rem(z + k, ZS)
        peer = (to * XS + x) * CS + core
        remote("rep", peer, s2.at[lax.rem(to, HEADS)], r2.at[core, x, z], sems, 0).start()

    for load in loads[4:7]:
        load.wait()
    pack_values(conv, proj, beta, live, s3)
    pack_states(states, s1)

    keep.wait()
    done = remote("rep", me, r2.at[0, 0, pl.ds(0, ZS - 1)], r2.at[0, 0, pl.ds(0, ZS - 1)], sems, 0)
    done.wait_send()
    done.wait_recv()
    right = (z * XS + lax.rem(x + 1, XS)) * CS + core
    left = (z * XS + lax.rem(x + XS - 1, XS)) * CS + core
    other = me + 1 - 2 * core
    half = ZS // 2
    behind, ahead = lax.rem(x + XS - 1, XS), lax.rem(x + 1, XS)

    def part(origin, n):
        return r2.at[core, origin, pl.ds(n * half, half)]

    def pass_on(peer, origin, n, sem):
        copy = remote("rep", peer, part(origin, n), part(origin, n), sems, sem)
        copy.start()
        return copy

    ring = [
        pass_on(right, x, 0, 1),
        pass_on(left, x, 1, 2),
        pass_on(right, x, 1, 3),
        pass_on(left, x, 0, 4),
    ]
    remote("rep", other, r2.at[core, x], r2.at[core, x], sems, 10).start()

    keep = [
        pltpu.make_async_copy(s1.at[mine], r1.at[mine], local.at[13]),
        pltpu.make_async_copy(s3.at[mine], r3.at[mine], local.at[14]),
    ]
    for copy in keep:
        copy.start()

    def to_all(pairs):
        def one(p):
            at = ((p % CS) * XS + (p // CS) % XS) * ZS + p // (XS * CS)
            for src, dst, n in pairs:
                remote("rep", p, src.at[at], dst.at[mine], sems, n).start()

        peers_far_first(me, one)

    def from_all(dst, n):
        most = dst.at[pl.ds(0, GROUPS - 1)]
        done = remote("rep", me, most, most, sems, n)
        done.wait_send()
        done.wait_recv()

    to_all([(s3, r3, 5), (s1, r1, 6)])

    widen_inputs(r2, f2, core, x, 0, ZS)

    def arrived(copy, origin, n):
        copy.wait_recv()
        pass_on(other, origin, n, 10)
        widen_inputs(r2, f2, core, origin, n * half, (n + 1) * half)

    ring[0].wait_recv()
    ring.append(pass_on(right, behind, 0, 11))
    pass_on(other, behind, 0, 10)
    ring[1].wait_recv()
    ring.append(pass_on(left, ahead, 1, 12))
    pass_on(other, ahead, 1, 10)
    for load in loads[7:9]:
        load.wait()
    find_places(targets, places)
    widen_inputs(r2, f2, core, behind, 0, half)
    widen_inputs(r2, f2, core, ahead, half, ZS)
    arrived(ring[2], behind, 1)
    arrived(ring[3], ahead, 0)
    opposite = lax.rem(x + 2, XS)
    arrived(ring[4], opposite, 0)
    arrived(ring[5], opposite, 1)
    for copy in keep:
        copy.wait()
    from_all(r1, 6)
    enter_states(r1, f1, mem)
    for copy in ring:
        copy.wait_send()
    done = remote("rep", me, r2.at[0], r2.at[0], sems, 10)
    done.wait_send()
    done.wait_recv()
    for n in range(XS):
        widen_inputs(r2, f2, 1 - core, n, 0, ZS)
    from_all(r3, 5)

    cols = pl.ds(pl.multiple_of(head * DK, DK), DK)
    returned = run_steps(jg, f2, r3, taps.at[:, :, cols], places, mem, xt)
    for s in range(2):
        b2[:, s, :] = returned[s * GROUPS : (s + 1) * GROUPS]
    keep = pltpu.make_async_copy(b2.at[mine], a2.at[mine], local.at[12])
    keep.start()
    to_all([(b2, a2, 7)])
    leave_states(places[STEPS - 1], mem, f1, b1)
    keep_states = pltpu.make_async_copy(b1.at[mine], a1.at[mine], local.at[13])
    keep_states.start()
    to_all([(b1, a1, 8)])

    for load in loads[9:]:
        load.wait()
    keep.wait()
    from_all(a2, 7)
    finish_rows(a2, gate, gain, live, weight, conv_out, partial, fc, fg)
    keep = pltpu.make_async_copy(partial.at[col], shares.at[col], local.at[12])
    keep.start()
    for k in (4, 3, 5, 2, 6, 1, 7):
        to = lax.rem(col + k, columns)
        remote("head", to, partial.at[to], shares.at[col], sems, 9).start()
    store = pltpu.make_async_copy(conv_out, conv_to, local.at[14])
    store.start()
    keep_states.wait()
    from_all(a1, 8)
    keep.wait()
    most = shares.at[pl.ds(0, columns - 1)]
    done = remote("head", col, most, most, sems, 9)
    done.wait_send()
    done.wait_recv()
    store.wait()


def settle(a1_in, shares_in, conv_in, out_to, states_to, conv_to, a1, shares, conv, out, states, sems):
    loads = [
        pltpu.make_async_copy(src, dst, sems.at[n])
        for n, (src, dst) in enumerate([(a1_in, a1), (shares_in, shares), (conv_in, conv)])
    ]
    for load in loads:
        load.start()
    loads[2].wait()
    stores = [pltpu.make_async_copy(conv, conv_to, sems.at[3])]
    stores[0].start()
    loads[0].wait()
    for h in range(HEADS):
        pieces = [a1[holder(h, jg)].astype(F32) for jg in range(JG)]
        for s in range(2):
            states[s, h] = jnp.concatenate([p[s * JW : (s + 1) * JW] for p in pieces], axis=0).T
            store = pltpu.make_async_copy(
                states.at[s, h], states_to.at[s, h], sems.at[4 + 2 * h + s]
            )
            store.start()
            stores.append(store)
    loads[1].wait()
    total = shares[0].astype(F32)
    for n in range(1, shares.shape[0]):
        total = total + shares[n].astype(F32)
    for t in range(STEPS):
        out[t] = total[2 * t : 2 * t + 2, : out.shape[2]].astype(BF16)
    stores.append(pltpu.make_async_copy(out, out_to, sems.at[4 + 2 * HEADS]))
    stores[-1].start()
    for store in stores:
        store.wait()


def shape(dims, kind):
    return jax.ShapeDtypeStruct(dims, kind)


def local(columns, *args):
    (
        states,
        conv_states,
        projected,
        conv_weight,
        decay_input,
        decay_rate,
        beta_logit,
        out_gate,
        norm_gain,
        out_weight,
        destinations,
        live_counts,
    ) = args
    operands = (
        states,
        conv_states.transpose(1, 2, 0, 3),
        projected.transpose(0, 2, 1, 3),
        conv_weight.transpose(1, 0, 2),
        decay_input,
        decay_rate.reshape(1, HEADS),
        beta_logit.transpose(1, 2, 0),
        out_gate,
        norm_gain.reshape(1, DK),
        out_weight,
        destinations,
        live_counts.transpose(1, 0),
    )
    share = out_weight.shape[1] // columns
    width = -(-share // DK) * DK
    block = pltpu.VMEM((GROUPS, 16, DK), BF16)
    small = pltpu.VMEM((GROUPS, 2, DK), F32)
    any_ = pl.BlockSpec(memory_space=pltpu.HBM)
    most = pltpu.CompilerParams(
        collective_id=0, has_side_effects=True, vmem_limit_bytes=60 * 1024 * 1024
    )
    landed = (
        shape((GROUPS, 16, DK), BF16),
        shape((columns, 16, width), BF16),
        shape(operands[1].shape, BF16),
    )
    pieces = pl.pallas_call(
        functools.partial(whole, columns),
        out_shape=landed,
        in_specs=[any_] * len(operands),
        out_specs=(any_,) * 3,
        scratch_shapes=[pltpu.VMEM(a.shape, a.dtype) for a in operands]
        + [
            pltpu.VMEM(operands[1].shape, BF16),
            block,
            pltpu.VMEM((HEADS, ROWS, DK), BF16),
            small,
            block,
            pltpu.VMEM((CS, XS, ZS, ROWS, DK), BF16),
            small,
            block,
            small,
            small,
            pltpu.VMEM((columns, 16, width), BF16),
            pltpu.VMEM((HEADS, ROWS, DK), F32),
            pltpu.VMEM((GROUPS * 16, DK), F32),
            pltpu.VMEM((GROUPS * ROWS, DK), F32),
            pltpu.VMEM((JW, DK, SLOTS), F32),
            pltpu.VMEM((STEPS, SLOTS, SLOTS), BF16),
            pltpu.VMEM((DK, SLOTS), F32),
            pltpu.VMEM(operands[1].shape, F32),
            pltpu.VMEM((16, HEADS * DK), F32),
            pltpu.SemaphoreType.DMA((15,)),
            pltpu.SemaphoreType.DMA((2, 13)),
        ],
        compiler_params=most,
        name="kda_steps",
    )(*operands)
    results = (
        shape((STEPS, 2, share), BF16),
        shape(states.shape, F32),
        shape(operands[1].shape, BF16),
    )
    out, states_out, conv_out = pl.pallas_call(
        settle,
        out_shape=results,
        in_specs=[any_] * 3,
        out_specs=(any_,) * 3,
        scratch_shapes=[pltpu.VMEM(a.shape, a.dtype) for a in landed]
        + [pltpu.VMEM(a.shape, a.dtype) for a in results[:2]]
        + [pltpu.SemaphoreType.DMA((5 + 2 * HEADS,))],
        compiler_params=pltpu.CompilerParams(vmem_limit_bytes=60 * 1024 * 1024),
        name="settle",
    )(*pieces)
    return out, states_out, conv_out.transpose(2, 0, 1, 3)


def solution(mesh):
    placed = (
        P("rep", "head", None, None),
        P("rep", None, None, "head"),
        P(None, "rep", None, "head"),
        P(None, None, "head"),
        P(None, "rep", "head"),
        P("head"),
        P(None, "rep", "head"),
        P(None, "rep", "head"),
        P(),
        P("head", None),
        P(),
        P(None, "rep"),
    )
    return jax.shard_map(
        functools.partial(local, mesh.shape["head"]),
        mesh=mesh,
        in_specs=placed,
        out_specs=(
            P(None, "rep", "head"),
            P("rep", "head", None, None),
            P("rep", None, None, "head"),
        ),
        check_vma=False,
    )
```

```python
import functools

import jax
import jax.numpy as jnp
from jax import lax
from jax.experimental import pallas as pl
from jax.experimental.pallas import tpu as pltpu
from jax.sharding import PartitionSpec as P

F32, BF16 = jnp.float32, jnp.bfloat16
STEPS, TAPS = 6, 4
HIST = TAPS - 1
ZS, XS, CS = 8, 4, 2
GROUPS, HEADS, DK = 64, 4, 128
SLOTS = 2 * GROUPS
JG, JW = 16, 8
WIN = HIST + STEPS
ROW_DECAY = WIN * 4
ROWS = ROW_DECAY + 2 * STEPS
LANE_ALIVE = WIN * JW
LANE_BETA = LANE_ALIVE + 8
CONV = 3 * HIST
BLOCKS = CONV + STEPS
EPS = 1e-6


def holder(h, jg):
    return (jg % 8) * ZS + (jg // 8) * HEADS + h


def iota(shape, dim):
    return lax.broadcasted_iota(jnp.int32, shape, dim)


def contract(a, b, da, db):
    return lax.dot_general(a, b, (((da,), (db,)), ((), ())), preferred_element_type=F32)


def halves(x):
    lead = x.astype(BF16)
    return lead, (x - lead.astype(F32)).astype(BF16)


def sigmoid(x):
    return 1.0 / (1.0 + jnp.exp(-x))


def softplus(x):
    return jnp.maximum(x, 0.0) + jnp.log1p(jnp.exp(-jnp.abs(x)))


def inner(slot):
    group = slot >> 1
    return ((slot & 1) << 6) + ((group & 1) << 5) + (((group >> 1) & 3) << 3) + (group >> 3)


def own_lanes():
    group = iota((SLOTS, DK), 0) & 63
    piece = (group >> 3) + ((group & 4) << 1)
    return jnp.where(piece == iota((SLOTS, DK), 1) >> 3, 1.0, 0.0)


def by_head(x):
    return [
        jnp.concatenate([x[s : s + 1, h * DK : (h + 1) * DK] for h in range(HEADS)], axis=0)
        for s in range(2)
    ]


def pack_inputs(conv, proj, decay, rate, s2, f):
    for w in range(WIN):
        for part in range(2):
            block = (conv[w, part] if w < HIST else proj[w - HIST, part]).astype(F32)
            at = (w * 2 + part) * 2
            for h in range(HEADS):
                f[h, at : at + 2, :] = block[:, h * DK : (h + 1) * DK]
    for t in range(STEPS):
        exponent = softplus(decay[t])
        for h in range(HEADS):
            at = ROW_DECAY + 2 * t
            f[h, at : at + 2, :] = exponent[:, h * DK : (h + 1) * DK] * rate[0:1, h : h + 1]
    for h in range(HEADS):
        s2[h] = f[h].astype(BF16)


def pack_values(conv, proj, beta, live, s3):
    mask = own_lanes()
    parts = []
    for w in range(WIN):
        block = (conv[w, 2] if w < HIST else proj[w - HIST, 2]).astype(F32)
        rows = []
        for four in by_head(block):
            rows += [four] * (2 * ZS)
        parts.append((jnp.concatenate(rows, axis=0) * mask).astype(BF16))
    shape = (WIN * DK, DK)
    place = jnp.where(((iota(shape, 0) >> 7) << 3) + (iota(shape, 0) & 7) == iota(shape, 1), 1.0, 0.0)
    packed = contract(jnp.concatenate(parts, axis=1), place.astype(BF16), 1, 0)
    for s in range(2):
        alive = jnp.where(live[...] > s, 1.0, 0.0)
        row = jnp.concatenate(
            [
                jnp.zeros((HEADS, LANE_ALIVE), F32),
                jnp.broadcast_to(alive, (HEADS, STEPS)),
                jnp.zeros((HEADS, 8 - STEPS), F32),
                beta[s],
                jnp.zeros((HEADS, DK - LANE_BETA - STEPS), F32),
            ],
            axis=1,
        )
        rest = jnp.concatenate([row] * (2 * ZS), axis=0)
        s3[:, s, :] = packed[s * GROUPS : (s + 1) * GROUPS] + rest


def pack_states(states, s1):
    for h in range(HEADS):
        first, second = states[0, h].T, states[1, h].T
        for jg in range(JG):
            rows = slice(jg * JW, (jg + 1) * JW)
            s1[holder(h, jg)] = jnp.concatenate([first[rows], second[rows]], axis=0).astype(BF16)


def widen_inputs(r2, f2, core, x, first, last):
    def one(i, _):
        at = pl.multiple_of(((core * XS + x) * ZS + i) * ROWS, ROWS)
        f2[pl.ds(at, ROWS), :] = r2[core, x, i].astype(F32)
        return 0

    lax.fori_loop(first, last, one, 0)


def enter_states(r1, f1, mem):
    def one(i, _):
        f1[pl.ds(pl.multiple_of(i * 16, 16), 16), :] = r1[i].astype(F32)
        return 0

    lax.fori_loop(0, GROUPS, one, 0)
    for j in range(JW):
        rows = [f1[pl.ds(s * JW + j, GROUPS, stride=16), :] for s in range(2)]
        mem[j] = jnp.concatenate(rows, axis=0).T


def find_places(targets, places):
    square = (SLOTS, SLOTS)
    back = jnp.where(inner(iota(square, 0)) == iota(square, 1), 1.0, 0.0).astype(BF16)
    held = back
    for t in range(STEPS):
        move = jnp.where(iota(square, 0) == inner(targets[t : t + 1, :]), 1.0, 0.0).astype(BF16)
        place = contract(move, held, 1, 0).astype(BF16)
        places[t] = place
        if t < STEPS - 1:
            held = contract(back, place, 1, 0).astype(BF16)


def prepare_steps(jg, f2, r3, weight, places, ready, rows8, xt):
    def both(row):
        return jnp.concatenate(
            [f2[pl.ds(row + s, GROUPS, stride=ROWS), :] for s in range(2)], axis=0
        )

    square = (SLOTS, SLOTS)
    eye = jnp.where(iota(square, 0) == iota(square, 1), 1.0, 0.0).astype(BF16)
    taps = [weight[part].T for part in range(3)]
    xt[0:DK, 0:TAPS] = taps[2]
    mine = pl.ds(pl.multiple_of(jg * JW, JW), JW)
    value_taps = xt[mine, 0:TAPS]
    values = jnp.concatenate([r3[:, s, :] for s in range(2)], axis=0)
    lead3, rest3 = halves(values)

    def pair(w, extra, at):
        x = jnp.concatenate([both(w * 4), both(w * 4 + 2)] + extra, axis=1)
        return contract(x.astype(BF16), at, 0, 0)

    start = contract(lead3, eye, 0, 0)
    hist = []
    for w in range(HIST):
        two = pair(w, [], eye)
        hist.append([two[:DK], two[DK:], start[w * JW : (w + 1) * JW]])
    for t in range(STEPS):
        place = places[t]
        three = pair(t + HIST, [both(ROW_DECAY + 2 * t)], place)
        small = contract(lead3, place, 0, 0) + contract(rest3, place, 0, 0)
        new = [three[:DK], three[DK : 2 * DK], small[(t + HIST) * JW : (t + HIST + 1) * JW]]
        alive = small[LANE_ALIVE + t : LANE_ALIVE + t + 1] > 0.5
        logit = small[LANE_BETA + t : LANE_BETA + t + 1]
        strength = jnp.where(alive, sigmoid(logit), 0.0)
        retain = jnp.where(alive, jnp.exp(-three[2 * DK :]), 1.0)
        window = hist + [new]
        acts = []
        for part in range(3):
            cols = value_taps if part == 2 else taps[part]
            total = window[0][part] * cols[:, 0:1]
            for n in range(1, TAPS):
                total = total + window[n][part] * cols[:, n : n + 1]
            acts.append(total / (1.0 + jnp.exp(-total)))
        hist = [
            [jnp.where(alive, window[n + 1][part], window[n][part]) for part in range(3)]
            for n in range(HIST)
        ]
        query, key, value = acts
        ready[t, 0] = query / jnp.sqrt(jnp.sum(query * query, axis=0, keepdims=True) + EPS)
        ready[t, 1] = key / jnp.sqrt(jnp.sum(key * key, axis=0, keepdims=True) + EPS)
        ready[t, 2] = retain
        rows8[t] = jnp.concatenate([value, jnp.broadcast_to(strength, (JW, SLOTS))], axis=0)
    kept = []
    for n in range(HIST):
        for part in range(3):
            block = hist[n][part]
            if part < 2:
                xt[...] = block
                block = xt[mine, :]
            kept.append(block)
    kept = jnp.concatenate(kept, axis=0).astype(BF16)
    return contract(places[STEPS - 1], kept, 1, 1)


def run_steps(ready, rows8, places, mem):
    readouts = []
    for t in range(STEPS):
        query, key, retain = ready[t, 0], ready[t, 1], ready[t, 2]
        strength = rows8[t, JW : JW + 1, :]
        rows = []
        for j in range(JW):
            decayed = retain * mem[j]
            recalled = jnp.sum(key * decayed, axis=0, keepdims=True)
            updated = decayed + key * (strength * (rows8[t, j : j + 1, :] - recalled))
            mem[j] = updated
            rows.append(jnp.sum(query * updated, axis=0, keepdims=True) * DK**-0.5)
        lead, rest = halves(jnp.concatenate(rows, axis=0))
        place = places[t]
        readouts.append(contract(place, lead, 1, 1) + contract(place, rest, 1, 1))
    return readouts


def leave_states(place, mem, f1, b1):
    for j in range(JW):
        final = contract(place, mem[j].astype(BF16), 1, 1)
        for s in range(2):
            f1[pl.ds(s * JW + j, GROUPS, stride=16), :] = final[s * GROUPS : (s + 1) * GROUPS]

    def one(i, _):
        b1[i] = f1[pl.ds(pl.multiple_of(i * 16, 16), 16), :].astype(BF16)
        return 0

    lax.fori_loop(0, GROUPS, one, 0)


def finish_rows(a2, gate, gain, live, weight, conv, partial, fc, fg):
    lead, rest = halves(jnp.concatenate([a2[:, s, :] for s in range(2)], axis=0))
    wide = (DK, BLOCKS * DK)
    source = ((iota(wide, 1) >> 7) << 3) + (iota(wide, 1) & 7)
    spread = jnp.where(iota(wide, 0) == source, 1.0, 0.0).astype(BF16)
    every = contract(lead, spread, 1, 0) + contract(rest, spread, 1, 0)
    mask = own_lanes()

    def block(b):
        picked = every[:, b * DK : (b + 1) * DK] * mask
        rows = []
        for s in range(2):
            total = picked[s * GROUPS : s * GROUPS + ZS]
            for n in range(1, GROUPS // ZS):
                total = total + picked[s * GROUPS + n * ZS : s * GROUPS + (n + 1) * ZS]
            rows.append(total[:HEADS] + total[HEADS:])
        return jnp.concatenate(rows, axis=0)

    fg[...] = jnp.zeros_like(fg)
    second = iota((2 * HEADS, DK), 0) >> 2
    for t in range(STEPS):
        readout = block(CONV + t)
        scaling = lax.rsqrt(jnp.sum(readout * readout, axis=1, keepdims=True) / DK + EPS)
        gates = sigmoid(jnp.concatenate(by_head(gate[t].astype(F32)), axis=0))
        gated = readout * scaling * gain[...] * gates
        gated = jnp.where(live[0:1, t : t + 1] > second, gated, 0.0)
        for s in range(2):
            for h in range(HEADS):
                r = s * HEADS + h
                fg[2 * t + s : 2 * t + s + 1, h * DK : (h + 1) * DK] = gated[r : r + 1]
    total = jnp.dot(fg[...].astype(BF16), weight[...], preferred_element_type=F32)
    width = partial.shape[2]
    share = total.shape[1] // partial.shape[0]
    for d in range(partial.shape[0]):
        turned = total if d == 0 else pltpu.roll(total, total.shape[1] - d * share, 1)
        partial[d] = turned[:, :width].astype(BF16)
    for n in range(HIST):
        for part in range(3):
            kept = block(n * 3 + part)
            for s in range(2):
                for h in range(HEADS):
                    r = s * HEADS + h
                    fc[n, part, s : s + 1, h * DK : (h + 1) * DK] = kept[r : r + 1]
    conv[...] = fc[...].astype(BF16)


def remote(axis, peer, src, dst, sems, n):
    return pltpu.make_async_remote_copy(
        src_ref=src,
        dst_ref=dst,
        send_sem=sems.at[0, n],
        recv_sem=sems.at[1, n],
        device_id={axis: peer},
        device_id_type=pl.DeviceIdType.MESH,
    )


def peers_far_first(me, act):
    act(lax.rem(me + GROUPS // 2, GROUPS))

    def two(i, _):
        act(lax.rem(me + 31 - i, GROUPS))
        act(lax.rem(me + GROUPS - 31 + i, GROUPS))
        return 0

    lax.fori_loop(0, GROUPS // 2 - 1, two, 0)


def whole(
    columns,
    states_in,
    conv_in,
    proj_in,
    taps_in,
    decay_in,
    rate_in,
    beta_in,
    gate_in,
    gain_in,
    weight_in,
    targets_in,
    live_in,
    a1,
    shares,
    conv_to,
    states,
    conv,
    proj,
    taps,
    decay,
    rate,
    beta,
    gate,
    gain,
    weight,
    targets,
    live,
    conv_out,
    s1,
    s2,
    s3,
    r1,
    r2,
    r3,
    b1,
    b2,
    a2,
    partial,
    f,
    f1,
    f2,
    mem,
    places,
    ready,
    rows8,
    xt,
    fc,
    fg,
    local,
    sems,
):
    me = lax.axis_index("rep")
    col = lax.axis_index("head")
    z, x, core = me // (XS * CS), (me // CS) % XS, me % CS
    mine = (core * XS + x) * ZS + z
    head, jg = z % HEADS, (z // HEADS) * 8 + core * XS + x

    barrier = pltpu.get_barrier_semaphore()

    def greet(axis, peer):
        pl.semaphore_signal(
            barrier, inc=1, device_id={axis: peer}, device_id_type=pl.DeviceIdType.MESH
        )

    for k in (4, 3, 5, 2, 6, 1, 7):
        greet("rep", (lax.rem(z + k, ZS) * XS + x) * CS + core)
    for k in (4, 3, 5, 2, 6, 1, 7):
        greet("head", lax.rem(col + k, columns))
    for k in range(1, XS * CS):
        greet("rep", z * XS * CS + lax.rem(x * CS + core + k, XS * CS))

    loads = [
        pltpu.make_async_copy(src, dst, local.at[n])
        for n, (src, dst) in enumerate(
            [
                (conv_in, conv),
                (proj_in, proj),
                (decay_in, decay),
                (rate_in, rate),
                (beta_in, beta),
                (live_in, live),
                (states_in, states),
                (targets_in, targets),
                (taps_in, taps),
                (gate_in, gate),
                (gain_in, gain),
                (weight_in, weight),
            ]
        )
    ]
    for load in loads:
        load.start()
    for load in loads[:4]:
        load.wait()
    pack_inputs(conv, proj, decay, rate, s2, f)
    pl.semaphore_wait(barrier, ZS - 1 + XS * CS - 1 + columns - 1)

    keep = pltpu.make_async_copy(s2.at[head], r2.at[core, x, z], local.at[12])
    keep.start()
    for k in (4, 3, 5, 2, 6, 1, 7):
        to = lax.rem(z + k, ZS)
        peer = (to * XS + x) * CS + core
        remote("rep", peer, s2.at[lax.rem(to, HEADS)], r2.at[core, x, z], sems, 0).start()

    for load in loads[4:7]:
        load.wait()
    pack_values(conv, proj, beta, live, s3)
    pack_states(states, s1)

    keep.wait()
    done = remote("rep", me, r2.at[0, 0, pl.ds(0, ZS - 1)], r2.at[0, 0, pl.ds(0, ZS - 1)], sems, 0)
    done.wait_send()
    done.wait_recv()
    right = (z * XS + lax.rem(x + 1, XS)) * CS + core
    left = (z * XS + lax.rem(x + XS - 1, XS)) * CS + core
    other = me + 1 - 2 * core
    half = ZS // 2
    behind, ahead = lax.rem(x + XS - 1, XS), lax.rem(x + 1, XS)

    def part(origin, n):
        return r2.at[core, origin, pl.ds(n * half, half)]

    def pass_on(peer, origin, n, sem):
        copy = remote("rep", peer, part(origin, n), part(origin, n), sems, sem)
        copy.start()
        return copy

    ring = [
        pass_on(right, x, 0, 1),
        pass_on(left, x, 1, 2),
        pass_on(right, x, 1, 3),
        pass_on(left, x, 0, 4),
    ]
    remote("rep", other, r2.at[core, x], r2.at[core, x], sems, 10).start()

    keep = [
        pltpu.make_async_copy(s1.at[mine], r1.at[mine], local.at[13]),
        pltpu.make_async_copy(s3.at[mine], r3.at[mine], local.at[14]),
    ]
    for copy in keep:
        copy.start()

    def to_all(pairs):
        def one(p):
            at = ((p % CS) * XS + (p // CS) % XS) * ZS + p // (XS * CS)
            for src, dst, n in pairs:
                remote("rep", p, src.at[at], dst.at[mine], sems, n).start()

        peers_far_first(me, one)

    def from_all(dst, n):
        most = dst.at[pl.ds(0, GROUPS - 1)]
        done = remote("rep", me, most, most, sems, n)
        done.wait_send()
        done.wait_recv()

    to_all([(s3, r3, 5), (s1, r1, 6)])

    widen_inputs(r2, f2, core, x, 0, ZS)

    def arrived(copy, origin, n):
        copy.wait_recv()
        pass_on(other, origin, n, 10)
        widen_inputs(r2, f2, core, origin, n * half, (n + 1) * half)

    ring[0].wait_recv()
    ring.append(pass_on(right, behind, 0, 11))
    pass_on(other, behind, 0, 10)
    ring[1].wait_recv()
    ring.append(pass_on(left, ahead, 1, 12))
    pass_on(other, ahead, 1, 10)
    for load in loads[7:9]:
        load.wait()
    find_places(targets, places)
    widen_inputs(r2, f2, core, behind, 0, half)
    widen_inputs(r2, f2, core, ahead, half, ZS)
    arrived(ring[2], behind, 1)
    arrived(ring[3], ahead, 0)
    opposite = lax.rem(x + 2, XS)
    arrived(ring[4], opposite, 0)
    arrived(ring[5], opposite, 1)
    for copy in keep:
        copy.wait()
    for copy in ring:
        copy.wait_send()
    done = remote("rep", me, r2.at[0], r2.at[0], sems, 10)
    done.wait_send()
    done.wait_recv()
    for n in range(XS):
        widen_inputs(r2, f2, 1 - core, n, 0, ZS)
    from_all(r3, 5)
    cols = pl.ds(pl.multiple_of(head * DK, DK), DK)
    kept = prepare_steps(jg, f2, r3, taps.at[:, :, cols], places, ready, rows8, xt)
    from_all(r1, 6)
    enter_states(r1, f1, mem)
    readouts = run_steps(ready, rows8, places, mem)
    pad = jnp.zeros((SLOTS, DK - BLOCKS * JW), F32)
    returned = jnp.concatenate([kept] + readouts + [pad], axis=1)
    for s in range(2):
        b2[:, s, :] = returned[s * GROUPS : (s + 1) * GROUPS]
    keep = pltpu.make_async_copy(b2.at[mine], a2.at[mine], local.at[12])
    keep.start()
    to_all([(b2, a2, 7)])
    leave_states(places[STEPS - 1], mem, f1, b1)
    keep_states = pltpu.make_async_copy(b1.at[mine], a1.at[mine], local.at[13])
    keep_states.start()
    to_all([(b1, a1, 8)])

    for load in loads[9:]:
        load.wait()
    keep.wait()
    from_all(a2, 7)
    finish_rows(a2, gate, gain, live, weight, conv_out, partial, fc, fg)
    keep = pltpu.make_async_copy(partial.at[col], shares.at[col], local.at[12])
    keep.start()
    for k in (4, 3, 5, 2, 6, 1, 7):
        to = lax.rem(col + k, columns)
        remote("head", to, partial.at[to], shares.at[col], sems, 9).start()
    store = pltpu.make_async_copy(conv_out, conv_to, local.at[14])
    store.start()
    keep_states.wait()
    from_all(a1, 8)
    keep.wait()
    most = shares.at[pl.ds(0, columns - 1)]
    done = remote("head", col, most, most, sems, 9)
    done.wait_send()
    done.wait_recv()
    store.wait()


def settle(a1_in, shares_in, conv_in, out_to, states_to, conv_to, a1, shares, conv, out, states, sems):
    loads = [
        pltpu.make_async_copy(src, dst, sems.at[n])
        for n, (src, dst) in enumerate([(a1_in, a1), (shares_in, shares), (conv_in, conv)])
    ]
    for load in loads:
        load.start()
    loads[2].wait()
    stores = [pltpu.make_async_copy(conv, conv_to, sems.at[3])]
    stores[0].start()
    loads[0].wait()
    for h in range(HEADS):
        pieces = [a1[holder(h, jg)].astype(F32) for jg in range(JG)]
        for s in range(2):
            states[s, h] = jnp.concatenate([p[s * JW : (s + 1) * JW] for p in pieces], axis=0).T
            store = pltpu.make_async_copy(
                states.at[s, h], states_to.at[s, h], sems.at[4 + 2 * h + s]
            )
            store.start()
            stores.append(store)
    loads[1].wait()
    total = shares[0].astype(F32)
    for n in range(1, shares.shape[0]):
        total = total + shares[n].astype(F32)
    for t in range(STEPS):
        out[t] = total[2 * t : 2 * t + 2, : out.shape[2]].astype(BF16)
    stores.append(pltpu.make_async_copy(out, out_to, sems.at[4 + 2 * HEADS]))
    stores[-1].start()
    for store in stores:
        store.wait()


def shape(dims, kind):
    return jax.ShapeDtypeStruct(dims, kind)


def local(columns, *args):
    (
        states,
        conv_states,
        projected,
        conv_weight,
        decay_input,
        decay_rate,
        beta_logit,
        out_gate,
        norm_gain,
        out_weight,
        destinations,
        live_counts,
    ) = args
    operands = (
        states,
        conv_states.transpose(1, 2, 0, 3),
        projected.transpose(0, 2, 1, 3),
        conv_weight.transpose(1, 0, 2),
        decay_input,
        decay_rate.reshape(1, HEADS),
        beta_logit.transpose(1, 2, 0),
        out_gate,
        norm_gain.reshape(1, DK),
        out_weight,
        destinations,
        live_counts.transpose(1, 0),
    )
    share = out_weight.shape[1] // columns
    width = -(-share // DK) * DK
    block = pltpu.VMEM((GROUPS, 16, DK), BF16)
    small = pltpu.VMEM((GROUPS, 2, DK), F32)
    any_ = pl.BlockSpec(memory_space=pltpu.HBM)
    most = pltpu.CompilerParams(
        collective_id=0, has_side_effects=True, vmem_limit_bytes=60 * 1024 * 1024
    )
    landed = (
        shape((GROUPS, 16, DK), BF16),
        shape((columns, 16, width), BF16),
        shape(operands[1].shape, BF16),
    )
    pieces = pl.pallas_call(
        functools.partial(whole, columns),
        out_shape=landed,
        in_specs=[any_] * len(operands),
        out_specs=(any_,) * 3,
        scratch_shapes=[pltpu.VMEM(a.shape, a.dtype) for a in operands]
        + [
            pltpu.VMEM(operands[1].shape, BF16),
            block,
            pltpu.VMEM((HEADS, ROWS, DK), BF16),
            small,
            block,
            pltpu.VMEM((CS, XS, ZS, ROWS, DK), BF16),
            small,
            block,
            small,
            small,
            pltpu.VMEM((columns, 16, width), BF16),
            pltpu.VMEM((HEADS, ROWS, DK), F32),
            pltpu.VMEM((GROUPS * 16, DK), F32),
            pltpu.VMEM((GROUPS * ROWS, DK), F32),
            pltpu.VMEM((JW, DK, SLOTS), F32),
            pltpu.VMEM((STEPS, SLOTS, SLOTS), BF16),
            pltpu.VMEM((STEPS, 3, DK, SLOTS), F32),
            pltpu.VMEM((STEPS, 2 * JW, SLOTS), F32),
            pltpu.VMEM((DK, SLOTS), F32),
            pltpu.VMEM(operands[1].shape, F32),
            pltpu.VMEM((16, HEADS * DK), F32),
            pltpu.SemaphoreType.DMA((15,)),
            pltpu.SemaphoreType.DMA((2, 13)),
        ],
        compiler_params=most,
        name="kda_steps",
    )(*operands)
    results = (
        shape((STEPS, 2, share), BF16),
        shape(states.shape, F32),
        shape(operands[1].shape, BF16),
    )
    out, states_out, conv_out = pl.pallas_call(
        settle,
        out_shape=results,
        in_specs=[any_] * 3,
        out_specs=(any_,) * 3,
        scratch_shapes=[pltpu.VMEM(a.shape, a.dtype) for a in landed]
        + [pltpu.VMEM(a.shape, a.dtype) for a in results[:2]]
        + [pltpu.SemaphoreType.DMA((5 + 2 * HEADS,))],
        compiler_params=pltpu.CompilerParams(vmem_limit_bytes=60 * 1024 * 1024),
        name="settle",
    )(*pieces)
    return out, states_out, conv_out.transpose(2, 0, 1, 3)


def solution(mesh):
    placed = (
        P("rep", "head", None, None),
        P("rep", None, None, "head"),
        P(None, "rep", None, "head"),
        P(None, None, "head"),
        P(None, "rep", "head"),
        P("head"),
        P(None, "rep", "head"),
        P(None, "rep", "head"),
        P(),
        P("head", None),
        P(),
        P(None, "rep"),
    )
    return jax.shard_map(
        functools.partial(local, mesh.shape["head"]),
        mesh=mesh,
        in_specs=placed,
        out_specs=(
            P(None, "rep", "head"),
            P("rep", "head", None, None),
            P("rep", None, None, "head"),
        ),
        check_vma=False,
    )
```

```python
import functools

import jax
import jax.numpy as jnp
from jax import lax
from jax.experimental import pallas as pl
from jax.experimental.pallas import tpu as pltpu
from jax.sharding import PartitionSpec as P

F32, BF16 = jnp.float32, jnp.bfloat16
STEPS, TAPS = 6, 4
HIST = TAPS - 1
ZS, XS, CS = 8, 4, 2
GROUPS, HEADS, DK = 64, 4, 128
SLOTS = 2 * GROUPS
JG, JW = 16, 8
WIN = HIST + STEPS
ROW_DECAY = WIN * 4
ROWS = ROW_DECAY + 2 * STEPS
LANE_ALIVE = WIN * JW
LANE_BETA = LANE_ALIVE + 8
CONV = 3 * HIST
BLOCKS = CONV + STEPS
EPS = 1e-6


def holder(h, jg):
    return (jg % 8) * ZS + (jg // 8) * HEADS + h


def iota(shape, dim):
    return lax.broadcasted_iota(jnp.int32, shape, dim)


def contract(a, b, da, db):
    return lax.dot_general(a, b, (((da,), (db,)), ((), ())), preferred_element_type=F32)


def halves(x):
    lead = x.astype(BF16)
    return lead, (x - lead.astype(F32)).astype(BF16)


def sigmoid(x):
    return 1.0 / (1.0 + jnp.exp(-x))


def softplus(x):
    return jnp.maximum(x, 0.0) + jnp.log1p(jnp.exp(-jnp.abs(x)))


def inner(slot):
    group = slot >> 1
    return ((slot & 1) << 6) + ((group & 1) << 5) + (((group >> 1) & 3) << 3) + (group >> 3)


def own_lanes():
    group = iota((SLOTS, DK), 0) & 63
    piece = (group >> 3) + ((group & 4) << 1)
    return jnp.where(piece == iota((SLOTS, DK), 1) >> 3, 1.0, 0.0)


def by_head(x):
    return [
        jnp.concatenate([x[s : s + 1, h * DK : (h + 1) * DK] for h in range(HEADS)], axis=0)
        for s in range(2)
    ]


def pack_inputs(conv, proj, decay, rate, s2, f):
    for w in range(WIN):
        for part in range(2):
            block = (conv[w, part] if w < HIST else proj[w - HIST, part]).astype(F32)
            at = (w * 2 + part) * 2
            for h in range(HEADS):
                f[h, at : at + 2, :] = block[:, h * DK : (h + 1) * DK]
    for t in range(STEPS):
        exponent = softplus(decay[t])
        for h in range(HEADS):
            at = ROW_DECAY + 2 * t
            f[h, at : at + 2, :] = exponent[:, h * DK : (h + 1) * DK] * rate[0:1, h : h + 1]
    for h in range(HEADS):
        s2[h] = f[h].astype(BF16)


def pack_values(conv, proj, beta, live, s3):
    mask = own_lanes()
    parts = []
    for w in range(WIN):
        block = (conv[w, 2] if w < HIST else proj[w - HIST, 2]).astype(F32)
        rows = []
        for four in by_head(block):
            rows += [four] * (2 * ZS)
        parts.append((jnp.concatenate(rows, axis=0) * mask).astype(BF16))
    shape = (WIN * DK, DK)
    place = jnp.where(((iota(shape, 0) >> 7) << 3) + (iota(shape, 0) & 7) == iota(shape, 1), 1.0, 0.0)
    packed = contract(jnp.concatenate(parts, axis=1), place.astype(BF16), 1, 0)
    for s in range(2):
        alive = jnp.where(live[...] > s, 1.0, 0.0)
        row = jnp.concatenate(
            [
                jnp.zeros((HEADS, LANE_ALIVE), F32),
                jnp.broadcast_to(alive, (HEADS, STEPS)),
                jnp.zeros((HEADS, 8 - STEPS), F32),
                beta[s],
                jnp.zeros((HEADS, DK - LANE_BETA - STEPS), F32),
            ],
            axis=1,
        )
        rest = jnp.concatenate([row] * (2 * ZS), axis=0)
        s3[:, s, :] = packed[s * GROUPS : (s + 1) * GROUPS] + rest


def pack_states(states, s1):
    for h in range(HEADS):
        first, second = states[0, h].T, states[1, h].T
        for jg in range(JG):
            rows = slice(jg * JW, (jg + 1) * JW)
            s1[holder(h, jg)] = jnp.concatenate([first[rows], second[rows]], axis=0).astype(BF16)


def widen_inputs(r2, f2, core, x, first, last):
    def one(i, _):
        at = pl.multiple_of(((core * XS + x) * ZS + i) * ROWS, ROWS)
        f2[pl.ds(at, ROWS), :] = r2[core, x, i].astype(F32)
        return 0

    lax.fori_loop(first, last, one, 0)


def enter_states(r1, f1, mem):
    def one(i, _):
        f1[pl.ds(pl.multiple_of(i * 16, 16), 16), :] = r1[i].astype(F32)
        return 0

    lax.fori_loop(0, GROUPS, one, 0)
    for j in range(JW):
        rows = [f1[pl.ds(s * JW + j, GROUPS, stride=16), :] for s in range(2)]
        mem[j] = jnp.concatenate(rows, axis=0).T


def find_places(targets, places):
    square = (SLOTS, SLOTS)
    back = jnp.where(inner(iota(square, 0)) == iota(square, 1), 1.0, 0.0).astype(BF16)
    held = back
    for t in range(STEPS):
        move = jnp.where(iota(square, 0) == inner(targets[t : t + 1, :]), 1.0, 0.0).astype(BF16)
        place = contract(move, held, 1, 0).astype(BF16)
        places[t] = place
        if t < STEPS - 1:
            held = contract(back, place, 1, 0).astype(BF16)


def prepare_steps(jg, f2, r3, weight, places, ready, rows8, xt):
    def both(row):
        return jnp.concatenate(
            [f2[pl.ds(row + s, GROUPS, stride=ROWS), :] for s in range(2)], axis=0
        )

    square = (SLOTS, SLOTS)
    eye = jnp.where(iota(square, 0) == iota(square, 1), 1.0, 0.0).astype(BF16)
    taps = [weight[part].T for part in range(3)]
    xt[0:DK, 0:TAPS] = taps[2]
    mine = pl.ds(pl.multiple_of(jg * JW, JW), JW)
    value_taps = xt[mine, 0:TAPS]
    values = jnp.concatenate([r3[:, s, :] for s in range(2)], axis=0)
    lead3, rest3 = halves(values)

    def pair(w, extra, at):
        x = jnp.concatenate([both(w * 4), both(w * 4 + 2)] + extra, axis=1)
        return contract(x.astype(BF16), at, 0, 0)

    turned = contract(jnp.concatenate([lead3, rest3], axis=1), eye, 0, 0)
    start = turned[:DK]
    turned = turned.astype(BF16)
    hist = []
    for w in range(HIST):
        two = pair(w, [], eye)
        hist.append([two[:DK], two[DK:], start[w * JW : (w + 1) * JW]])
    for t in range(STEPS):
        place = places[t]
        three = pair(t + HIST, [both(ROW_DECAY + 2 * t)], place)
        small = contract(turned, place, 1, 0)
        small = small[:DK] + small[DK:]
        new = [three[:DK], three[DK : 2 * DK], small[(t + HIST) * JW : (t + HIST + 1) * JW]]
        alive = small[LANE_ALIVE + t : LANE_ALIVE + t + 1] > 0.5
        logit = small[LANE_BETA + t : LANE_BETA + t + 1]
        strength = jnp.where(alive, sigmoid(logit), 0.0)
        retain = jnp.where(alive, jnp.exp(-three[2 * DK :]), 1.0)
        window = hist + [new]
        acts = []
        for part in range(3):
            cols = value_taps if part == 2 else taps[part]
            total = window[0][part] * cols[:, 0:1]
            for n in range(1, TAPS):
                total = total + window[n][part] * cols[:, n : n + 1]
            acts.append(total / (1.0 + jnp.exp(-total)))
        hist = [
            [jnp.where(alive, window[n + 1][part], window[n][part]) for part in range(3)]
            for n in range(HIST)
        ]
        query, key, value = acts
        ready[t, 0] = query / jnp.sqrt(jnp.sum(query * query, axis=0, keepdims=True) + EPS)
        ready[t, 1] = key / jnp.sqrt(jnp.sum(key * key, axis=0, keepdims=True) + EPS)
        ready[t, 2] = retain
        rows8[t] = jnp.concatenate([value, jnp.broadcast_to(strength, (JW, SLOTS))], axis=0)
    kept = []
    for n in range(HIST):
        for part in range(3):
            block = hist[n][part]
            if part < 2:
                xt[...] = block
                block = xt[mine, :]
            kept.append(block)
    kept = jnp.concatenate(kept, axis=0).astype(BF16)
    return contract(places[STEPS - 1], kept, 1, 1)


def run_steps(ready, rows8, places, mem):
    readouts = []
    for t in range(STEPS):
        query, key, retain = ready[t, 0], ready[t, 1], ready[t, 2]
        strength = rows8[t, JW : JW + 1, :]
        rows = []
        for j in range(JW):
            decayed = retain * mem[j]
            recalled = jnp.sum(key * decayed, axis=0, keepdims=True)
            updated = decayed + key * (strength * (rows8[t, j : j + 1, :] - recalled))
            mem[j] = updated
            rows.append(jnp.sum(query * updated, axis=0, keepdims=True) * DK**-0.5)
        lead, rest = halves(jnp.concatenate(rows, axis=0))
        place = places[t]
        readouts.append(contract(place, lead, 1, 1) + contract(place, rest, 1, 1))
    return readouts


def leave_states(place, mem, f1, b1):
    for j in range(JW):
        final = contract(place, mem[j].astype(BF16), 1, 1)
        for s in range(2):
            f1[pl.ds(s * JW + j, GROUPS, stride=16), :] = final[s * GROUPS : (s + 1) * GROUPS]

    def one(i, _):
        b1[i] = f1[pl.ds(pl.multiple_of(i * 16, 16), 16), :].astype(BF16)
        return 0

    lax.fori_loop(0, GROUPS, one, 0)


def ready_finish(gate, gain, live, spread, own, gains):
    own[...] = own_lanes()
    square = (DK, DK)
    for b in range(BLOCKS):
        spread[b] = jnp.where(iota(square, 0) == b * JW + (iota(square, 1) & 7), 1.0, 0.0).astype(BF16)
    second = iota((2 * HEADS, DK), 0) >> 2
    for t in range(STEPS):
        gates = sigmoid(jnp.concatenate(by_head(gate[t].astype(F32)), axis=0)) * gain[...]
        gains[t] = jnp.where(live[0:1, t : t + 1] > second, gates, 0.0)


def finish_rows(a2, gains, spread, own, weight, conv, partial, fc, fg):
    lead, rest = halves(jnp.concatenate([a2[:, s, :] for s in range(2)], axis=0))
    mask = own[...]

    def block(b):
        picked = contract(lead, spread[b], 1, 0)
        if b >= CONV:
            picked = picked + contract(rest, spread[b], 1, 0)
        picked = picked * mask
        rows = []
        for s in range(2):
            total = picked[s * GROUPS : s * GROUPS + ZS]
            for n in range(1, GROUPS // ZS):
                total = total + picked[s * GROUPS + n * ZS : s * GROUPS + (n + 1) * ZS]
            rows.append(total[:HEADS] + total[HEADS:])
        return jnp.concatenate(rows, axis=0)

    fg[...] = jnp.zeros_like(fg)
    for t in range(STEPS):
        readout = block(CONV + t)
        scaling = lax.rsqrt(jnp.sum(readout * readout, axis=1, keepdims=True) / DK + EPS)
        gated = readout * scaling * gains[t]
        for s in range(2):
            for h in range(HEADS):
                r = s * HEADS + h
                fg[2 * t + s : 2 * t + s + 1, h * DK : (h + 1) * DK] = gated[r : r + 1]
    total = jnp.dot(fg[...].astype(BF16), weight[...], preferred_element_type=F32)
    width = partial.shape[2]
    share = total.shape[1] // partial.shape[0]
    for d in range(partial.shape[0]):
        turned = total if d == 0 else pltpu.roll(total, total.shape[1] - d * share, 1)
        partial[d] = turned[:, :width].astype(BF16)
    for n in range(HIST):
        for part in range(3):
            kept = block(n * 3 + part)
            for s in range(2):
                for h in range(HEADS):
                    r = s * HEADS + h
                    fc[n, part, s : s + 1, h * DK : (h + 1) * DK] = kept[r : r + 1]
    conv[...] = fc[...].astype(BF16)


def remote(axis, peer, src, dst, sems, n):
    return pltpu.make_async_remote_copy(
        src_ref=src,
        dst_ref=dst,
        send_sem=sems.at[0, n],
        recv_sem=sems.at[1, n],
        device_id={axis: peer},
        device_id_type=pl.DeviceIdType.MESH,
    )


def peers_in_order(z, x, core, act, near=True, far=True):
    def off(dz, dx, dc):
        act(lax.rem(z + dz, ZS), lax.rem(x + dx, XS), lax.rem(core + dc, CS))

    def along_z(dx, dc):
        def one(q, _):
            off(4 + (1 - 2 * (q % 2)) * ((q + 1) // 2), dx, dc)
            return 0

        lax.fori_loop(0, ZS - 1, one, 0)

    if far:
        for dx in (2, 1, 3):
            for dc in (1, 0):
                along_z(dx, dc)
        along_z(0, 1)
    if near:
        along_z(0, 0)
        for dx in (2, 1, 3):
            off(0, dx, 1)
            off(0, dx, 0)
        off(0, 0, 1)


def whole(
    columns,
    states_in,
    conv_in,
    proj_in,
    taps_in,
    decay_in,
    rate_in,
    beta_in,
    gate_in,
    gain_in,
    weight_in,
    targets_in,
    live_in,
    a1,
    shares,
    conv_to,
    states,
    conv,
    proj,
    taps,
    decay,
    rate,
    beta,
    gate,
    gain,
    weight,
    targets,
    live,
    conv_out,
    s1,
    s2,
    s3,
    r1,
    r2,
    r3,
    b1,
    b2,
    a2,
    partial,
    f,
    f1,
    f2,
    mem,
    places,
    ready,
    rows8,
    xt,
    fc,
    fg,
    spread,
    own,
    gains,
    local,
    sems,
):
    me = lax.axis_index("rep")
    col = lax.axis_index("head")
    z, x, core = me // (XS * CS), (me // CS) % XS, me % CS
    mine = (core * XS + x) * ZS + z
    head, jg = z % HEADS, (z // HEADS) * 8 + core * XS + x

    barrier = pltpu.get_barrier_semaphore()

    def greet(axis, peer):
        pl.semaphore_signal(
            barrier, inc=1, device_id={axis: peer}, device_id_type=pl.DeviceIdType.MESH
        )

    for k in (4, 3, 5, 2, 6, 1, 7):
        greet("rep", (lax.rem(z + k, ZS) * XS + x) * CS + core)
    for k in (4, 3, 5, 2, 6, 1, 7):
        greet("head", lax.rem(col + k, columns))
    for k in range(1, XS * CS):
        greet("rep", z * XS * CS + lax.rem(x * CS + core + k, XS * CS))

    loads = [
        pltpu.make_async_copy(src, dst, local.at[n])
        for n, (src, dst) in enumerate(
            [
                (conv_in, conv),
                (proj_in, proj),
                (decay_in, decay),
                (rate_in, rate),
                (beta_in, beta),
                (live_in, live),
                (states_in, states),
                (targets_in, targets),
                (taps_in, taps),
                (gate_in, gate),
                (gain_in, gain),
                (weight_in, weight),
            ]
        )
    ]
    for load in loads:
        load.start()
    for load in loads[:4]:
        load.wait()
    pack_inputs(conv, proj, decay, rate, s2, f)
    pl.semaphore_wait(barrier, ZS - 1 + XS * CS - 1 + columns - 1)

    keep = pltpu.make_async_copy(s2.at[head], r2.at[core, x, z], local.at[12])
    keep.start()
    for k in (4, 3, 5, 2, 6, 1, 7):
        to = lax.rem(z + k, ZS)
        peer = (to * XS + x) * CS + core
        remote("rep", peer, s2.at[lax.rem(to, HEADS)], r2.at[core, x, z], sems, 0).start()

    for load in loads[4:9]:
        load.wait()
    pack_values(conv, proj, beta, live, s3)
    pack_states(states, s1)
    find_places(targets, places)

    keep_s = [
        pltpu.make_async_copy(s1.at[mine], r1.at[mine], local.at[13]),
        pltpu.make_async_copy(s3.at[mine], r3.at[mine], local.at[14]),
    ]
    for copy in keep_s:
        copy.start()

    def to_all(pairs, **which):
        def one(to_z, to_x, to_core):
            at = (to_core * XS + to_x) * ZS + to_z
            peer = (to_z * XS + to_x) * CS + to_core
            for src, dst, n in pairs:
                remote("rep", peer, src.at[at], dst.at[mine], sems, n).start()

        peers_in_order(z, x, core, one, **which)

    def from_all(dst, n):
        most = dst.at[pl.ds(0, GROUPS - 1)]
        done = remote("rep", me, most, most, sems, n)
        done.wait_send()
        done.wait_recv()

    to_all([(s3, r3, 5), (s1, r1, 6)], far=False)

    keep.wait()
    done = remote("rep", me, r2.at[0, 0, pl.ds(0, ZS - 1)], r2.at[0, 0, pl.ds(0, ZS - 1)], sems, 0)
    done.wait_send()
    done.wait_recv()
    right = (z * XS + lax.rem(x + 1, XS)) * CS + core
    left = (z * XS + lax.rem(x + XS - 1, XS)) * CS + core
    other = me + 1 - 2 * core
    half = ZS // 2
    behind, ahead = lax.rem(x + XS - 1, XS), lax.rem(x + 1, XS)

    def part(origin, n):
        return r2.at[core, origin, pl.ds(n * half, half)]

    def pass_on(peer, origin, n, sem):
        copy = remote("rep", peer, part(origin, n), part(origin, n), sems, sem)
        copy.start()
        return copy

    ring = [
        pass_on(right, x, 0, 1),
        pass_on(left, x, 1, 2),
        pass_on(right, x, 1, 3),
        pass_on(left, x, 0, 4),
    ]
    remote("rep", other, r2.at[core, x], r2.at[core, x], sems, 10).start()

    to_all([(s3, r3, 5), (s1, r1, 6)], near=False)

    widen_inputs(r2, f2, core, x, 0, ZS)

    def arrived(copy, origin, n):
        copy.wait_recv()
        pass_on(other, origin, n, 10)
        widen_inputs(r2, f2, core, origin, n * half, (n + 1) * half)

    ring[0].wait_recv()
    ring.append(pass_on(right, behind, 0, 11))
    pass_on(other, behind, 0, 10)
    ring[1].wait_recv()
    ring.append(pass_on(left, ahead, 1, 12))
    pass_on(other, ahead, 1, 10)
    widen_inputs(r2, f2, core, behind, 0, half)
    widen_inputs(r2, f2, core, ahead, half, ZS)
    arrived(ring[2], behind, 1)
    arrived(ring[3], ahead, 0)
    opposite = lax.rem(x + 2, XS)
    arrived(ring[4], opposite, 0)
    arrived(ring[5], opposite, 1)
    for copy in keep_s:
        copy.wait()
    for copy in ring:
        copy.wait_send()
    done = remote("rep", me, r2.at[0], r2.at[0], sems, 10)
    done.wait_send()
    done.wait_recv()
    for n in range(XS):
        widen_inputs(r2, f2, 1 - core, n, 0, ZS)
    from_all(r3, 5)
    cols = pl.ds(pl.multiple_of(head * DK, DK), DK)
    kept = prepare_steps(jg, f2, r3, taps.at[:, :, cols], places, ready, rows8, xt)
    from_all(r1, 6)
    enter_states(r1, f1, mem)
    readouts = run_steps(ready, rows8, places, mem)
    pad = jnp.zeros((SLOTS, DK - BLOCKS * JW), F32)
    returned = jnp.concatenate([kept] + readouts + [pad], axis=1)
    for s in range(2):
        b2[:, s, :] = returned[s * GROUPS : (s + 1) * GROUPS]
    keep = pltpu.make_async_copy(b2.at[mine], a2.at[mine], local.at[12])
    keep.start()
    to_all([(b2, a2, 7)])
    leave_states(places[STEPS - 1], mem, f1, b1)
    keep_states = pltpu.make_async_copy(b1.at[mine], a1.at[mine], local.at[13])
    keep_states.start()
    to_all([(b1, a1, 8)])
    for load in loads[9:]:
        load.wait()
    ready_finish(gate, gain, live, spread, own, gains)

    keep.wait()
    from_all(a2, 7)
    finish_rows(a2, gains, spread, own, weight, conv_out, partial, fc, fg)
    keep = pltpu.make_async_copy(partial.at[col], shares.at[col], local.at[12])
    keep.start()
    for k in (4, 3, 5, 2, 6, 1, 7):
        to = lax.rem(col + k, columns)
        remote("head", to, partial.at[to], shares.at[col], sems, 9).start()
    store = pltpu.make_async_copy(conv_out, conv_to, local.at[14])
    store.start()
    keep_states.wait()
    from_all(a1, 8)
    keep.wait()
    most = shares.at[pl.ds(0, columns - 1)]
    done = remote("head", col, most, most, sems, 9)
    done.wait_send()
    done.wait_recv()
    store.wait()


def settle(a1_in, shares_in, conv_in, out_to, states_to, conv_to, a1, shares, conv, out, states, sems):
    loads = [
        pltpu.make_async_copy(src, dst, sems.at[n])
        for n, (src, dst) in enumerate([(a1_in, a1), (shares_in, shares), (conv_in, conv)])
    ]
    for load in loads:
        load.start()
    loads[2].wait()
    stores = [pltpu.make_async_copy(conv, conv_to, sems.at[3])]
    stores[0].start()
    loads[0].wait()
    for h in range(HEADS):
        pieces = [a1[holder(h, jg)].astype(F32) for jg in range(JG)]
        for s in range(2):
            states[s, h] = jnp.concatenate([p[s * JW : (s + 1) * JW] for p in pieces], axis=0).T
            store = pltpu.make_async_copy(
                states.at[s, h], states_to.at[s, h], sems.at[4 + 2 * h + s]
            )
            store.start()
            stores.append(store)
    loads[1].wait()
    total = shares[0].astype(F32)
    for n in range(1, shares.shape[0]):
        total = total + shares[n].astype(F32)
    for t in range(STEPS):
        out[t] = total[2 * t : 2 * t + 2, : out.shape[2]].astype(BF16)
    stores.append(pltpu.make_async_copy(out, out_to, sems.at[4 + 2 * HEADS]))
    stores[-1].start()
    for store in stores:
        store.wait()


def shape(dims, kind):
    return jax.ShapeDtypeStruct(dims, kind)


def local(columns, *args):
    (
        states,
        conv_states,
        projected,
        conv_weight,
        decay_input,
        decay_rate,
        beta_logit,
        out_gate,
        norm_gain,
        out_weight,
        destinations,
        live_counts,
    ) = args
    operands = (
        states,
        conv_states.transpose(1, 2, 0, 3),
        projected.transpose(0, 2, 1, 3),
        conv_weight.transpose(1, 0, 2),
        decay_input,
        decay_rate.reshape(1, HEADS),
        beta_logit.transpose(1, 2, 0),
        out_gate,
        norm_gain.reshape(1, DK),
        out_weight,
        destinations,
        live_counts.transpose(1, 0),
    )
    share = out_weight.shape[1] // columns
    width = -(-share // DK) * DK
    block = pltpu.VMEM((GROUPS, 16, DK), BF16)
    small = pltpu.VMEM((GROUPS, 2, DK), F32)
    any_ = pl.BlockSpec(memory_space=pltpu.HBM)
    most = pltpu.CompilerParams(
        collective_id=0, has_side_effects=True, vmem_limit_bytes=60 * 1024 * 1024
    )
    landed = (
        shape((GROUPS, 16, DK), BF16),
        shape((columns, 16, width), BF16),
        shape(operands[1].shape, BF16),
    )
    pieces = pl.pallas_call(
        functools.partial(whole, columns),
        out_shape=landed,
        in_specs=[any_] * len(operands),
        out_specs=(any_,) * 3,
        scratch_shapes=[pltpu.VMEM(a.shape, a.dtype) for a in operands]
        + [
            pltpu.VMEM(operands[1].shape, BF16),
            block,
            pltpu.VMEM((HEADS, ROWS, DK), BF16),
            small,
            block,
            pltpu.VMEM((CS, XS, ZS, ROWS, DK), BF16),
            small,
            block,
            small,
            small,
            pltpu.VMEM((columns, 16, width), BF16),
            pltpu.VMEM((HEADS, ROWS, DK), F32),
            pltpu.VMEM(((GROUPS + 1) * 16, DK), F32),
            pltpu.VMEM(((GROUPS + 1) * ROWS, DK), F32),
            pltpu.VMEM((JW, DK, SLOTS), F32),
            pltpu.VMEM((STEPS, SLOTS, SLOTS), BF16),
            pltpu.VMEM((STEPS, 3, DK, SLOTS), F32),
            pltpu.VMEM((STEPS, 2 * JW, SLOTS), F32),
            pltpu.VMEM((DK, SLOTS), F32),
            pltpu.VMEM(operands[1].shape, F32),
            pltpu.VMEM((16, HEADS * DK), F32),
            pltpu.VMEM((BLOCKS, DK, DK), BF16),
            pltpu.VMEM((SLOTS, DK), F32),
            pltpu.VMEM((STEPS, 2 * HEADS, DK), F32),
            pltpu.SemaphoreType.DMA((15,)),
            pltpu.SemaphoreType.DMA((2, 13)),
        ],
        compiler_params=most,
        name="kda_steps",
    )(*operands)
    results = (
        shape((STEPS, 2, share), BF16),
        shape(states.shape, F32),
        shape(operands[1].shape, BF16),
    )
    out, states_out, conv_out = pl.pallas_call(
        settle,
        out_shape=results,
        in_specs=[any_] * 3,
        out_specs=(any_,) * 3,
        scratch_shapes=[pltpu.VMEM(a.shape, a.dtype) for a in landed]
        + [pltpu.VMEM(a.shape, a.dtype) for a in results[:2]]
        + [pltpu.SemaphoreType.DMA((5 + 2 * HEADS,))],
        compiler_params=pltpu.CompilerParams(vmem_limit_bytes=60 * 1024 * 1024),
        name="settle",
    )(*pieces)
    return out, states_out, conv_out.transpose(2, 0, 1, 3)


def solution(mesh):
    placed = (
        P("rep", "head", None, None),
        P("rep", None, None, "head"),
        P(None, "rep", None, "head"),
        P(None, None, "head"),
        P(None, "rep", "head"),
        P("head"),
        P(None, "rep", "head"),
        P(None, "rep", "head"),
        P(),
        P("head", None),
        P(),
        P(None, "rep"),
    )
    return jax.shard_map(
        functools.partial(local, mesh.shape["head"]),
        mesh=mesh,
        in_specs=placed,
        out_specs=(
            P(None, "rep", "head"),
            P("rep", "head", None, None),
            P("rep", None, None, "head"),
        ),
        check_vma=False,
    )
```

```python
import functools

import jax
import jax.numpy as jnp
from jax import lax
from jax.experimental import pallas as pl
from jax.experimental.pallas import tpu as pltpu
from jax.sharding import PartitionSpec as P

F32, BF16 = jnp.float32, jnp.bfloat16
STEPS, TAPS = 6, 4
HIST = TAPS - 1
ZS, XS, CS = 8, 4, 2
GROUPS, HEADS, DK = 64, 4, 128
SLOTS = 2 * GROUPS
JG, JW = 16, 8
WIN = HIST + STEPS
ROW_DECAY = WIN * 4
ROWS = ROW_DECAY + 2 * STEPS
LANE_ALIVE = WIN * JW
LANE_BETA = LANE_ALIVE + 8
CONV = 3 * HIST
BLOCKS = CONV + STEPS
EPS = 1e-6


def holder(h, jg):
    return (jg % 8) * ZS + (jg // 8) * HEADS + h


def iota(shape, dim):
    return lax.broadcasted_iota(jnp.int32, shape, dim)


def contract(a, b, da, db):
    return lax.dot_general(a, b, (((da,), (db,)), ((), ())), preferred_element_type=F32)


def halves(x):
    lead = x.astype(BF16)
    return lead, (x - lead.astype(F32)).astype(BF16)


def sigmoid(x):
    return 1.0 / (1.0 + jnp.exp(-x))


def softplus(x):
    return jnp.maximum(x, 0.0) + jnp.log1p(jnp.exp(-jnp.abs(x)))


def inner(slot):
    group = slot >> 1
    return ((slot & 1) << 6) + ((group & 1) << 5) + (((group >> 1) & 3) << 3) + (group >> 3)


def own_lanes():
    group = iota((SLOTS, DK), 0) & 63
    piece = (group >> 3) + ((group & 4) << 1)
    return jnp.where(piece == iota((SLOTS, DK), 1) >> 3, 1.0, 0.0)


def by_head(x):
    return [
        jnp.concatenate([x[s : s + 1, h * DK : (h + 1) * DK] for h in range(HEADS)], axis=0)
        for s in range(2)
    ]


def pack_inputs(conv, proj, decay, rate, s2, f):
    for w in range(WIN):
        for part in range(2):
            block = (conv[w, part] if w < HIST else proj[w - HIST, part]).astype(F32)
            at = (w * 2 + part) * 2
            for h in range(HEADS):
                f[h, at : at + 2, :] = block[:, h * DK : (h + 1) * DK]
    for t in range(STEPS):
        exponent = softplus(decay[t])
        for h in range(HEADS):
            at = ROW_DECAY + 2 * t
            f[h, at : at + 2, :] = exponent[:, h * DK : (h + 1) * DK] * rate[0:1, h : h + 1]
    for h in range(HEADS):
        s2[h] = f[h].astype(BF16)


def pack_values(conv, proj, beta, live, s3):
    mask = own_lanes()
    parts = []
    for w in range(WIN):
        block = (conv[w, 2] if w < HIST else proj[w - HIST, 2]).astype(F32)
        rows = []
        for four in by_head(block):
            rows += [four] * (2 * ZS)
        parts.append((jnp.concatenate(rows, axis=0) * mask).astype(BF16))
    shape = (WIN * DK, DK)
    place = jnp.where(((iota(shape, 0) >> 7) << 3) + (iota(shape, 0) & 7) == iota(shape, 1), 1.0, 0.0)
    packed = contract(jnp.concatenate(parts, axis=1), place.astype(BF16), 1, 0)
    for s in range(2):
        alive = jnp.where(live[...] > s, 1.0, 0.0)
        row = jnp.concatenate(
            [
                jnp.zeros((HEADS, LANE_ALIVE), F32),
                jnp.broadcast_to(alive, (HEADS, STEPS)),
                jnp.zeros((HEADS, 8 - STEPS), F32),
                beta[s],
                jnp.zeros((HEADS, DK - LANE_BETA - STEPS), F32),
            ],
            axis=1,
        )
        rest = jnp.concatenate([row] * (2 * ZS), axis=0)
        s3[:, s, :] = packed[s * GROUPS : (s + 1) * GROUPS] + rest


def pack_states(states, s1):
    for h in range(HEADS):
        first, second = states[0, h].T, states[1, h].T
        for jg in range(JG):
            rows = slice(jg * JW, (jg + 1) * JW)
            s1[holder(h, jg)] = jnp.concatenate([first[rows], second[rows]], axis=0).astype(BF16)


def widen_inputs(r2, f2, core, x):
    def one(i, _):
        at = pl.multiple_of(((core * XS + x) * ZS + i) * ROWS, ROWS)
        f2[pl.ds(at, ROWS), :] = r2[core, x, i].astype(F32)
        return 0

    lax.fori_loop(0, ZS, one, 0)


def enter_states(r1, f1, mem):
    def one(i, _):
        f1[pl.ds(pl.multiple_of(i * 16, 16), 16), :] = r1[i].astype(F32)
        return 0

    lax.fori_loop(0, GROUPS, one, 0)
    for j in range(JW):
        rows = [f1[pl.ds(s * JW + j, GROUPS, stride=16), :] for s in range(2)]
        mem[j] = jnp.concatenate(rows, axis=0).T


def find_places(targets, places):
    square = (SLOTS, SLOTS)
    back = jnp.where(inner(iota(square, 0)) == iota(square, 1), 1.0, 0.0).astype(BF16)
    held = back
    for t in range(STEPS):
        move = jnp.where(iota(square, 0) == inner(targets[t : t + 1, :]), 1.0, 0.0).astype(BF16)
        place = contract(move, held, 1, 0).astype(BF16)
        places[t] = place
        if t < STEPS - 1:
            held = contract(back, place, 1, 0).astype(BF16)


def prepare_steps(jg, f2, r3, weight, places, ready, rows8, xt):
    def both(row):
        return jnp.concatenate(
            [f2[pl.ds(row + s, GROUPS, stride=ROWS), :] for s in range(2)], axis=0
        )

    square = (SLOTS, SLOTS)
    eye = jnp.where(iota(square, 0) == iota(square, 1), 1.0, 0.0).astype(BF16)
    taps = [weight[part].T for part in range(3)]
    xt[0:DK, 0:TAPS] = taps[2]
    mine = pl.ds(pl.multiple_of(jg * JW, JW), JW)
    value_taps = xt[mine, 0:TAPS]
    values = jnp.concatenate([r3[:, s, :] for s in range(2)], axis=0)
    lead3, rest3 = halves(values)

    def pair(w, extra, at):
        x = jnp.concatenate([both(w * 4), both(w * 4 + 2)] + extra, axis=1)
        return contract(x.astype(BF16), at, 0, 0)

    turned = contract(jnp.concatenate([lead3, rest3], axis=1), eye, 0, 0)
    start = turned[:DK]
    turned = turned.astype(BF16)
    hist = []
    for w in range(HIST):
        two = pair(w, [], eye)
        hist.append([two[:DK], two[DK:], start[w * JW : (w + 1) * JW]])
    for t in range(STEPS):
        place = places[t]
        three = pair(t + HIST, [both(ROW_DECAY + 2 * t)], place)
        small = contract(turned, place, 1, 0)
        small = small[:DK] + small[DK:]
        new = [three[:DK], three[DK : 2 * DK], small[(t + HIST) * JW : (t + HIST + 1) * JW]]
        alive = small[LANE_ALIVE + t : LANE_ALIVE + t + 1] > 0.5
        logit = small[LANE_BETA + t : LANE_BETA + t + 1]
        strength = jnp.where(alive, sigmoid(logit), 0.0)
        retain = jnp.where(alive, jnp.exp(-three[2 * DK :]), 1.0)
        window = hist + [new]
        acts = []
        for part in range(3):
            cols = value_taps if part == 2 else taps[part]
            total = window[0][part] * cols[:, 0:1]
            for n in range(1, TAPS):
                total = total + window[n][part] * cols[:, n : n + 1]
            acts.append(total / (1.0 + jnp.exp(-total)))
        hist = [
            [jnp.where(alive, window[n + 1][part], window[n][part]) for part in range(3)]
            for n in range(HIST)
        ]
        query, key, value = acts
        ready[t, 0] = query / jnp.sqrt(jnp.sum(query * query, axis=0, keepdims=True) + EPS)
        ready[t, 1] = key / jnp.sqrt(jnp.sum(key * key, axis=0, keepdims=True) + EPS)
        ready[t, 2] = retain
        rows8[t] = jnp.concatenate([value, jnp.broadcast_to(strength, (JW, SLOTS))], axis=0)
    kept = []
    for n in range(HIST):
        for part in range(3):
            block = hist[n][part]
            if part < 2:
                xt[...] = block
                block = xt[mine, :]
            kept.append(block)
    kept = jnp.concatenate(kept, axis=0).astype(BF16)
    return contract(places[STEPS - 1], kept, 1, 1)


def run_steps(ready, rows8, places, mem):
    readouts = []
    for t in range(STEPS):
        query, key, retain = ready[t, 0], ready[t, 1], ready[t, 2]
        strength = rows8[t, JW : JW + 1, :]
        rows = []
        for j in range(JW):
            decayed = retain * mem[j]
            recalled = jnp.sum(key * decayed, axis=0, keepdims=True)
            updated = decayed + key * (strength * (rows8[t, j : j + 1, :] - recalled))
            mem[j] = updated
            rows.append(jnp.sum(query * updated, axis=0, keepdims=True) * DK**-0.5)
        lead, rest = halves(jnp.concatenate(rows, axis=0))
        place = places[t]
        readouts.append(contract(place, lead, 1, 1) + contract(place, rest, 1, 1))
    return readouts


def leave_states(place, mem, f1, b1):
    for j in range(JW):
        final = contract(place, mem[j].astype(BF16), 1, 1)
        for s in range(2):
            f1[pl.ds(s * JW + j, GROUPS, stride=16), :] = final[s * GROUPS : (s + 1) * GROUPS]

    def one(i, _):
        b1[i] = f1[pl.ds(pl.multiple_of(i * 16, 16), 16), :].astype(BF16)
        return 0

    lax.fori_loop(0, GROUPS, one, 0)


def ready_finish(gate, gain, live, spread, own, gains):
    own[...] = own_lanes()
    square = (DK, DK)
    for b in range(BLOCKS):
        spread[b] = jnp.where(iota(square, 0) == b * JW + (iota(square, 1) & 7), 1.0, 0.0).astype(BF16)
    second = iota((2 * HEADS, DK), 0) >> 2
    for t in range(STEPS):
        gates = sigmoid(jnp.concatenate(by_head(gate[t].astype(F32)), axis=0)) * gain[...]
        gains[t] = jnp.where(live[0:1, t : t + 1] > second, gates, 0.0)


def finish_rows(a2, gains, spread, own, weight, conv, partial, fc, fg):
    lead, rest = halves(jnp.concatenate([a2[:, s, :] for s in range(2)], axis=0))
    mask = own[...]

    def block(b):
        picked = contract(lead, spread[b], 1, 0)
        if b >= CONV:
            picked = picked + contract(rest, spread[b], 1, 0)
        picked = picked * mask
        rows = []
        for s in range(2):
            total = picked[s * GROUPS : s * GROUPS + ZS]
            for n in range(1, GROUPS // ZS):
                total = total + picked[s * GROUPS + n * ZS : s * GROUPS + (n + 1) * ZS]
            rows.append(total[:HEADS] + total[HEADS:])
        return jnp.concatenate(rows, axis=0)

    fg[...] = jnp.zeros_like(fg)
    for t in range(STEPS):
        readout = block(CONV + t)
        scaling = lax.rsqrt(jnp.sum(readout * readout, axis=1, keepdims=True) / DK + EPS)
        gated = readout * scaling * gains[t]
        for s in range(2):
            for h in range(HEADS):
                r = s * HEADS + h
                fg[2 * t + s : 2 * t + s + 1, h * DK : (h + 1) * DK] = gated[r : r + 1]
    total = jnp.dot(fg[...].astype(BF16), weight[...], preferred_element_type=F32)
    width = partial.shape[2]
    share = total.shape[1] // partial.shape[0]
    for d in range(partial.shape[0]):
        base = d * share // DK * DK
        piece = total[:, base : min(base + width + DK, total.shape[1])]
        if d * share > base:
            piece = pltpu.roll(piece, piece.shape[1] - (d * share - base), 1)
        partial[d] = piece[:, :width].astype(BF16)
    for n in range(HIST):
        for part in range(3):
            kept = block(n * 3 + part)
            for s in range(2):
                for h in range(HEADS):
                    r = s * HEADS + h
                    fc[n, part, s : s + 1, h * DK : (h + 1) * DK] = kept[r : r + 1]
    conv[...] = fc[...].astype(BF16)


def remote(axis, peer, src, dst, sems, n):
    return pltpu.make_async_remote_copy(
        src_ref=src,
        dst_ref=dst,
        send_sem=sems.at[0, n],
        recv_sem=sems.at[1, n],
        device_id={axis: peer},
        device_id_type=pl.DeviceIdType.MESH,
    )


def peers_in_order(z, x, core, act, near=True, far=True):
    def off(dz, dx, dc):
        act(lax.rem(z + dz, ZS), lax.rem(x + dx, XS), lax.rem(core + dc, CS))

    def along_z(dx, dc):
        def one(q, _):
            off(4 + (1 - 2 * (q % 2)) * ((q + 1) // 2), dx, dc)
            return 0

        lax.fori_loop(0, ZS - 1, one, 0)

    if far:
        for dx in (2, 1, 3):
            for dc in (1, 0):
                along_z(dx, dc)
        along_z(0, 1)
    if near:
        along_z(0, 0)
        for dx in (2, 1, 3):
            off(0, dx, 1)
            off(0, dx, 0)
        off(0, 0, 1)


def whole(
    columns,
    states_in,
    conv_in,
    proj_in,
    taps_in,
    decay_in,
    rate_in,
    beta_in,
    gate_in,
    gain_in,
    weight_in,
    targets_in,
    live_in,
    a1,
    shares,
    conv_to,
    states,
    conv,
    proj,
    taps,
    decay,
    rate,
    beta,
    gate,
    gain,
    weight,
    targets,
    live,
    conv_out,
    s1,
    s2,
    s3,
    r1,
    r2,
    r3,
    b1,
    b2,
    a2,
    partial,
    f,
    f1,
    f2,
    mem,
    places,
    ready,
    rows8,
    xt,
    fc,
    fg,
    spread,
    own,
    gains,
    local,
    sems,
):
    me = lax.axis_index("rep")
    col = lax.axis_index("head")
    z, x, core = me // (XS * CS), (me // CS) % XS, me % CS
    mine = (core * XS + x) * ZS + z
    head, jg = z % HEADS, (z // HEADS) * 8 + core * XS + x

    barrier = pltpu.get_barrier_semaphore()

    def greet(axis, peer):
        pl.semaphore_signal(
            barrier, inc=1, device_id={axis: peer}, device_id_type=pl.DeviceIdType.MESH
        )

    for k in (4, 3, 5, 2, 6, 1, 7):
        greet("rep", (lax.rem(z + k, ZS) * XS + x) * CS + core)
    for k in (4, 3, 5, 2, 6, 1, 7):
        greet("head", lax.rem(col + k, columns))
    for k in range(1, XS * CS):
        greet("rep", z * XS * CS + lax.rem(x * CS + core + k, XS * CS))

    loads = [
        pltpu.make_async_copy(src, dst, local.at[n])
        for n, (src, dst) in enumerate(
            [
                (conv_in, conv),
                (proj_in, proj),
                (decay_in, decay),
                (rate_in, rate),
                (beta_in, beta),
                (live_in, live),
                (states_in, states),
                (targets_in, targets),
                (taps_in, taps),
                (gate_in, gate),
                (gain_in, gain),
                (weight_in, weight),
            ]
        )
    ]
    for load in loads:
        load.start()
    for load in loads[:4]:
        load.wait()
    pack_inputs(conv, proj, decay, rate, s2, f)
    pl.semaphore_wait(barrier, ZS - 1 + XS * CS - 1 + columns - 1)

    keep = pltpu.make_async_copy(s2.at[head], r2.at[core, x, z], local.at[12])
    keep.start()
    for k in (4, 3, 5, 2, 6, 1, 7):
        to = lax.rem(z + k, ZS)
        peer = (to * XS + x) * CS + core
        remote("rep", peer, s2.at[lax.rem(to, HEADS)], r2.at[core, x, z], sems, 0).start()

    for load in loads[4:9]:
        load.wait()
    pack_values(conv, proj, beta, live, s3)
    pack_states(states, s1)
    find_places(targets, places)

    keep_s = [
        pltpu.make_async_copy(s1.at[mine], r1.at[mine], local.at[13]),
        pltpu.make_async_copy(s3.at[mine], r3.at[mine], local.at[14]),
    ]
    for copy in keep_s:
        copy.start()

    def to_all(pairs, **which):
        def one(to_z, to_x, to_core):
            at = (to_core * XS + to_x) * ZS + to_z
            peer = (to_z * XS + to_x) * CS + to_core
            for src, dst, n in pairs:
                remote("rep", peer, src.at[at], dst.at[mine], sems, n).start()

        peers_in_order(z, x, core, one, **which)

    def from_all(dst, n):
        most = dst.at[pl.ds(0, GROUPS - 1)]
        done = remote("rep", me, most, most, sems, n)
        done.wait_send()
        done.wait_recv()

    to_all([(s3, r3, 5), (s1, r1, 6)], far=False)

    keep.wait()
    done = remote("rep", me, r2.at[0, 0, pl.ds(0, ZS - 1)], r2.at[0, 0, pl.ds(0, ZS - 1)], sems, 0)
    done.wait_send()
    done.wait_recv()
    right = (z * XS + lax.rem(x + 1, XS)) * CS + core
    left = (z * XS + lax.rem(x + XS - 1, XS)) * CS + core
    other = me + 1 - 2 * core
    behind, ahead = lax.rem(x + XS - 1, XS), lax.rem(x + 1, XS)

    opposite = lax.rem(x + 2, XS)
    facing = (z * XS + opposite) * CS + core

    def block_to(peer, origin, sem):
        copy = remote("rep", peer, r2.at[core, origin], r2.at[core, origin], sems, sem)
        copy.start()
        return copy

    ring = [block_to(facing, x, 1), block_to(right, x, 2), block_to(left, x, 3)]

    to_all([(s3, r3, 5), (s1, r1, 6)], near=False)

    block_to(other, x, 10)
    widen_inputs(r2, f2, core, x)

    for copy, origin in ((ring[1], behind), (ring[2], ahead), (ring[0], opposite)):
        copy.wait_recv()
        block_to(other, origin, 10)
        widen_inputs(r2, f2, core, origin)
    for copy in keep_s:
        copy.wait()
    for copy in ring:
        copy.wait_send()
    done = remote("rep", me, r2.at[0], r2.at[0], sems, 10)
    done.wait_send()
    done.wait_recv()
    for n in range(XS):
        widen_inputs(r2, f2, 1 - core, n)
    from_all(r3, 5)
    cols = pl.ds(pl.multiple_of(head * DK, DK), DK)
    kept = prepare_steps(jg, f2, r3, taps.at[:, :, cols], places, ready, rows8, xt)
    from_all(r1, 6)
    enter_states(r1, f1, mem)
    readouts = run_steps(ready, rows8, places, mem)
    pad = jnp.zeros((SLOTS, DK - BLOCKS * JW), F32)
    returned = jnp.concatenate([kept] + readouts + [pad], axis=1)
    for s in range(2):
        b2[:, s, :] = returned[s * GROUPS : (s + 1) * GROUPS]
    keep = pltpu.make_async_copy(b2.at[mine], a2.at[mine], local.at[12])
    keep.start()
    to_all([(b2, a2, 7)])
    leave_states(places[STEPS - 1], mem, f1, b1)
    keep_states = pltpu.make_async_copy(b1.at[mine], a1.at[mine], local.at[13])
    keep_states.start()
    to_all([(b1, a1, 8)])
    for load in loads[9:]:
        load.wait()
    ready_finish(gate, gain, live, spread, own, gains)

    keep.wait()
    from_all(a2, 7)
    finish_rows(a2, gains, spread, own, weight, conv_out, partial, fc, fg)
    keep = pltpu.make_async_copy(partial.at[col], shares.at[col], local.at[12])
    keep.start()
    for k in (4, 3, 5, 2, 6, 1, 7):
        to = lax.rem(col + k, columns)
        remote("head", to, partial.at[to], shares.at[col], sems, 9).start()
    store = pltpu.make_async_copy(conv_out, conv_to, local.at[14])
    store.start()
    keep_states.wait()
    from_all(a1, 8)
    keep.wait()
    most = shares.at[pl.ds(0, columns - 1)]
    done = remote("head", col, most, most, sems, 9)
    done.wait_send()
    done.wait_recv()
    store.wait()


def settle(a1_in, shares_in, conv_in, out_to, states_to, conv_to, a1, shares, conv, out, states, sems):
    loads = [
        pltpu.make_async_copy(src, dst, sems.at[n])
        for n, (src, dst) in enumerate([(a1_in, a1), (shares_in, shares), (conv_in, conv)])
    ]
    for n in (1, 0, 2):
        loads[n].start()
    loads[2].wait()
    stores = [pltpu.make_async_copy(conv, conv_to, sems.at[3])]
    stores[0].start()
    loads[1].wait()
    total = shares[0].astype(F32)
    for n in range(1, shares.shape[0]):
        total = total + shares[n].astype(F32)
    for t in range(STEPS):
        out[t] = total[2 * t : 2 * t + 2, : out.shape[2]].astype(BF16)
    stores.append(pltpu.make_async_copy(out, out_to, sems.at[4 + 2 * HEADS]))
    stores[-1].start()
    loads[0].wait()
    for h in range(HEADS):
        pieces = [a1[holder(h, jg)].astype(F32) for jg in range(JG)]
        for s in range(2):
            states[s, h] = jnp.concatenate([p[s * JW : (s + 1) * JW] for p in pieces], axis=0).T
            store = pltpu.make_async_copy(
                states.at[s, h], states_to.at[s, h], sems.at[4 + 2 * h + s]
            )
            store.start()
            stores.append(store)
    for store in stores:
        store.wait()


def shape(dims, kind):
    return jax.ShapeDtypeStruct(dims, kind)


def local(columns, *args):
    (
        states,
        conv_states,
        projected,
        conv_weight,
        decay_input,
        decay_rate,
        beta_logit,
        out_gate,
        norm_gain,
        out_weight,
        destinations,
        live_counts,
    ) = args
    operands = (
        states,
        conv_states.transpose(1, 2, 0, 3),
        projected.transpose(0, 2, 1, 3),
        conv_weight.transpose(1, 0, 2),
        decay_input,
        decay_rate.reshape(1, HEADS),
        beta_logit.transpose(1, 2, 0),
        out_gate,
        norm_gain.reshape(1, DK),
        out_weight,
        destinations,
        live_counts.transpose(1, 0),
    )
    share = out_weight.shape[1] // columns
    width = -(-share // DK) * DK
    block = pltpu.VMEM((GROUPS, 16, DK), BF16)
    small = pltpu.VMEM((GROUPS, 2, DK), F32)
    any_ = pl.BlockSpec(memory_space=pltpu.HBM)
    most = pltpu.CompilerParams(
        collective_id=0, has_side_effects=True, vmem_limit_bytes=60 * 1024 * 1024
    )
    landed = (
        shape((GROUPS, 16, DK), BF16),
        shape((columns, 16, width), BF16),
        shape(operands[1].shape, BF16),
    )
    pieces = pl.pallas_call(
        functools.partial(whole, columns),
        out_shape=landed,
        in_specs=[any_] * len(operands),
        out_specs=(any_,) * 3,
        scratch_shapes=[pltpu.VMEM(a.shape, a.dtype) for a in operands]
        + [
            pltpu.VMEM(operands[1].shape, BF16),
            block,
            pltpu.VMEM((HEADS, ROWS, DK), BF16),
            small,
            block,
            pltpu.VMEM((CS, XS, ZS, ROWS, DK), BF16),
            small,
            block,
            small,
            small,
            pltpu.VMEM((columns, 16, width), BF16),
            pltpu.VMEM((HEADS, ROWS, DK), F32),
            pltpu.VMEM(((GROUPS + 1) * 16, DK), F32),
            pltpu.VMEM(((GROUPS + 1) * ROWS, DK), F32),
            pltpu.VMEM((JW, DK, SLOTS), F32),
            pltpu.VMEM((STEPS, SLOTS, SLOTS), BF16),
            pltpu.VMEM((STEPS, 3, DK, SLOTS), F32),
            pltpu.VMEM((STEPS, 2 * JW, SLOTS), F32),
            pltpu.VMEM((DK, SLOTS), F32),
            pltpu.VMEM(operands[1].shape, F32),
            pltpu.VMEM((16, HEADS * DK), F32),
            pltpu.VMEM((BLOCKS, DK, DK), BF16),
            pltpu.VMEM((SLOTS, DK), F32),
            pltpu.VMEM((STEPS, 2 * HEADS, DK), F32),
            pltpu.SemaphoreType.DMA((15,)),
            pltpu.SemaphoreType.DMA((2, 13)),
        ],
        compiler_params=most,
        name="kda_steps",
    )(*operands)
    results = (
        shape((STEPS, 2, share), BF16),
        shape(states.shape, F32),
        shape(operands[1].shape, BF16),
    )
    out, states_out, conv_out = pl.pallas_call(
        settle,
        out_shape=results,
        in_specs=[any_] * 3,
        out_specs=(any_,) * 3,
        scratch_shapes=[pltpu.VMEM(a.shape, a.dtype) for a in landed]
        + [pltpu.VMEM(a.shape, a.dtype) for a in results[:2]]
        + [pltpu.SemaphoreType.DMA((5 + 2 * HEADS,))],
        compiler_params=pltpu.CompilerParams(vmem_limit_bytes=60 * 1024 * 1024),
        name="settle",
    )(*pieces)
    return out, states_out, conv_out.transpose(2, 0, 1, 3)


def solution(mesh):
    placed = (
        P("rep", "head", None, None),
        P("rep", None, None, "head"),
        P(None, "rep", None, "head"),
        P(None, None, "head"),
        P(None, "rep", "head"),
        P("head"),
        P(None, "rep", "head"),
        P(None, "rep", "head"),
        P(),
        P("head", None),
        P(),
        P(None, "rep"),
    )
    return jax.shard_map(
        functools.partial(local, mesh.shape["head"]),
        mesh=mesh,
        in_specs=placed,
        out_specs=(
            P(None, "rep", "head"),
            P("rep", "head", None, None),
            P("rep", None, None, "head"),
        ),
        check_vma=False,
    )
```

```python
import functools

import jax
import jax.numpy as jnp
from jax import lax
from jax.experimental import pallas as pl
from jax.experimental.pallas import tpu as pltpu
from jax.sharding import PartitionSpec as P

F32, BF16 = jnp.float32, jnp.bfloat16
STEPS, TAPS = 6, 4
HIST = TAPS - 1
ZS, XS, CS = 8, 4, 2
GROUPS, HEADS, DK = 64, 4, 128
SLOTS = 2 * GROUPS
JG, JW = 16, 8
WIN = HIST + STEPS
ROW_DECAY = WIN * 4
ROWS = ROW_DECAY + 2 * STEPS
LANE_ALIVE = WIN * JW
LANE_BETA = LANE_ALIVE + 8
CONV = 3 * HIST
BLOCKS = CONV + STEPS
EPS = 1e-6


def holder(h, jg):
    return (jg % 8) * ZS + (jg // 8) * HEADS + h


def iota(shape, dim):
    return lax.broadcasted_iota(jnp.int32, shape, dim)


def contract(a, b, da, db):
    return lax.dot_general(a, b, (((da,), (db,)), ((), ())), preferred_element_type=F32)


def halves(x):
    lead = x.astype(BF16)
    return lead, (x - lead.astype(F32)).astype(BF16)


def sigmoid(x):
    return 1.0 / (1.0 + jnp.exp(-x))


def softplus(x):
    return jnp.maximum(x, 0.0) + jnp.log1p(jnp.exp(-jnp.abs(x)))


def inner(slot):
    group = slot >> 1
    return ((slot & 1) << 6) + ((group & 1) << 5) + (((group >> 1) & 3) << 3) + (group >> 3)


def own_lanes():
    group = iota((SLOTS, DK), 0) & 63
    piece = (group >> 3) + ((group & 4) << 1)
    return jnp.where(piece == iota((SLOTS, DK), 1) >> 3, 1.0, 0.0)


def by_head(x):
    return [
        jnp.concatenate([x[s : s + 1, h * DK : (h + 1) * DK] for h in range(HEADS)], axis=0)
        for s in range(2)
    ]


def pack_inputs(conv, proj, decay, rate, s2, f):
    for w in range(WIN):
        for part in range(2):
            block = (conv[w, part] if w < HIST else proj[w - HIST, part]).astype(F32)
            at = (w * 2 + part) * 2
            for h in range(HEADS):
                f[h, at : at + 2, :] = block[:, h * DK : (h + 1) * DK]
    for t in range(STEPS):
        exponent = softplus(decay[t])
        for h in range(HEADS):
            at = ROW_DECAY + 2 * t
            f[h, at : at + 2, :] = exponent[:, h * DK : (h + 1) * DK] * rate[0:1, h : h + 1]
    for h in range(HEADS):
        s2[h] = f[h].astype(BF16)


def pack_values(conv, proj, beta, live, s3):
    mask = own_lanes()
    parts = []
    for w in range(WIN):
        block = (conv[w, 2] if w < HIST else proj[w - HIST, 2]).astype(F32)
        rows = []
        for four in by_head(block):
            rows += [four] * (2 * ZS)
        parts.append((jnp.concatenate(rows, axis=0) * mask).astype(BF16))
    shape = (WIN * DK, DK)
    place = jnp.where(((iota(shape, 0) >> 7) << 3) + (iota(shape, 0) & 7) == iota(shape, 1), 1.0, 0.0)
    packed = contract(jnp.concatenate(parts, axis=1), place.astype(BF16), 1, 0)
    for s in range(2):
        alive = jnp.where(live[...] > s, 1.0, 0.0)
        row = jnp.concatenate(
            [
                jnp.zeros((HEADS, LANE_ALIVE), F32),
                jnp.broadcast_to(alive, (HEADS, STEPS)),
                jnp.zeros((HEADS, 8 - STEPS), F32),
                beta[s],
                jnp.zeros((HEADS, DK - LANE_BETA - STEPS), F32),
            ],
            axis=1,
        )
        rest = jnp.concatenate([row] * (2 * ZS), axis=0)
        s3[:, s, :] = packed[s * GROUPS : (s + 1) * GROUPS] + rest


def pack_states(states, s1):
    for h in range(HEADS):
        first, second = states[0, h].T, states[1, h].T
        for jg in range(JG):
            rows = slice(jg * JW, (jg + 1) * JW)
            s1[holder(h, jg)] = jnp.concatenate([first[rows], second[rows]], axis=0).astype(BF16)


def widen_inputs(r2, f2, core, x, first, last):
    def one(i, _):
        at = pl.multiple_of(((core * XS + x) * ZS + i) * ROWS, ROWS)
        f2[pl.ds(at, ROWS), :] = r2[core, x, i].astype(F32)
        return 0

    lax.fori_loop(first, last, one, 0)


def enter_states(r1, f1, mem):
    def one(i, _):
        f1[pl.ds(pl.multiple_of(i * 16, 16), 16), :] = r1[i].astype(F32)
        return 0

    lax.fori_loop(0, GROUPS, one, 0)
    for j in range(JW):
        rows = [f1[pl.ds(s * JW + j, GROUPS, stride=16), :] for s in range(2)]
        mem[j] = jnp.concatenate(rows, axis=0).T


def find_places(targets, places):
    square = (SLOTS, SLOTS)
    back = jnp.where(inner(iota(square, 0)) == iota(square, 1), 1.0, 0.0).astype(BF16)
    held = back
    for t in range(STEPS):
        move = jnp.where(iota(square, 0) == inner(targets[t : t + 1, :]), 1.0, 0.0).astype(BF16)
        place = contract(move, held, 1, 0).astype(BF16)
        places[t] = place
        if t < STEPS - 1:
            held = contract(back, place, 1, 0).astype(BF16)


def prepare_steps(jg, f2, r3, weight, places, ready, rows8, xt):
    def both(row):
        return jnp.concatenate(
            [f2[pl.ds(row + s, GROUPS, stride=ROWS), :] for s in range(2)], axis=0
        )

    square = (SLOTS, SLOTS)
    eye = jnp.where(iota(square, 0) == iota(square, 1), 1.0, 0.0).astype(BF16)
    taps = [weight[part].T for part in range(3)]
    xt[0:DK, 0:TAPS] = taps[2]
    mine = pl.ds(pl.multiple_of(jg * JW, JW), JW)
    value_taps = xt[mine, 0:TAPS]
    values = jnp.concatenate([r3[:, s, :] for s in range(2)], axis=0)
    lead3, rest3 = halves(values)

    def pair(w, extra, at):
        x = jnp.concatenate([both(w * 4), both(w * 4 + 2)] + extra, axis=1)
        return contract(x.astype(BF16), at, 0, 0)

    turned = contract(jnp.concatenate([lead3, rest3], axis=1), eye, 0, 0)
    start = turned[:DK]
    turned = turned.astype(BF16)
    hist = []
    for w in range(HIST):
        two = pair(w, [], eye)
        hist.append([two[:DK], two[DK:], start[w * JW : (w + 1) * JW]])
    for t in range(STEPS):
        place = places[t]
        three = pair(t + HIST, [both(ROW_DECAY + 2 * t)], place)
        small = contract(turned, place, 1, 0)
        small = small[:DK] + small[DK:]
        new = [three[:DK], three[DK : 2 * DK], small[(t + HIST) * JW : (t + HIST + 1) * JW]]
        alive = small[LANE_ALIVE + t : LANE_ALIVE + t + 1] > 0.5
        logit = small[LANE_BETA + t : LANE_BETA + t + 1]
        strength = jnp.where(alive, sigmoid(logit), 0.0)
        retain = jnp.where(alive, jnp.exp(-three[2 * DK :]), 1.0)
        window = hist + [new]
        acts = []
        for part in range(3):
            cols = value_taps if part == 2 else taps[part]
            total = window[0][part] * cols[:, 0:1]
            for n in range(1, TAPS):
                total = total + window[n][part] * cols[:, n : n + 1]
            acts.append(total / (1.0 + jnp.exp(-total)))
        hist = [
            [jnp.where(alive, window[n + 1][part], window[n][part]) for part in range(3)]
            for n in range(HIST)
        ]
        query, key, value = acts
        ready[t, 0] = query / jnp.sqrt(jnp.sum(query * query, axis=0, keepdims=True) + EPS)
        ready[t, 1] = key / jnp.sqrt(jnp.sum(key * key, axis=0, keepdims=True) + EPS)
        ready[t, 2] = retain
        rows8[t] = jnp.concatenate([value, jnp.broadcast_to(strength, (JW, SLOTS))], axis=0)
    kept = []
    for n in range(HIST):
        for part in range(3):
            block = hist[n][part]
            if part < 2:
                xt[...] = block
                block = xt[mine, :]
            kept.append(block)
    kept = jnp.concatenate(kept, axis=0).astype(BF16)
    return contract(places[STEPS - 1], kept, 1, 1)


def run_steps(ready, rows8, places, mem):
    readouts = []
    for t in range(STEPS):
        query, key, retain = ready[t, 0], ready[t, 1], ready[t, 2]
        strength = rows8[t, JW : JW + 1, :]
        rows = []
        for j in range(JW):
            decayed = retain * mem[j]
            recalled = jnp.sum(key * decayed, axis=0, keepdims=True)
            updated = decayed + key * (strength * (rows8[t, j : j + 1, :] - recalled))
            mem[j] = updated
            rows.append(jnp.sum(query * updated, axis=0, keepdims=True) * DK**-0.5)
        lead, rest = halves(jnp.concatenate(rows, axis=0))
        place = places[t]
        readouts.append(contract(place, lead, 1, 1) + contract(place, rest, 1, 1))
    return readouts


def leave_states(place, mem, f1, b1):
    for j in range(JW):
        final = contract(place, mem[j].astype(BF16), 1, 1)
        for s in range(2):
            f1[pl.ds(s * JW + j, GROUPS, stride=16), :] = final[s * GROUPS : (s + 1) * GROUPS]

    def one(i, _):
        b1[i] = f1[pl.ds(pl.multiple_of(i * 16, 16), 16), :].astype(BF16)
        return 0

    lax.fori_loop(0, GROUPS, one, 0)


def ready_finish(gate, gain, live, spread, own, gains):
    own[...] = own_lanes()
    square = (DK, DK)
    for b in range(BLOCKS):
        spread[b] = jnp.where(iota(square, 0) == b * JW + (iota(square, 1) & 7), 1.0, 0.0).astype(BF16)
    second = iota((2 * HEADS, DK), 0) >> 2
    for t in range(STEPS):
        gates = sigmoid(jnp.concatenate(by_head(gate[t].astype(F32)), axis=0)) * gain[...]
        gains[t] = jnp.where(live[0:1, t : t + 1] > second, gates, 0.0)


def finish_rows(a2, gains, spread, own, weight, conv, partial, fc, fg):
    lead, rest = halves(jnp.concatenate([a2[:, s, :] for s in range(2)], axis=0))
    mask = own[...]

    def block(b):
        picked = contract(lead, spread[b], 1, 0)
        if b >= CONV:
            picked = picked + contract(rest, spread[b], 1, 0)
        picked = picked * mask
        rows = []
        for s in range(2):
            total = picked[s * GROUPS : s * GROUPS + ZS]
            for n in range(1, GROUPS // ZS):
                total = total + picked[s * GROUPS + n * ZS : s * GROUPS + (n + 1) * ZS]
            rows.append(total[:HEADS] + total[HEADS:])
        return jnp.concatenate(rows, axis=0)

    fg[...] = jnp.zeros_like(fg)
    for t in range(STEPS):
        readout = block(CONV + t)
        scaling = lax.rsqrt(jnp.sum(readout * readout, axis=1, keepdims=True) / DK + EPS)
        gated = readout * scaling * gains[t]
        for s in range(2):
            for h in range(HEADS):
                r = s * HEADS + h
                fg[2 * t + s : 2 * t + s + 1, h * DK : (h + 1) * DK] = gated[r : r + 1]
    total = jnp.dot(fg[...].astype(BF16), weight[...], preferred_element_type=F32)
    width = partial.shape[2]
    share = total.shape[1] // partial.shape[0]
    for d in range(partial.shape[0]):
        turned = total if d == 0 else pltpu.roll(total, total.shape[1] - d * share, 1)
        partial[d] = turned[:, :width].astype(BF16)
    for n in range(HIST):
        for part in range(3):
            kept = block(n * 3 + part)
            for s in range(2):
                for h in range(HEADS):
                    r = s * HEADS + h
                    fc[n, part, s : s + 1, h * DK : (h + 1) * DK] = kept[r : r + 1]
    conv[...] = fc[...].astype(BF16)


def remote(axis, peer, src, dst, sems, n):
    return pltpu.make_async_remote_copy(
        src_ref=src,
        dst_ref=dst,
        send_sem=sems.at[0, n],
        recv_sem=sems.at[1, n],
        device_id={axis: peer},
        device_id_type=pl.DeviceIdType.MESH,
    )


def peers_in_order(z, x, core, act, near=True, far=True):
    def off(dz, dx, dc):
        act(lax.rem(z + dz, ZS), lax.rem(x + dx, XS), lax.rem(core + dc, CS))

    def along_z(dx, dc):
        def one(q, _):
            off(4 + (1 - 2 * (q % 2)) * ((q + 1) // 2), dx, dc)
            return 0

        lax.fori_loop(0, ZS - 1, one, 0)

    if far:
        for dx in (2, 1, 3):
            for dc in (1, 0):
                along_z(dx, dc)
        along_z(0, 1)
    if near:
        along_z(0, 0)
        for dx in (2, 1, 3):
            off(0, dx, 1)
            off(0, dx, 0)
        off(0, 0, 1)


def whole(
    columns,
    states_in,
    conv_in,
    proj_in,
    taps_in,
    decay_in,
    rate_in,
    beta_in,
    gate_in,
    gain_in,
    weight_in,
    targets_in,
    live_in,
    a1,
    shares,
    conv_to,
    states,
    conv,
    proj,
    taps,
    decay,
    rate,
    beta,
    gate,
    gain,
    weight,
    targets,
    live,
    conv_out,
    s1,
    s2,
    s3,
    r1,
    r2,
    r3,
    b1,
    b2,
    a2,
    partial,
    f,
    f1,
    f2,
    mem,
    places,
    ready,
    rows8,
    xt,
    fc,
    fg,
    spread,
    own,
    gains,
    local,
    sems,
):
    me = lax.axis_index("rep")
    col = lax.axis_index("head")
    z, x, core = me // (XS * CS), (me // CS) % XS, me % CS
    mine = (core * XS + x) * ZS + z
    head, jg = z % HEADS, (z // HEADS) * 8 + core * XS + x

    barrier = pltpu.get_barrier_semaphore()

    def greet(axis, peer):
        pl.semaphore_signal(
            barrier, inc=1, device_id={axis: peer}, device_id_type=pl.DeviceIdType.MESH
        )

    for k in (4, 3, 5, 2, 6, 1, 7):
        greet("rep", (lax.rem(z + k, ZS) * XS + x) * CS + core)
    for k in (4, 3, 5, 2, 6, 1, 7):
        greet("head", lax.rem(col + k, columns))
    for k in range(1, XS * CS):
        greet("rep", z * XS * CS + lax.rem(x * CS + core + k, XS * CS))

    loads = [
        pltpu.make_async_copy(src, dst, local.at[n])
        for n, (src, dst) in enumerate(
            [
                (conv_in, conv),
                (proj_in, proj),
                (decay_in, decay),
                (rate_in, rate),
                (beta_in, beta),
                (live_in, live),
                (states_in, states),
                (targets_in, targets),
                (taps_in, taps),
                (gate_in, gate),
                (gain_in, gain),
                (weight_in, weight),
            ]
        )
    ]
    for load in loads:
        load.start()
    for load in loads[:4]:
        load.wait()
    pack_inputs(conv, proj, decay, rate, s2, f)
    pl.semaphore_wait(barrier, ZS - 1 + XS * CS - 1 + columns - 1)

    keep = pltpu.make_async_copy(s2.at[head], r2.at[core, x, z], local.at[12])
    keep.start()
    for k in (4, 3, 5, 2, 6, 1, 7):
        to = lax.rem(z + k, ZS)
        peer = (to * XS + x) * CS + core
        remote("rep", peer, s2.at[lax.rem(to, HEADS)], r2.at[core, x, z], sems, 0).start()

    for load in loads[4:9]:
        load.wait()
    pack_values(conv, proj, beta, live, s3)
    pack_states(states, s1)
    find_places(targets, places)

    keep_s = [
        pltpu.make_async_copy(s1.at[mine], r1.at[mine], local.at[13]),
        pltpu.make_async_copy(s3.at[mine], r3.at[mine], local.at[14]),
    ]
    for copy in keep_s:
        copy.start()

    def to_all(pairs, **which):
        def one(to_z, to_x, to_core):
            at = (to_core * XS + to_x) * ZS + to_z
            peer = (to_z * XS + to_x) * CS + to_core
            for src, dst, n in pairs:
                remote("rep", peer, src.at[at], dst.at[mine], sems, n).start()

        peers_in_order(z, x, core, one, **which)

    def from_all(dst, n):
        most = dst.at[pl.ds(0, GROUPS - 1)]
        done = remote("rep", me, most, most, sems, n)
        done.wait_send()
        done.wait_recv()

    to_all([(s3, r3, 5), (s1, r1, 6)], far=False)

    keep.wait()
    done = remote("rep", me, r2.at[0, 0, pl.ds(0, ZS - 1)], r2.at[0, 0, pl.ds(0, ZS - 1)], sems, 0)
    done.wait_send()
    done.wait_recv()
    right = (z * XS + lax.rem(x + 1, XS)) * CS + core
    left = (z * XS + lax.rem(x + XS - 1, XS)) * CS + core
    other = me + 1 - 2 * core
    half = ZS // 2
    behind, ahead = lax.rem(x + XS - 1, XS), lax.rem(x + 1, XS)

    def part(origin, n):
        return r2.at[core, origin, pl.ds(n * half, half)]

    def pass_on(peer, origin, n, sem):
        copy = remote("rep", peer, part(origin, n), part(origin, n), sems, sem)
        copy.start()
        return copy

    ring = [
        pass_on(right, x, 0, 1),
        pass_on(left, x, 1, 2),
        pass_on(right, x, 1, 3),
        pass_on(left, x, 0, 4),
    ]

    to_all([(s3, r3, 5), (s1, r1, 6)], near=False)

    pass_whole = remote("rep", other, r2.at[core, x], r2.at[core, x], sems, 10)
    pass_whole.start()
    widen_inputs(r2, f2, core, x, 0, ZS)

    def arrived(copy, origin, n):
        copy.wait_recv()
        pass_on(other, origin, n, 10)
        widen_inputs(r2, f2, core, origin, n * half, (n + 1) * half)

    ring[0].wait_recv()
    ring.append(pass_on(right, behind, 0, 11))
    pass_on(other, behind, 0, 10)
    ring[1].wait_recv()
    ring.append(pass_on(left, ahead, 1, 12))
    pass_on(other, ahead, 1, 10)
    widen_inputs(r2, f2, core, behind, 0, half)
    widen_inputs(r2, f2, core, ahead, half, ZS)
    arrived(ring[2], behind, 1)
    arrived(ring[3], ahead, 0)
    opposite = lax.rem(x + 2, XS)
    arrived(ring[4], opposite, 0)
    arrived(ring[5], opposite, 1)
    for copy in keep_s:
        copy.wait()
    for copy in ring:
        copy.wait_send()
    done = remote("rep", me, r2.at[0], r2.at[0], sems, 10)
    done.wait_send()
    done.wait_recv()
    for n in range(XS):
        widen_inputs(r2, f2, 1 - core, n, 0, ZS)
    from_all(r3, 5)
    cols = pl.ds(pl.multiple_of(head * DK, DK), DK)
    kept = prepare_steps(jg, f2, r3, taps.at[:, :, cols], places, ready, rows8, xt)
    from_all(r1, 6)
    enter_states(r1, f1, mem)
    readouts = run_steps(ready, rows8, places, mem)
    pad = jnp.zeros((SLOTS, DK - BLOCKS * JW), F32)
    returned = jnp.concatenate([kept] + readouts + [pad], axis=1)
    for s in range(2):
        b2[:, s, :] = returned[s * GROUPS : (s + 1) * GROUPS]
    keep = pltpu.make_async_copy(b2.at[mine], a2.at[mine], local.at[12])
    keep.start()
    to_all([(b2, a2, 7)])
    leave_states(places[STEPS - 1], mem, f1, b1)
    keep_states = pltpu.make_async_copy(b1.at[mine], a1.at[mine], local.at[13])
    keep_states.start()
    to_all([(b1, a1, 8)])
    for load in loads[9:]:
        load.wait()
    ready_finish(gate, gain, live, spread, own, gains)

    keep.wait()
    from_all(a2, 7)
    finish_rows(a2, gains, spread, own, weight, conv_out, partial, fc, fg)
    keep = pltpu.make_async_copy(partial.at[col], shares.at[col], local.at[12])
    keep.start()
    for k in (4, 3, 5, 2, 6, 1, 7):
        to = lax.rem(col + k, columns)
        remote("head", to, partial.at[to], shares.at[col], sems, 9).start()
    store = pltpu.make_async_copy(conv_out, conv_to, local.at[14])
    store.start()
    keep_states.wait()
    from_all(a1, 8)
    keep.wait()
    most = shares.at[pl.ds(0, columns - 1)]
    done = remote("head", col, most, most, sems, 9)
    done.wait_send()
    done.wait_recv()
    store.wait()


def settle(a1_in, shares_in, conv_in, out_to, states_to, conv_to, a1, shares, conv, out, states, sems):
    loads = [
        pltpu.make_async_copy(src, dst, sems.at[n])
        for n, (src, dst) in enumerate([(a1_in, a1), (shares_in, shares), (conv_in, conv)])
    ]
    for load in loads:
        load.start()
    loads[2].wait()
    stores = [pltpu.make_async_copy(conv, conv_to, sems.at[3])]
    stores[0].start()
    loads[0].wait()
    for h in range(HEADS):
        pieces = [a1[holder(h, jg)].astype(F32) for jg in range(JG)]
        for s in range(2):
            states[s, h] = jnp.concatenate([p[s * JW : (s + 1) * JW] for p in pieces], axis=0).T
            store = pltpu.make_async_copy(
                states.at[s, h], states_to.at[s, h], sems.at[4 + 2 * h + s]
            )
            store.start()
            stores.append(store)
    loads[1].wait()
    total = shares[0].astype(F32)
    for n in range(1, shares.shape[0]):
        total = total + shares[n].astype(F32)
    for t in range(STEPS):
        out[t] = total[2 * t : 2 * t + 2, : out.shape[2]].astype(BF16)
    stores.append(pltpu.make_async_copy(out, out_to, sems.at[4 + 2 * HEADS]))
    stores[-1].start()
    for store in stores:
        store.wait()


def shape(dims, kind):
    return jax.ShapeDtypeStruct(dims, kind)


def local(columns, *args):
    (
        states,
        conv_states,
        projected,
        conv_weight,
        decay_input,
        decay_rate,
        beta_logit,
        out_gate,
        norm_gain,
        out_weight,
        destinations,
        live_counts,
    ) = args
    operands = (
        states,
        conv_states.transpose(1, 2, 0, 3),
        projected.transpose(0, 2, 1, 3),
        conv_weight.transpose(1, 0, 2),
        decay_input,
        decay_rate.reshape(1, HEADS),
        beta_logit.transpose(1, 2, 0),
        out_gate,
        norm_gain.reshape(1, DK),
        out_weight,
        destinations,
        live_counts.transpose(1, 0),
    )
    share = out_weight.shape[1] // columns
    width = -(-share // DK) * DK
    block = pltpu.VMEM((GROUPS, 16, DK), BF16)
    small = pltpu.VMEM((GROUPS, 2, DK), F32)
    any_ = pl.BlockSpec(memory_space=pltpu.HBM)
    most = pltpu.CompilerParams(
        collective_id=0, has_side_effects=True, vmem_limit_bytes=60 * 1024 * 1024
    )
    landed = (
        shape((GROUPS, 16, DK), BF16),
        shape((columns, 16, width), BF16),
        shape(operands[1].shape, BF16),
    )
    pieces = pl.pallas_call(
        functools.partial(whole, columns),
        out_shape=landed,
        in_specs=[any_] * len(operands),
        out_specs=(any_,) * 3,
        scratch_shapes=[pltpu.VMEM(a.shape, a.dtype) for a in operands]
        + [
            pltpu.VMEM(operands[1].shape, BF16),
            block,
            pltpu.VMEM((HEADS, ROWS, DK), BF16),
            small,
            block,
            pltpu.VMEM((CS, XS, ZS, ROWS, DK), BF16),
            small,
            block,
            small,
            small,
            pltpu.VMEM((columns, 16, width), BF16),
            pltpu.VMEM((HEADS, ROWS, DK), F32),
            pltpu.VMEM(((GROUPS + 1) * 16, DK), F32),
            pltpu.VMEM(((GROUPS + 1) * ROWS, DK), F32),
            pltpu.VMEM((JW, DK, SLOTS), F32),
            pltpu.VMEM((STEPS, SLOTS, SLOTS), BF16),
            pltpu.VMEM((STEPS, 3, DK, SLOTS), F32),
            pltpu.VMEM((STEPS, 2 * JW, SLOTS), F32),
            pltpu.VMEM((DK, SLOTS), F32),
            pltpu.VMEM(operands[1].shape, F32),
            pltpu.VMEM((16, HEADS * DK), F32),
            pltpu.VMEM((BLOCKS, DK, DK), BF16),
            pltpu.VMEM((SLOTS, DK), F32),
            pltpu.VMEM((STEPS, 2 * HEADS, DK), F32),
            pltpu.SemaphoreType.DMA((15,)),
            pltpu.SemaphoreType.DMA((2, 13)),
        ],
        compiler_params=most,
        name="kda_steps",
    )(*operands)
    results = (
        shape((STEPS, 2, share), BF16),
        shape(states.shape, F32),
        shape(operands[1].shape, BF16),
    )
    out, states_out, conv_out = pl.pallas_call(
        settle,
        out_shape=results,
        in_specs=[any_] * 3,
        out_specs=(any_,) * 3,
        scratch_shapes=[pltpu.VMEM(a.shape, a.dtype) for a in landed]
        + [pltpu.VMEM(a.shape, a.dtype) for a in results[:2]]
        + [pltpu.SemaphoreType.DMA((5 + 2 * HEADS,))],
        compiler_params=pltpu.CompilerParams(vmem_limit_bytes=60 * 1024 * 1024),
        name="settle",
    )(*pieces)
    return out, states_out, conv_out.transpose(2, 0, 1, 3)


def solution(mesh):
    placed = (
        P("rep", "head", None, None),
        P("rep", None, None, "head"),
        P(None, "rep", None, "head"),
        P(None, None, "head"),
        P(None, "rep", "head"),
        P("head"),
        P(None, "rep", "head"),
        P(None, "rep", "head"),
        P(),
        P("head", None),
        P(),
        P(None, "rep"),
    )
    return jax.shard_map(
        functools.partial(local, mesh.shape["head"]),
        mesh=mesh,
        in_specs=placed,
        out_specs=(
            P(None, "rep", "head"),
            P("rep", "head", None, None),
            P("rep", None, None, "head"),
        ),
        check_vma=False,
    )
```
